32 devices in a mesh: kern: 4 (over x, core), tile: 8 (over z, y).
Axes of the slice: x: 2, y: 2, z: 4, core: 2. Of those that a mesh axis runs over, the one named last changes fastest.
Arguments:
- mask: int32 [256, 512], P('tile'), may hold values 0 or 1
- kernels: bfloat16 [24, 2, 64, 64], replicated, may hold values from -0.09375 to 0.09375
- socs_weights: float32 [24], replicated, may hold values from 0.02 to 0.3
- quencher: float32 [256, 512], P('tile', 'kern'), may hold values from 0.1 to 0.6
Outputs:
- intensity: float32 [256, 512], P('tile', 'kern')
- acid_final: float32 [256, 512], P('tile', 'kern')
- base_final: float32 [256, 512], P('tile', 'kern')
The draws below stay inside these ranges and needn't reach their ends.
All inputs are finite; a program needn't handle non-finite values. No bound on the sum of `mask` on one device may be relied on, other than what follows from the above.
Results may differ from the reference program's by a relative error of at most 0.0003.
Values sent between devices are 32-bit elements; how exact they have to be, the bound alone decides.
No kernel may reach another device: no remote copies, remote signals or barrier semaphores. Data moves between devices by JAX's collectives and lax.ppermute only.
A program may use at most 128 MiB of HBM per device.

```python
import math
import jax
import jax.numpy as jnp
from jax import lax

K = 24
AMBIT = 64
STEPS = 8
ROWS = 256
COLS = 512


def touch_ends(array, own_key, least, top_value):
    longest = array.shape.index(max(array.shape))
    spots = []
    for shift in (0, 1):
        where = [jax.random.randint(jax.random.fold_in(own_key, axis), (), 0, length) for axis, length in enumerate(array.shape)]
        where[longest] = (where[longest] + shift) % array.shape[longest]
        spots.append(tuple(where))
    return array.at[spots[0]].set(least).at[spots[1]].set(top_value)


def level_of(own_key, extent, cuts, least, top_value):
    level, own = 1.0, jax.random.fold_in(own_key, 6)
    for axis_at, parts in cuts:
        heights = jnp.exp(jax.random.uniform(jax.random.fold_in(own, axis_at), (parts,), jnp.float32, least / len(cuts), top_value / len(cuts)))
        level = level * jnp.repeat(heights, extent[axis_at] // parts).reshape([-1 if axis == axis_at else 1 for axis in range(len(extent))])
    return level


def bell_draw(key, extent, scale, reach, dtype=jnp.bfloat16):
    return jnp.clip(scale * jax.random.normal(key, extent, jnp.float32), -reach, reach).astype(dtype)


def setup_inputs(seed: int = 0) -> dict:
    streams_of = jax.random.split(jax.random.key(seed), 5)
    mask = touch_ends((jax.random.randint(streams_of[0], (ROWS, COLS), 0, 2) < 1).astype(jnp.int32), jax.random.fold_in(streams_of[0], 1), 0, 1)
    kernels = bell_draw(streams_of[1], (K, 2, AMBIT, AMBIT), (AMBIT * AMBIT) ** -0.5, 0.09375)
    socs_weights = jnp.clip(jnp.exp(jax.random.uniform(streams_of[2], (K,), jnp.float32, math.log(0.02), math.log(0.3))), 0.02, 0.3)
    quencher = jnp.clip(0.1 + 0.5 * jax.random.uniform(streams_of[3], (ROWS, COLS), jnp.float32) ** level_of(streams_of[3], (ROWS, COLS), ((0, 8), (1, 4)), -0.2, 0.2), 0.1, 0.6)
    return {"mask": mask, "kernels": kernels, "socs_weights": socs_weights, "quencher": quencher}


DIFFUSE_ACID = 0.2
DIFFUSE_BASE = 0.1
QUENCH_RATE = 0.5
EXPOSURE = 0.35


def react(padded):
    middle = padded[:, 1:-1, 1:-1]
    spread = padded[:, :-2, 1:-1] + padded[:, 2:, 1:-1] + padded[:, 1:-1, :-2] + padded[:, 1:-1, 2:] - 4.0 * middle
    quenched = QUENCH_RATE * middle[0] * middle[1]
    acid_next = middle[0] + DIFFUSE_ACID * spread[0] - quenched
    base_next = middle[1] + DIFFUSE_BASE * spread[1] - quenched
    return jnp.stack([acid_next, base_next], axis=0)


def reference(mask, kernels, socs_weights, quencher):
    total_rows = mask.shape[0]
    total_cols = mask.shape[1]
    half_ambit = AMBIT // 2
    frame = (total_rows + AMBIT, total_cols + AMBIT)
    mask_field = jnp.zeros(frame, jnp.float32).at[:total_rows, :total_cols].set(mask.astype(jnp.float32))
    mask_spectrum = jnp.fft.rfft2(mask_field)

    def add_kernel(carry, member):
        kernel_pair, weight = member
        placed = jnp.zeros((2,) + frame, jnp.float32).at[:, :AMBIT, :AMBIT].set(kernel_pair.astype(jnp.float32))
        placed = jnp.roll(placed, (-half_ambit, -half_ambit), axis=(1, 2))
        spectrum = jnp.conj(jnp.fft.rfft2(placed))
        fields = jnp.fft.irfft2(mask_spectrum[None] * spectrum, s=frame)[:, :total_rows, :total_cols]
        return carry + weight * jnp.sum(fields * fields, axis=0), weight

    intensity = lax.scan(add_kernel, jnp.zeros((total_rows, total_cols), jnp.float32), (kernels, socs_weights))[0]
    acid = 1.0 - jnp.exp(-EXPOSURE * intensity)
    resist_state = jnp.stack([acid, quencher], axis=0)
    for step_index in range(STEPS):
        resist_state = react(jnp.pad(resist_state, ((0, 0), (1, 1), (1, 1))))
    return intensity, resist_state[0], resist_state[1]
```

```python
import functools

import jax
import jax.numpy as jnp
from jax import lax
from jax.experimental import pallas as pl
from jax.experimental.pallas import tpu as pltpu
from jax.sharding import PartitionSpec as P

STEPS = 8
DIFFUSE_ACID = 0.2
DIFFUSE_BASE = 0.1
QUENCH_RATE = 0.5
EXPOSURE = 0.35

LANES = 128
RIM = 8
GROUP = 4


def lane_roll_left(value, amount):
    width = value.shape[1]
    amount %= width
    return value if amount == 0 else pltpu.roll(value, width - amount, 1)


def three_blocks(ref, rows, kern, kern_count):
    blocks = []
    for step in (-1, 0, 1):
        place = jnp.clip(kern + step, 0, kern_count - 1)
        block = ref[rows, pl.ds(pl.multiple_of(place * LANES, LANES), LANES)].astype(jnp.float32)
        inside = jnp.logical_and(kern + step >= 0, kern + step < kern_count)
        blocks.append(jnp.where(inside, block, 0.0))
    return jnp.concatenate(blocks, axis=1)


def prepare_kernel(kern_count, tile_count, lead, mask_ref, quencher_ref, send_ref, window_ref):
    kern, tile = lax.axis_index("kern"), lax.axis_index("tile")
    rows = mask_ref.shape[0]
    window_ref[...] = lane_roll_left(
        three_blocks(mask_ref, slice(None), kern, kern_count), LANES - lead
    )[:, : 2 * LANES]
    send_ref[...] = jnp.zeros_like(send_ref)
    own = pl.ds(pl.multiple_of(kern * LANES, LANES), LANES)
    for step, value in (
        (1, quencher_ref[rows - RIM :, :]),
        (-1, quencher_ref[:RIM, :]),
        (2, mask_ref[rows - RIM :, own].astype(jnp.float32)),
        (-2, mask_ref[:RIM, own].astype(jnp.float32)),
    ):
        target = tile + step

        @pl.when(jnp.logical_and(target >= 0, target < tile_count))
        def _(target=target, value=value):
            for column in range(kern_count):
                send_ref[column, target] = value

    lane = lax.broadcasted_iota(jnp.int32, (RIM, LANES), 1)
    for step, first in ((-1, 0), (1, LANES - RIM)):
        edge = jnp.zeros((RIM, LANES), jnp.float32)
        for part in range(rows // RIM):
            moved = lane_roll_left(quencher_ref[RIM * part : RIM * part + RIM, :], first - RIM * part)
            here = jnp.logical_and(lane >= RIM * part, lane < RIM * part + RIM)
            edge = jnp.where(here, moved, edge)
        target = kern + step

        @pl.when(jnp.logical_and(target >= 0, target < kern_count))
        def _(target=target, edge=edge):
            send_ref[target, tile] = edge


def shifted(value, axis, steps):
    count = lax.axis_size(axis)
    leading, last = (max(0, -steps), min(count, count - steps))
    return lax.ppermute(value, axis, [(source, source + steps) for source in range(leading, last)])


def resist_kernel(
    kern_count,
    tile_count,
    ambit,
    own_ref,
    above_ref,
    below_ref,
    received_ref,
    quencher_ref,
    taps_ref,
    weights_ref,
    intensity_ref,
    acid_ref,
    base_ref,
    rows_ref,
    slanted_ref,
    main_ref,
    strip_ref,
    total_ref,
    image_ref,
):
    kern, tile = lax.axis_index("kern"), lax.axis_index("tile")
    rows = own_ref.shape[0]
    lead = ambit // 2 + RIM
    height = rows + 2 * RIM
    span = rows + 2 * lead
    planes = taps_ref.shape[0] // (ambit // GROUP)

    def far_rows(step):
        place = jnp.clip(tile + step, 0, tile_count - 1)
        inside_tile = jnp.logical_and(tile + step >= 0, tile + step < tile_count)
        blocks = []
        for side in (-1, 0, 1):
            column = jnp.clip(kern + side, 0, kern_count - 1)
            inside = jnp.logical_and(kern + side >= 0, kern + side < kern_count)
            block = received_ref[column, place]
            blocks.append(jnp.where(jnp.logical_and(inside, inside_tile), block, 0.0))
        return lane_roll_left(jnp.concatenate(blocks, axis=1), LANES - lead)[:, : 2 * LANES]

    rows_ref[:RIM, :] = far_rows(-2)
    rows_ref[RIM : RIM + rows, :] = above_ref[...]
    rows_ref[RIM + rows : RIM + 2 * rows, :] = own_ref[...]
    rows_ref[RIM + 2 * rows : RIM + 3 * rows, :] = below_ref[...]
    rows_ref[RIM + 3 * rows :, :] = far_rows(2)

    window = rows_ref[...]
    for shift in range(8):
        moved = lane_roll_left(window, shift)
        for half in range(2):
            slanted_ref[half, pl.ds(shift, span, stride=8), :] = moved[:, LANES * half : LANES * half + LANES]

    lane = lax.broadcasted_iota(jnp.int32, (8, LANES), 1)

    def slant(row, carry):
        at = pl.multiple_of(row * 8, 8)
        after = pl.multiple_of(jnp.minimum(row + 1, span - 1) * 8, 8)
        low, high = slanted_ref[0, pl.ds(at, 8), :], slanted_ref[1, pl.ds(at, 8), :]
        next_high = slanted_ref[1, pl.ds(after, 8), :]
        for pair in range(ambit // 16):
            mains, strips = [], []
            for offset in (16 * pair, 16 * pair + 8):
                moved_high = lane_roll_left(high, offset)
                mains.append(jnp.where(lane < LANES - offset, lane_roll_left(low, offset), moved_high))
                strips.append(
                    jnp.where(lane < LANES // 2, moved_high, lane_roll_left(next_high, offset - LANES // 2))
                )
            place = pl.ds(pl.multiple_of(row * ambit + 16 * pair, 16), 16)
            main_ref[place, :] = jnp.concatenate(mains, axis=0).astype(jnp.bfloat16)
            strip_ref[place, :] = jnp.concatenate(strips, axis=0).astype(jnp.bfloat16)
        return carry

    lax.fori_loop(0, span, slant, 0, unroll=4)

    groups = height // GROUP
    tap_groups = ambit // GROUP
    tile_depth = GROUP * ambit
    total_ref[...] = jnp.zeros_like(total_ref)
    for s in range(groups + tap_groups - 1):
        first, last = max(0, s - tap_groups + 1), min(groups - 1, s)
        taps = taps_ref[planes * (tap_groups - 1 - s + first) : planes * (tap_groups - s + last), :]
        at = s * tile_depth
        for part, pieces in enumerate(
            (
                (main_ref[at : at + tile_depth], main_ref[at + ambit : at + ambit + tile_depth]),
                (main_ref[at + 2 * ambit : at + 2 * ambit + tile_depth], main_ref[at + 3 * ambit : at + 3 * ambit + tile_depth]),
                (strip_ref[at : at + tile_depth], strip_ref[at + 2 * ambit : at + 2 * ambit + tile_depth]),
            )
        ):
            total_ref[planes * first : planes * (last + 1), 2 * LANES * part : 2 * LANES * (part + 1)] += jnp.dot(
                taps, jnp.concatenate(pieces, axis=1), preferred_element_type=jnp.float32
            )

    plane = lax.broadcasted_iota(jnp.int32, (planes, 1), 0)
    weight = jnp.zeros((planes, 1), jnp.float32)
    for member in range(planes // 2):
        weight = jnp.where(plane // 2 == member, weights_ref[member], weight)
    for group in range(groups):
        field = total_ref[planes * group : planes * (group + 1), :]
        summed = jnp.sum(weight * (field * field), axis=0, keepdims=True)
        for part in range(GROUP):
            row = GROUP * group + part
            image_ref[row : row + 1, :LANES] = summed[:, LANES * part : LANES * (part + 1)]
            at = LANES * (GROUP + part // 2)
            strip = summed[:, at : at + LANES]
            image_ref[row : row + 1, LANES:] = strip if part % 2 == 0 else lane_roll_left(strip, LANES // 2)

    image = image_ref[...]
    row_id = lax.broadcasted_iota(jnp.int32, image.shape, 0)
    lane_id = lax.broadcasted_iota(jnp.int32, image.shape, 1)
    at_row = tile * rows + row_id - RIM
    at_column = kern * LANES + lane_id - RIM
    valid = (at_row >= 0) & (at_row < tile_count * rows) & (at_column >= 0) & (at_column < kern_count * LANES)
    valid = valid & (lane_id < LANES + 2 * RIM)

    def rim_rows(step):
        place = jnp.clip(tile + step, 0, tile_count - 1)
        return jnp.concatenate(
            [received_ref[jnp.clip(kern + side, 0, kern_count - 1), place] for side in (-1, 0, 1)], axis=1
        )

    before = received_ref[jnp.clip(kern - 1, 0, kern_count - 1), tile]
    after = received_ref[jnp.clip(kern + 1, 0, kern_count - 1), tile]
    middle = [
        jnp.concatenate(
            [
                lane_roll_left(before, RIM * part + RIM),
                quencher_ref[RIM * part : RIM * part + RIM, :],
                lane_roll_left(after, RIM * part),
            ],
            axis=1,
        )
        for part in range(rows // RIM)
    ]
    base = jnp.concatenate([rim_rows(-1)] + middle + [rim_rows(1)], axis=0)
    base = lane_roll_left(base, LANES - RIM)[:, : 2 * LANES]
    base = jnp.where(valid, base, 0.0)
    acid = jnp.where(valid, 1.0 - jnp.exp(-EXPOSURE * image), 0.0)

    def spread(value):
        return (
            pltpu.roll(value, 1, 0)
            + pltpu.roll(value, value.shape[0] - 1, 0)
            + pltpu.roll(value, 1, 1)
            + pltpu.roll(value, value.shape[1] - 1, 1)
            - 4.0 * value
        )

    for _ in range(STEPS):
        quenched = QUENCH_RATE * acid * base
        acid, base = (
            jnp.where(valid, acid + DIFFUSE_ACID * spread(acid) - quenched, 0.0),
            jnp.where(valid, base + DIFFUSE_BASE * spread(base) - quenched, 0.0),
        )
    for ref, value in ((intensity_ref, image), (acid_ref, acid), (base_ref, base)):
        ref[...] = lane_roll_left(value, RIM)[RIM : RIM + rows, :LANES]


def on_device(mask, kernels, socs_weights, quencher):
    ambit = kernels.shape[2]
    planes = kernels.shape[0] * kernels.shape[1]
    kern_count, tile_count = lax.axis_size("kern"), lax.axis_size("tile")
    rows = mask.shape[0]
    lead = ambit // 2 + RIM
    height = rows + 2 * RIM
    span = rows + 2 * lead

    send, window = pl.pallas_call(
        functools.partial(prepare_kernel, kern_count, tile_count, lead),
        out_shape=(
            jax.ShapeDtypeStruct((kern_count, tile_count, RIM, LANES), jnp.float32),
            jax.ShapeDtypeStruct((rows, 2 * LANES), jnp.float32),
        ),
        name="prepare",
    )(mask, quencher)
    received = lax.all_to_all(
        send.reshape(kern_count * tile_count, RIM, LANES), ("kern", "tile"), 0, 0, tiled=True
    ).reshape(send.shape)
    above = shifted(window, "tile", 1)
    below = shifted(window, "tile", -1)
    tap_groups = ambit // GROUP
    taps = kernels.reshape(planes, tap_groups, GROUP * ambit)[:, ::-1].transpose(1, 0, 2)
    taps = taps.reshape(tap_groups * planes, GROUP * ambit)
    block = jax.ShapeDtypeStruct((rows, LANES), jnp.float32)
    vmem = pl.BlockSpec(memory_space=pltpu.VMEM)
    return pl.pallas_call(
        functools.partial(resist_kernel, kern_count, tile_count, ambit),
        out_shape=(block, block, block),
        in_specs=[vmem] * 6 + [pl.BlockSpec(memory_space=pltpu.SMEM)],
        scratch_shapes=[
            pltpu.VMEM((span, 2 * LANES), jnp.float32),
            pltpu.VMEM((2, 8 * span, LANES), jnp.float32),
            pltpu.VMEM((span * ambit, LANES), jnp.bfloat16),
            pltpu.VMEM((span * ambit, LANES), jnp.bfloat16),
            pltpu.VMEM((height // GROUP * planes, 6 * LANES), jnp.float32),
            pltpu.VMEM((height, 2 * LANES), jnp.float32),
        ],
        compiler_params=pltpu.CompilerParams(vmem_limit_bytes=48 * 1024 * 1024),
        name="image_and_resist",
    )(window, above, below, received, quencher, taps, socs_weights)


def solution(mesh):
    placed = (P("tile", None), P(), P(), P("tile", "kern"))
    return jax.shard_map(
        on_device,
        mesh=mesh,
        in_specs=placed,
        out_specs=(P("tile", "kern"), P("tile", "kern"), P("tile", "kern")),
        check_vma=False,
    )
```

```python
import functools

import jax
import jax.numpy as jnp
from jax import lax
from jax.experimental import pallas as pl
from jax.experimental.pallas import tpu as pltpu
from jax.sharding import PartitionSpec as P

STEPS = 8
DIFFUSE_ACID = 0.2
DIFFUSE_BASE = 0.1
QUENCH_RATE = 0.5
EXPOSURE = 0.35

LANES = 128
RIM = 8
GROUP = 4
WORD = 16


def lane_roll_left(value, amount):
    width = value.shape[1]
    amount %= width
    return value if amount == 0 else pltpu.roll(value, width - amount, 1)


def three_blocks(ref, rows, kern, kern_count):
    blocks = []
    for step in (-1, 0, 1):
        place = jnp.clip(kern + step, 0, kern_count - 1)
        block = ref[rows, pl.ds(pl.multiple_of(place * LANES, LANES), LANES)].astype(jnp.float32)
        inside = jnp.logical_and(kern + step >= 0, kern + step < kern_count)
        blocks.append(jnp.where(inside, block, 0.0))
    return jnp.concatenate(blocks, axis=1)


def own_window(mask_ref, kern, kern_count, lead):
    blocks = three_blocks(mask_ref, slice(None), kern, kern_count)
    return lane_roll_left(blocks, LANES - lead)[:, : 2 * LANES]


def prepare_kernel(kern_count, tile_count, lead, mask_ref, quencher_ref, send_ref, window_ref):
    kern, tile = lax.axis_index("kern"), lax.axis_index("tile")
    rows = mask_ref.shape[0]
    window_ref[...] = own_window(mask_ref, kern, kern_count, lead)
    send_ref[...] = jnp.zeros_like(send_ref)
    own = pl.ds(pl.multiple_of(kern * LANES, LANES), LANES)
    for step, value in (
        (1, quencher_ref[rows - RIM :, :]),
        (-1, quencher_ref[:RIM, :]),
        (2, mask_ref[rows - RIM :, own].astype(jnp.float32)),
        (-2, mask_ref[:RIM, own].astype(jnp.float32)),
    ):
        target = tile + step

        @pl.when(jnp.logical_and(target >= 0, target < tile_count))
        def _(target=target, value=value):
            for column in range(kern_count):
                send_ref[column, target] = value

    lane = lax.broadcasted_iota(jnp.int32, (RIM, LANES), 1)
    for step, first in ((-1, 0), (1, LANES - RIM)):
        edge = jnp.zeros((RIM, LANES), jnp.float32)
        for part in range(rows // RIM):
            moved = lane_roll_left(quencher_ref[RIM * part : RIM * part + RIM, :], first - RIM * part)
            here = jnp.logical_and(lane >= RIM * part, lane < RIM * part + RIM)
            edge = jnp.where(here, moved, edge)
        target = kern + step

        @pl.when(jnp.logical_and(target >= 0, target < kern_count))
        def _(target=target, edge=edge):
            send_ref[target, tile] = edge


def swapped(value, axis, first):
    count = lax.axis_size(axis)
    pairs = [(low, low + 1) for low in range(first, count - 1, 2)]
    return lax.ppermute(value, axis, pairs + [(high, low) for low, high in pairs])


def mask_words(window):
    bits = window.astype(jnp.int32)
    row = lax.broadcasted_iota(jnp.int32, (WORD, bits.shape[1]), 0)
    count = bits.shape[0] // WORD
    low = [
        jnp.sum(bits[WORD * w : WORD * (w + 1)] << row, axis=0, keepdims=True) for w in range(count)
    ]
    return [low[w] + (((low[w + 1] & 0xFF) << WORD) if w + 1 < count else 0) for w in range(count)]


def lay_shifts(window, ambit, main_ref, strip_ref, main_rows, strip_rows):
    words = mask_words(window)
    slanted = jnp.concatenate([jnp.broadcast_to(word, (8, 2 * LANES)) for word in words], axis=0)
    sublane = lax.broadcasted_iota(jnp.int32, slanted.shape, 0)
    for bit in (1, 2, 4):
        slanted = jnp.where((sublane & bit) != 0, lane_roll_left(slanted, bit), slanted)
    low, high = slanted[:, :LANES], slanted[:, LANES:]
    lane = lax.broadcasted_iota(jnp.int32, low.shape, 1)
    mains, strips = [], []
    for offset in range(0, ambit, 8):
        mains.append(lane_roll_left(jnp.where(lane < offset, high, low), offset))
        strip = lane_roll_left(high, offset)
        for width in (16, 32, 64):
            strip = jnp.where(lane < width, strip, pltpu.roll(strip, width, 1))
        strips.append(strip >> (lane // 16))
    for shifts, ref, rows in ((mains, main_ref, main_rows), (strips, strip_ref, strip_rows)):
        for w in range(len(words)):
            for pair in range(ambit // 16):
                word = jnp.concatenate(
                    [shifts[2 * pair][8 * w : 8 * w + 8], shifts[2 * pair + 1][8 * w : 8 * w + 8]], axis=0
                )
                for bit in range(WORD):
                    row = WORD * w + bit
                    if row in rows:
                        plane = ((word >> bit) & 1).astype(jnp.float32).astype(jnp.bfloat16)
                        ref[ambit * row + 16 * pair : ambit * row + 16 * pair + 16, :] = plane


def add_main(total_ref, taps_ref, main_ref, s, first_row, groups, tap_groups, ambit):
    planes = taps_ref.shape[0] // tap_groups
    first, last = max(0, s - tap_groups + 1), min(groups - 1, s)
    taps = taps_ref[planes * (tap_groups - 1 - s + first) : planes * (tap_groups - s + last), :]
    depth = GROUP * ambit
    for half in range(2):
        at = ambit * (GROUP * s + 2 * half - first_row)
        shifts = jnp.concatenate([main_ref[at : at + depth], main_ref[at + ambit : at + ambit + depth]], axis=1)
        place = (slice(planes * first, planes * (last + 1)), slice(2 * LANES * half, 2 * LANES * (half + 1)))
        total_ref[place] += jnp.dot(taps, shifts, preferred_element_type=jnp.float32)


def add_strip(total_ref, taps_ref, strip_ref, s, first_row, groups, tap_groups, ambit):
    planes = taps_ref.shape[0] // tap_groups
    members = [g for g in range(groups // GROUP) if 0 <= s - GROUP * g < tap_groups]
    pieces = [tap_groups - 1 - s + GROUP * g for g in members]
    taps = jnp.concatenate([taps_ref[planes * p : planes * (p + 1), :] for p in pieces], axis=0)
    depth = GROUP * ambit
    at = ambit * (GROUP * s - first_row)
    shifts = jnp.concatenate(
        [strip_ref[at : at + depth], strip_ref[at + 8 * ambit : at + 8 * ambit + depth]], axis=1
    )
    total_ref[planes * members[0] : planes * (members[-1] + 1), :] += jnp.dot(
        taps, shifts, preferred_element_type=jnp.float32
    )


class Plan:
    def __init__(self, rows, ambit):
        self.rows, self.ambit = rows, ambit
        self.lead = ambit // 2 + RIM
        self.height, self.span = rows + 2 * RIM, rows + 2 * self.lead
        self.groups, self.tap_groups = self.height // GROUP, ambit // GROUP
        self.strip_groups = self.height // 16
        own = range(self.lead, self.lead + rows)
        self.main = {s: range(GROUP * s, GROUP * s + 7) for s in range(self.groups + self.tap_groups - 1)}
        self.strip = {
            s: range(GROUP * s, GROUP * s + 12) for s in range(GROUP * (self.strip_groups - 1) + self.tap_groups)
        }
        self.own_main = [s for s, used in self.main.items() if used[0] in own and used[-1] in own]
        self.own_strip = [s for s, used in self.strip.items() if used[0] in own and used[-1] + 7 in own]
        self.far_main = [s for s in self.main if s not in self.own_main]
        self.far_strip = [s for s in self.strip if s not in self.own_strip]


def own_rows_kernel(
    plan,
    kern_count,
    kernels_ref,
    weights_ref,
    mask_ref,
    taps_ref,
    main_total_ref,
    strip_total_ref,
    window_ref,
    weight_ref,
    wide_ref,
    main_ref,
    strip_ref,
):
    ambit, lead = plan.ambit, plan.lead
    planes = kernels_ref.shape[0] * kernels_ref.shape[1]
    wanted = (weight_ref.shape[0], weights_ref.shape[0])
    plane = lax.broadcasted_iota(jnp.int32, wanted, 0)
    member = lax.broadcasted_iota(jnp.int32, wanted, 1)
    spread = jnp.broadcast_to(weights_ref[...].reshape(1, wanted[1]), wanted)
    column = jnp.sum(jnp.where(plane // 2 == member, spread, 0.0), axis=1, keepdims=True)
    weight_ref[...] = jnp.broadcast_to(column, weight_ref.shape)
    kern = lax.axis_index("kern")
    window_ref[...] = own_window(mask_ref, kern, kern_count, lead)
    wide_ref[...] = kernels_ref[...].reshape(planes * ambit, ambit).astype(jnp.float32)
    for group in range(plan.tap_groups):
        pieces = [wide_ref[pl.ds(GROUP * group + part, planes, stride=ambit), :] for part in range(GROUP)]
        place = planes * (plan.tap_groups - 1 - group)
        taps_ref[place : place + planes, :] = jnp.concatenate(pieces, axis=1).astype(jnp.bfloat16)
    main_rows = {row - lead for s in plan.own_main for row in plan.main[s]}
    strip_rows = {row - lead for s in plan.own_strip for row in plan.strip[s]}
    lay_shifts(window_ref[...], ambit, main_ref, strip_ref, main_rows, strip_rows)
    main_total_ref[...] = jnp.zeros_like(main_total_ref)
    strip_total_ref[...] = jnp.zeros_like(strip_total_ref)
    for s in plan.own_main:
        add_main(main_total_ref, taps_ref, main_ref, s, lead, plan.groups, plan.tap_groups, ambit)
    for s in plan.own_strip:
        add_strip(strip_total_ref, taps_ref, strip_ref, s, lead, plan.groups, plan.tap_groups, ambit)


def resist_kernel(
    plan,
    kern_count,
    tile_count,
    own_ref,
    pair_ref,
    other_ref,
    received_ref,
    quencher_ref,
    taps_ref,
    own_main_ref,
    own_strip_ref,
    weight_ref,
    intensity_ref,
    acid_ref,
    base_ref,
    main_ref,
    strip_ref,
    main_total_ref,
    strip_total_ref,
    image_ref,
):
    kern, tile = lax.axis_index("kern"), lax.axis_index("tile")
    rows, ambit = plan.rows, plan.ambit
    planes = taps_ref.shape[0] // plan.tap_groups
    main_total_ref[...] = own_main_ref[...]
    strip_total_ref[...] = own_strip_ref[...]

    def far_rows(step):
        place = jnp.clip(tile + step, 0, tile_count - 1)
        inside_tile = jnp.logical_and(tile + step >= 0, tile + step < tile_count)
        blocks = []
        for side in (-1, 0, 1):
            column = jnp.clip(kern + side, 0, kern_count - 1)
            inside = jnp.logical_and(kern + side >= 0, kern + side < kern_count)
            block = received_ref[column, place]
            blocks.append(jnp.where(jnp.logical_and(inside, inside_tile), block, 0.0))
        return lane_roll_left(jnp.concatenate(blocks, axis=1), LANES - plan.lead)[:, : 2 * LANES]

    even = tile % 2 == 0
    pair, other = pair_ref[...], other_ref[...]
    above, below = jnp.where(even, other, pair), jnp.where(even, pair, other)
    window = jnp.concatenate([far_rows(-2), above, own_ref[...], below, far_rows(2)], axis=0)
    main_rows = {row for s in plan.far_main for row in plan.main[s]}
    strip_rows = {row for s in plan.far_strip for row in plan.strip[s]}
    lay_shifts(window, ambit, main_ref, strip_ref, main_rows, strip_rows)
    for s in plan.far_main:
        add_main(main_total_ref, taps_ref, main_ref, s, 0, plan.groups, plan.tap_groups, ambit)
    for s in plan.far_strip:
        add_strip(strip_total_ref, taps_ref, strip_ref, s, 0, plan.groups, plan.tap_groups, ambit)

    weight = weight_ref[:, :1]

    def weighted(total_ref, group):
        field = total_ref[planes * group : planes * (group + 1), :]
        return jnp.sum(weight * (field * field), axis=0, keepdims=True)

    for group in range(plan.groups):
        summed = weighted(main_total_ref, group)
        for part in range(GROUP):
            row = GROUP * group + part
            image_ref[row : row + 1, :LANES] = summed[:, LANES * part : LANES * (part + 1)]
    for group in range(plan.strip_groups):
        summed = weighted(strip_total_ref, group)
        for part in range(16):
            row = 16 * group + part
            half = summed[:, LANES * (part // 8) : LANES * (part // 8 + 1)]
            image_ref[row : row + 1, LANES:] = lane_roll_left(half, 16 * (part % 8))

    image = image_ref[...]
    row_id = lax.broadcasted_iota(jnp.int32, image.shape, 0)
    lane_id = lax.broadcasted_iota(jnp.int32, image.shape, 1)
    at_row = tile * rows + row_id - RIM
    at_column = kern * LANES + lane_id - RIM
    valid = (at_row >= 0) & (at_row < tile_count * rows) & (at_column >= 0) & (at_column < kern_count * LANES)
    valid = valid & (lane_id < LANES + 2 * RIM)

    def rim_rows(step):
        place = jnp.clip(tile + step, 0, tile_count - 1)
        return jnp.concatenate(
            [received_ref[jnp.clip(kern + side, 0, kern_count - 1), place] for side in (-1, 0, 1)], axis=1
        )

    before = received_ref[jnp.clip(kern - 1, 0, kern_count - 1), tile]
    after = received_ref[jnp.clip(kern + 1, 0, kern_count - 1), tile]
    middle = [
        jnp.concatenate(
            [
                lane_roll_left(before, RIM * part + RIM),
                quencher_ref[RIM * part : RIM * part + RIM, :],
                lane_roll_left(after, RIM * part),
            ],
            axis=1,
        )
        for part in range(rows // RIM)
    ]
    base = jnp.concatenate([rim_rows(-1)] + middle + [rim_rows(1)], axis=0)
    base = lane_roll_left(base, LANES - RIM)[:, : 2 * LANES]
    base = jnp.where(valid, base, 0.0)
    acid = jnp.where(valid, 1.0 - jnp.exp(-EXPOSURE * image), 0.0)

    def spread(value):
        return (
            pltpu.roll(value, 1, 0)
            + pltpu.roll(value, value.shape[0] - 1, 0)
            + pltpu.roll(value, 1, 1)
            + pltpu.roll(value, value.shape[1] - 1, 1)
            - 4.0 * value
        )

    for _ in range(STEPS):
        quenched = QUENCH_RATE * acid * base
        acid, base = (
            jnp.where(valid, acid + DIFFUSE_ACID * spread(acid) - quenched, 0.0),
            jnp.where(valid, base + DIFFUSE_BASE * spread(base) - quenched, 0.0),
        )
    for ref, value in ((intensity_ref, image), (acid_ref, acid), (base_ref, base)):
        ref[...] = lane_roll_left(value, RIM)[RIM : RIM + rows, :LANES]


def on_device(mask, kernels, socs_weights, quencher):
    ambit = kernels.shape[2]
    planes = kernels.shape[0] * kernels.shape[1]
    kern_count, tile_count = lax.axis_size("kern"), lax.axis_size("tile")
    rows = mask.shape[0]
    plan = Plan(rows, ambit)
    vmem = pl.BlockSpec(memory_space=pltpu.VMEM)
    limit = pltpu.CompilerParams(vmem_limit_bytes=24 * 1024 * 1024)

    send, window = pl.pallas_call(
        functools.partial(prepare_kernel, kern_count, tile_count, plan.lead),
        out_shape=(
            jax.ShapeDtypeStruct((kern_count, tile_count, RIM, LANES), jnp.float32),
            jax.ShapeDtypeStruct((rows, 2 * LANES), jnp.float32),
        ),
        cost_estimate=pl.CostEstimate(flops=10**9, bytes_accessed=10**7, transcendentals=0),
        name="prepare",
    )(mask, quencher)
    received = lax.all_to_all(
        send.reshape(kern_count * tile_count, RIM, LANES), ("kern", "tile"), 0, 0, tiled=True
    ).reshape(send.shape)
    pair = swapped(window, "tile", 0)
    other = swapped(window, "tile", 1)

    main_total = jax.ShapeDtypeStruct((plan.groups * planes, 4 * LANES), jnp.float32)
    strip_total = jax.ShapeDtypeStruct((plan.strip_groups * planes, 2 * LANES), jnp.float32)
    taps, own_main, own_strip, own_mask, weight = pl.pallas_call(
        functools.partial(own_rows_kernel, plan, kern_count),
        out_shape=(
            jax.ShapeDtypeStruct((plan.tap_groups * planes, GROUP * ambit), jnp.bfloat16),
            main_total,
            strip_total,
            jax.ShapeDtypeStruct(window.shape, jnp.float32),
            jax.ShapeDtypeStruct((planes, LANES), jnp.float32),
        ),
        in_specs=[vmem] * 3,
        out_specs=(vmem,) * 5,
        scratch_shapes=[
            pltpu.VMEM((planes * ambit, ambit), jnp.float32),
            pltpu.VMEM((rows * ambit, LANES), jnp.bfloat16),
            pltpu.VMEM((rows * ambit, LANES), jnp.bfloat16),
        ],
        compiler_params=limit,
        name="own_rows",
    )(kernels, socs_weights, mask)
    block = jax.ShapeDtypeStruct((rows, LANES), jnp.float32)
    return pl.pallas_call(
        functools.partial(resist_kernel, plan, kern_count, tile_count),
        out_shape=(block, block, block),
        in_specs=[vmem] * 9,
        scratch_shapes=[
            pltpu.VMEM((plan.span * ambit, LANES), jnp.bfloat16),
            pltpu.VMEM((plan.span * ambit, LANES), jnp.bfloat16),
            pltpu.VMEM(main_total.shape, jnp.float32),
            pltpu.VMEM(strip_total.shape, jnp.float32),
            pltpu.VMEM((plan.height, 2 * LANES), jnp.float32),
        ],
        compiler_params=limit,
        name="image_and_resist",
    )(own_mask, pair, other, received, quencher, taps, own_main, own_strip, weight)


def solution(mesh):
    placed = (P("tile", None), P(), P(), P("tile", "kern"))
    return jax.shard_map(
        on_device,
        mesh=mesh,
        in_specs=placed,
        out_specs=(P("tile", "kern"), P("tile", "kern"), P("tile", "kern")),
        check_vma=False,
    )
```

```python
import copy
import functools

import jax
import jax.numpy as jnp
from jax import lax
from jax.experimental import pallas as pl
from jax.experimental.pallas import tpu as pltpu
from jax.sharding import PartitionSpec as P

STEPS = 8
DIFFUSE_ACID = 0.2
DIFFUSE_BASE = 0.1
QUENCH_RATE = 0.5
EXPOSURE = 0.35

LANES = 128
RIM = 8
GROUP = 4
WORD = 16


def lane_roll_left(value, amount):
    width = value.shape[1]
    amount %= width
    return value if amount == 0 else pltpu.roll(value, width - amount, 1)


def three_blocks(ref, rows, kern, kern_count):
    blocks = []
    for step in (-1, 0, 1):
        place = jnp.clip(kern + step, 0, kern_count - 1)
        block = ref[rows, pl.ds(pl.multiple_of(place * LANES, LANES), LANES)].astype(jnp.float32)
        inside = jnp.logical_and(kern + step >= 0, kern + step < kern_count)
        blocks.append(jnp.where(inside, block, 0.0))
    return jnp.concatenate(blocks, axis=1)


def own_window(mask_ref, kern, kern_count, lead):
    blocks = three_blocks(mask_ref, slice(None), kern, kern_count)
    return lane_roll_left(blocks, LANES - lead)[:, : 2 * LANES]


def prepare_kernel(kern_count, tile_count, lead, mask_ref, quencher_ref, send_ref, window_ref):
    kern, tile = lax.axis_index("kern"), lax.axis_index("tile")
    rows = mask_ref.shape[0]
    window_ref[...] = own_window(mask_ref, kern, kern_count, lead)
    send_ref[...] = jnp.zeros_like(send_ref)
    own = pl.ds(pl.multiple_of(kern * LANES, LANES), LANES)
    for step, value in (
        (1, quencher_ref[rows - RIM :, :]),
        (-1, quencher_ref[:RIM, :]),
        (2, mask_ref[rows - RIM :, own].astype(jnp.float32)),
        (-2, mask_ref[:RIM, own].astype(jnp.float32)),
    ):
        target = tile + step

        @pl.when(jnp.logical_and(target >= 0, target < tile_count))
        def _(target=target, value=value):
            for column in range(kern_count):
                send_ref[column, target] = value

    lane = lax.broadcasted_iota(jnp.int32, (RIM, LANES), 1)
    for step, first in ((-1, 0), (1, LANES - RIM)):
        edge = jnp.zeros((RIM, LANES), jnp.float32)
        for part in range(rows // RIM):
            moved = lane_roll_left(quencher_ref[RIM * part : RIM * part + RIM, :], first - RIM * part)
            here = jnp.logical_and(lane >= RIM * part, lane < RIM * part + RIM)
            edge = jnp.where(here, moved, edge)
        target = kern + step

        @pl.when(jnp.logical_and(target >= 0, target < kern_count))
        def _(target=target, edge=edge):
            send_ref[target, tile] = edge


def swapped(value, axis, first):
    count = lax.axis_size(axis)
    pairs = [(low, low + 1) for low in range(first, count - 1, 2)]
    return lax.ppermute(value, axis, pairs + [(high, low) for low, high in pairs])


def mask_words(window):
    bits = window.astype(jnp.int32)
    row = lax.broadcasted_iota(jnp.int32, (WORD, bits.shape[1]), 0)
    count = bits.shape[0] // WORD
    low = [
        jnp.sum(bits[WORD * w : WORD * (w + 1)] << row, axis=0, keepdims=True) for w in range(count)
    ]
    return [low[w] + (((low[w + 1] & 0xFF) << WORD) if w + 1 < count else 0) for w in range(count)]


class Shifts:
    def __init__(self, window, ambit, first_row, main_ref, strip_ref):
        words = mask_words(window)
        slanted = jnp.concatenate([jnp.broadcast_to(word, (8, 2 * LANES)) for word in words], axis=0)
        sublane = lax.broadcasted_iota(jnp.int32, slanted.shape, 0)
        for bit in (1, 2, 4):
            slanted = jnp.where((sublane & bit) != 0, lane_roll_left(slanted, bit), slanted)
        low, high = slanted[:, :LANES], slanted[:, LANES:]
        lane = lax.broadcasted_iota(jnp.int32, low.shape, 1)
        mains, strips = [], []
        for offset in range(0, ambit, 8):
            mains.append(lane_roll_left(jnp.where(lane < offset, high, low), offset))
            strip = lane_roll_left(high, offset)
            for width in (16, 32, 64):
                strip = jnp.where(lane < width, strip, pltpu.roll(strip, width, 1))
            strips.append(strip >> (lane // 16))
        self.ambit, self.first_row = ambit, first_row
        self.sources = {"main": mains, "strip": strips}
        self.refs = {"main": main_ref, "strip": strip_ref}
        self.laid = {"main": set(), "strip": set()}

    def view(self, first_row):
        view = copy.copy(self)
        view.first_row, view.laid = first_row, {"main": set(), "strip": set()}
        return view

    def lay(self, kind, rows):
        for row in rows:
            row -= self.first_row
            if row in self.laid[kind]:
                continue
            self.laid[kind].add(row)
            word, bit = divmod(row, WORD)
            source = self.sources[kind]
            for pair in range(self.ambit // 16):
                value = jnp.concatenate(
                    [source[2 * pair + part][8 * word : 8 * word + 8] for part in range(2)], axis=0
                )
                plane = ((value >> bit) & 1).astype(jnp.float32).astype(jnp.bfloat16)
                at = self.ambit * row + 16 * pair
                self.refs[kind][at : at + 16, :] = plane


def add_main(plan, total_ref, taps_ref, shifts, s):
    groups, tap_groups, ambit = plan.groups, plan.tap_groups, plan.ambit
    planes = taps_ref.shape[0] // tap_groups
    shifts.lay("main", plan.main[s])
    main_ref = shifts.refs["main"]
    first, last = max(0, s - tap_groups + 1), min(groups - 1, s)
    taps = taps_ref[planes * (tap_groups - 1 - s + first) : planes * (tap_groups - s + last), :]
    depth = GROUP * ambit
    for half in range(2):
        at = ambit * (GROUP * s + 2 * half - shifts.first_row)
        moved = jnp.concatenate([main_ref[at : at + depth], main_ref[at + ambit : at + ambit + depth]], axis=1)
        place = (slice(planes * first, planes * (last + 1)), slice(2 * LANES * half, 2 * LANES * (half + 1)))
        total_ref[place] += jnp.dot(taps, moved, preferred_element_type=jnp.float32)


def add_strip(plan, total_ref, taps_ref, shifts, s):
    groups, tap_groups, ambit = plan.groups, plan.tap_groups, plan.ambit
    planes = taps_ref.shape[0] // tap_groups
    shifts.lay("strip", plan.strip[s])
    strip_ref = shifts.refs["strip"]
    members = [g for g in range(groups // GROUP) if 0 <= s - GROUP * g < tap_groups]
    pieces = [tap_groups - 1 - s + GROUP * g for g in members]
    taps = jnp.concatenate([taps_ref[planes * p : planes * (p + 1), :] for p in pieces], axis=0)
    depth = GROUP * ambit
    at = ambit * (GROUP * s - shifts.first_row)
    moved = jnp.concatenate(
        [strip_ref[at : at + depth], strip_ref[at + 8 * ambit : at + 8 * ambit + depth]], axis=1
    )
    total_ref[planes * members[0] : planes * (members[-1] + 1), :] += jnp.dot(
        taps, moved, preferred_element_type=jnp.float32
    )


class Plan:
    def __init__(self, rows, ambit):
        self.rows, self.ambit = rows, ambit
        self.lead = ambit // 2 + RIM
        self.height, self.span = rows + 2 * RIM, rows + 2 * self.lead
        self.groups, self.tap_groups = self.height // GROUP, ambit // GROUP
        self.strip_groups = self.height // 16
        main = {s: range(GROUP * s, GROUP * s + 7) for s in range(self.groups + self.tap_groups - 1)}
        strip = {
            s: range(GROUP * s, GROUP * s + 12) for s in range(GROUP * (self.strip_groups - 1) + self.tap_groups)
        }
        self.main, self.strip = main, strip
        first, middle, last = RIM, self.lead, self.lead + rows
        self.parts = {}
        taken = {"main": set(), "strip": set()}
        for name, low, high in (
            ("own", middle, last),
            ("upper", first, last),
            ("lower", middle, last + rows),
            ("top", 0, last),
            ("bottom", middle, self.span),
        ):
            self.parts[name] = {}
            for kind, steps, reach in (("main", main, 0), ("strip", strip, 7)):
                chosen = [
                    s for s, used in steps.items()
                    if s not in taken[kind] and low <= used[0] and used[-1] + reach < high
                ]
                taken[kind].update(chosen)
                self.parts[name][kind] = chosen
        assert taken == {"main": set(main), "strip": set(strip)}

    def add(self, name, main_total_ref, strip_total_ref, taps_ref, shifts):
        for s in self.parts[name]["main"]:
            add_main(self, main_total_ref, taps_ref, shifts, s)
        for s in self.parts[name]["strip"]:
            add_strip(self, strip_total_ref, taps_ref, shifts, s)


def own_rows_kernel(
    plan,
    kern_count,
    kernels_ref,
    weights_ref,
    mask_ref,
    taps_ref,
    main_total_ref,
    strip_total_ref,
    window_ref,
    weight_ref,
    wide_ref,
    main_ref,
    strip_ref,
):
    ambit, lead = plan.ambit, plan.lead
    planes = kernels_ref.shape[0] * kernels_ref.shape[1]
    wanted = (weight_ref.shape[0], weights_ref.shape[0])
    plane = lax.broadcasted_iota(jnp.int32, wanted, 0)
    member = lax.broadcasted_iota(jnp.int32, wanted, 1)
    spread = jnp.broadcast_to(weights_ref[...].reshape(1, wanted[1]), wanted)
    column = jnp.sum(jnp.where(plane // 2 == member, spread, 0.0), axis=1, keepdims=True)
    weight_ref[...] = jnp.broadcast_to(column, weight_ref.shape)
    kern = lax.axis_index("kern")
    window_ref[...] = own_window(mask_ref, kern, kern_count, lead)
    wide_ref[...] = kernels_ref[...].reshape(planes * ambit, ambit).astype(jnp.float32)
    for group in range(plan.tap_groups):
        pieces = [wide_ref[pl.ds(GROUP * group + part, planes, stride=ambit), :] for part in range(GROUP)]
        place = planes * (plan.tap_groups - 1 - group)
        taps_ref[place : place + planes, :] = jnp.concatenate(pieces, axis=1).astype(jnp.bfloat16)
    shifts = Shifts(window_ref[...], ambit, lead, main_ref, strip_ref)
    main_total_ref[...] = jnp.zeros_like(main_total_ref)
    strip_total_ref[...] = jnp.zeros_like(strip_total_ref)
    plan.add("own", main_total_ref, strip_total_ref, taps_ref, shifts)


def weighted_rows(weight, total_ref, group):
    planes = weight.shape[0]
    field = total_ref[planes * group : planes * (group + 1), :]
    return jnp.sum(weight * (field * field), axis=0, keepdims=True)


def write_main_rows(image_ref, weight, total_ref, groups):
    for group in groups:
        summed = weighted_rows(weight, total_ref, group)
        for part in range(GROUP):
            row = GROUP * group + part
            image_ref[row : row + 1, :LANES] = summed[:, LANES * part : LANES * (part + 1)]


def add_side(plan, below, main_total_ref, strip_total_ref, taps_ref, shifts, first_row):
    @pl.when(below)
    def _():
        plan.add("lower", main_total_ref, strip_total_ref, taps_ref, shifts.view(first_row["lower"]))

    @pl.when(jnp.logical_not(below))
    def _():
        plan.add("upper", main_total_ref, strip_total_ref, taps_ref, shifts.view(first_row["upper"]))


def pair_rows_kernel(
    plan,
    own_ref,
    pair_ref,
    taps_ref,
    main_in_ref,
    strip_in_ref,
    main_total_ref,
    strip_total_ref,
    main_ref,
    strip_ref,
):
    even = lax.axis_index("tile") % 2 == 0
    main_total_ref[...] = main_in_ref[...]
    strip_total_ref[...] = strip_in_ref[...]
    own, pair = own_ref[...], pair_ref[...]
    window = jnp.concatenate([jnp.where(even, own, pair), jnp.where(even, pair, own)], axis=0)
    shifts = Shifts(window, plan.ambit, 0, main_ref, strip_ref)
    first_row = {"upper": RIM, "lower": plan.lead}
    add_side(plan, even, main_total_ref, strip_total_ref, taps_ref, shifts, first_row)


def resist_kernel(
    plan,
    kern_count,
    tile_count,
    own_ref,
    other_ref,
    pair_ref,
    received_ref,
    quencher_ref,
    taps_ref,
    main_in_ref,
    strip_in_ref,
    weight_ref,
    intensity_ref,
    acid_ref,
    base_ref,
    main_ref,
    strip_ref,
    main_total_ref,
    strip_total_ref,
    image_ref,
):
    kern, tile = lax.axis_index("kern"), lax.axis_index("tile")
    rows, ambit = plan.rows, plan.ambit
    planes = taps_ref.shape[0] // plan.tap_groups
    main_total_ref[...] = main_in_ref[...]
    strip_total_ref[...] = strip_in_ref[...]

    def far_rows(step):
        place = jnp.clip(tile + step, 0, tile_count - 1)
        inside_tile = jnp.logical_and(tile + step >= 0, tile + step < tile_count)
        blocks = []
        for side in (-1, 0, 1):
            column = jnp.clip(kern + side, 0, kern_count - 1)
            inside = jnp.logical_and(kern + side >= 0, kern + side < kern_count)
            block = received_ref[column, place]
            blocks.append(jnp.where(jnp.logical_and(inside, inside_tile), block, 0.0))
        return lane_roll_left(jnp.concatenate(blocks, axis=1), LANES - plan.lead)[:, : 2 * LANES]

    even = tile % 2 == 0
    pair, other = pair_ref[...], other_ref[...]
    above, below = jnp.where(even, other, pair), jnp.where(even, pair, other)
    window = jnp.concatenate([far_rows(-2), above, own_ref[...], below, far_rows(2)], axis=0)
    shifts = Shifts(window, ambit, 0, main_ref, strip_ref)
    first_row = {"upper": 0, "lower": 0}
    add_side(plan, jnp.logical_not(even), main_total_ref, strip_total_ref, taps_ref, shifts, first_row)
    shifts = shifts.view(0)
    plan.add("top", main_total_ref, strip_total_ref, taps_ref, shifts)
    plan.add("bottom", main_total_ref, strip_total_ref, taps_ref, shifts)

    weight = weight_ref[:, :1]
    write_main_rows(image_ref, weight, main_total_ref, range(plan.groups))
    for group in range(plan.strip_groups):
        summed = weighted_rows(weight, strip_total_ref, group)
        for part in range(16):
            row = 16 * group + part
            half = summed[:, LANES * (part // 8) : LANES * (part // 8 + 1)]
            image_ref[row : row + 1, LANES:] = lane_roll_left(half, 16 * (part % 8))

    image = image_ref[...]
    row_id = lax.broadcasted_iota(jnp.int32, image.shape, 0)
    lane_id = lax.broadcasted_iota(jnp.int32, image.shape, 1)
    at_row = tile * rows + row_id - RIM
    at_column = kern * LANES + lane_id - RIM
    valid = (at_row >= 0) & (at_row < tile_count * rows) & (at_column >= 0) & (at_column < kern_count * LANES)
    valid = valid & (lane_id < LANES + 2 * RIM)

    def rim_rows(step):
        place = jnp.clip(tile + step, 0, tile_count - 1)
        return jnp.concatenate(
            [received_ref[jnp.clip(kern + side, 0, kern_count - 1), place] for side in (-1, 0, 1)], axis=1
        )

    before = received_ref[jnp.clip(kern - 1, 0, kern_count - 1), tile]
    after = received_ref[jnp.clip(kern + 1, 0, kern_count - 1), tile]
    middle = [
        jnp.concatenate(
            [
                lane_roll_left(before, RIM * part + RIM),
                quencher_ref[RIM * part : RIM * part + RIM, :],
                lane_roll_left(after, RIM * part),
            ],
            axis=1,
        )
        for part in range(rows // RIM)
    ]
    base = jnp.concatenate([rim_rows(-1)] + middle + [rim_rows(1)], axis=0)
    base = lane_roll_left(base, LANES - RIM)[:, : 2 * LANES]
    base = jnp.where(valid, base, 0.0)
    acid = jnp.where(valid, 1.0 - jnp.exp(-EXPOSURE * image), 0.0)

    def spread(value):
        return (
            pltpu.roll(value, 1, 0)
            + pltpu.roll(value, value.shape[0] - 1, 0)
            + pltpu.roll(value, 1, 1)
            + pltpu.roll(value, value.shape[1] - 1, 1)
            - 4.0 * value
        )

    for _ in range(STEPS):
        quenched = QUENCH_RATE * acid * base
        acid, base = (
            jnp.where(valid, acid + DIFFUSE_ACID * spread(acid) - quenched, 0.0),
            jnp.where(valid, base + DIFFUSE_BASE * spread(base) - quenched, 0.0),
        )
    for ref, value in ((intensity_ref, image), (acid_ref, acid), (base_ref, base)):
        ref[...] = lane_roll_left(value, RIM)[RIM : RIM + rows, :LANES]


def on_device(mask, kernels, socs_weights, quencher):
    ambit = kernels.shape[2]
    planes = kernels.shape[0] * kernels.shape[1]
    kern_count, tile_count = lax.axis_size("kern"), lax.axis_size("tile")
    rows = mask.shape[0]
    plan = Plan(rows, ambit)
    vmem = pl.BlockSpec(memory_space=pltpu.VMEM)
    limit = pltpu.CompilerParams(vmem_limit_bytes=24 * 1024 * 1024)

    send, window = pl.pallas_call(
        functools.partial(prepare_kernel, kern_count, tile_count, plan.lead),
        out_shape=(
            jax.ShapeDtypeStruct((kern_count, tile_count, RIM, LANES), jnp.float32),
            jax.ShapeDtypeStruct((rows, 2 * LANES), jnp.float32),
        ),
        cost_estimate=pl.CostEstimate(flops=10**9, bytes_accessed=10**7, transcendentals=0),
        name="prepare",
    )(mask, quencher)
    received = lax.all_to_all(
        send.reshape(kern_count * tile_count, RIM, LANES), ("kern", "tile"), 0, 0, tiled=True
    ).reshape(send.shape)
    pair = swapped(window, "tile", 0)
    other = swapped(window, "tile", 1)

    main_total = jax.ShapeDtypeStruct((plan.groups * planes, 4 * LANES), jnp.float32)
    strip_total = jax.ShapeDtypeStruct((plan.strip_groups * planes, 2 * LANES), jnp.float32)
    taps, own_main, own_strip, own_mask, weight = pl.pallas_call(
        functools.partial(own_rows_kernel, plan, kern_count),
        out_shape=(
            jax.ShapeDtypeStruct((plan.tap_groups * planes, GROUP * ambit), jnp.bfloat16),
            main_total,
            strip_total,
            jax.ShapeDtypeStruct(window.shape, jnp.float32),
            jax.ShapeDtypeStruct((planes, LANES), jnp.float32),
        ),
        in_specs=[vmem] * 3,
        out_specs=(vmem,) * 5,
        scratch_shapes=[
            pltpu.VMEM((planes * ambit, ambit), jnp.float32),
            pltpu.VMEM((rows * ambit, LANES), jnp.bfloat16),
            pltpu.VMEM((rows * ambit, LANES), jnp.bfloat16),
        ],
        compiler_params=limit,
        name="own_rows",
    )(kernels, socs_weights, mask)
    totals = pl.pallas_call(
        functools.partial(pair_rows_kernel, plan),
        out_shape=(main_total, strip_total),
        in_specs=[vmem] * 5,
        out_specs=(vmem,) * 2,
        scratch_shapes=[pltpu.VMEM((2 * rows * ambit, LANES), jnp.bfloat16)] * 2,
        compiler_params=limit,
        name="pair_rows",
    )(own_mask, pair, taps, own_main, own_strip)
    block = jax.ShapeDtypeStruct((rows, LANES), jnp.float32)
    return pl.pallas_call(
        functools.partial(resist_kernel, plan, kern_count, tile_count),
        out_shape=(block, block, block),
        in_specs=[vmem] * 9,
        scratch_shapes=[pltpu.VMEM((plan.span * ambit, LANES), jnp.bfloat16)] * 2
        + [
            pltpu.VMEM(main_total.shape, jnp.float32),
            pltpu.VMEM(strip_total.shape, jnp.float32),
            pltpu.VMEM((plan.height, 2 * LANES), jnp.float32),
        ],
        compiler_params=limit,
        name="image_and_resist",
    )(own_mask, other, pair, received, quencher, taps, *totals, weight)


def solution(mesh):
    placed = (P("tile", None), P(), P(), P("tile", "kern"))
    return jax.shard_map(
        on_device,
        mesh=mesh,
        in_specs=placed,
        out_specs=(P("tile", "kern"), P("tile", "kern"), P("tile", "kern")),
        check_vma=False,
    )
```

```python
import copy
import functools

import jax
import jax.numpy as jnp
from jax import lax
from jax.experimental import pallas as pl
from jax.experimental.pallas import tpu as pltpu
from jax.sharding import PartitionSpec as P

STEPS = 8
DIFFUSE_ACID = 0.2
DIFFUSE_BASE = 0.1
QUENCH_RATE = 0.5
EXPOSURE = 0.35

LANES = 128
RIM = 8
GROUP = 4
WORD = 16


def lane_roll_left(value, amount):
    width = value.shape[1]
    amount %= width
    return value if amount == 0 else pltpu.roll(value, width - amount, 1)


def three_blocks(ref, rows, kern, kern_count):
    blocks = []
    for step in (-1, 0, 1):
        place = jnp.clip(kern + step, 0, kern_count - 1)
        block = ref[rows, pl.ds(pl.multiple_of(place * LANES, LANES), LANES)].astype(jnp.float32)
        inside = jnp.logical_and(kern + step >= 0, kern + step < kern_count)
        blocks.append(jnp.where(inside, block, 0.0))
    return jnp.concatenate(blocks, axis=1)


def own_window(mask_ref, kern, kern_count, lead):
    blocks = three_blocks(mask_ref, slice(None), kern, kern_count)
    return lane_roll_left(blocks, LANES - lead)[:, : 2 * LANES]


def prepare_kernel(kern_count, tile_count, lead, mask_ref, quencher_ref, send_ref, window_ref):
    kern, tile = lax.axis_index("kern"), lax.axis_index("tile")
    rows = mask_ref.shape[0]
    window_ref[...] = own_window(mask_ref, kern, kern_count, lead)
    send_ref[...] = jnp.zeros_like(send_ref)
    own = pl.ds(pl.multiple_of(kern * LANES, LANES), LANES)
    for step, value in (
        (1, quencher_ref[rows - RIM :, :]),
        (-1, quencher_ref[:RIM, :]),
        (2, mask_ref[rows - RIM :, own].astype(jnp.float32)),
        (-2, mask_ref[:RIM, own].astype(jnp.float32)),
    ):
        target = tile + step

        @pl.when(jnp.logical_and(target >= 0, target < tile_count))
        def _(target=target, value=value):
            for column in range(kern_count):
                send_ref[column, target] = value

    lane = lax.broadcasted_iota(jnp.int32, (RIM, LANES), 1)
    for step, first in ((-1, 0), (1, LANES - RIM)):
        edge = jnp.zeros((RIM, LANES), jnp.float32)
        for part in range(rows // RIM):
            moved = lane_roll_left(quencher_ref[RIM * part : RIM * part + RIM, :], first - RIM * part)
            here = jnp.logical_and(lane >= RIM * part, lane < RIM * part + RIM)
            edge = jnp.where(here, moved, edge)
        target = kern + step

        @pl.when(jnp.logical_and(target >= 0, target < kern_count))
        def _(target=target, edge=edge):
            send_ref[target, tile] = edge


def swapped(value, axis, first):
    count = lax.axis_size(axis)
    pairs = [(low, low + 1) for low in range(first, count - 1, 2)]
    return lax.ppermute(value, axis, pairs + [(high, low) for low, high in pairs])


def mask_words(window):
    bits = window.astype(jnp.int32)
    row = lax.broadcasted_iota(jnp.int32, (WORD, bits.shape[1]), 0)
    count = bits.shape[0] // WORD
    low = [
        jnp.sum(bits[WORD * w : WORD * (w + 1)] << row, axis=0, keepdims=True) for w in range(count)
    ]
    return [low[w] + (((low[w + 1] & 0xFF) << WORD) if w + 1 < count else 0) for w in range(count)]


class Shifts:
    def __init__(self, window, ambit, first_row, main_ref, strip_ref):
        words = mask_words(window)
        slanted = [
            pltpu.roll(jnp.broadcast_to(word, (8, 2 * LANES)), 2 * LANES - 7, 1, stride=1, stride_axis=0)
            for word in words
        ]
        slanted = jnp.concatenate(slanted, axis=0)
        low, high = slanted[:, :LANES], slanted[:, LANES:]
        lane = lax.broadcasted_iota(jnp.int32, low.shape, 1)
        mains, strips = [], []
        for offset in range(0, ambit, 8):
            mains.append(lane_roll_left(jnp.where(lane < offset, high, low), offset))
            strip = lane_roll_left(high, offset)
            for width in (16, 32, 64):
                strip = jnp.where(lane < width, strip, pltpu.roll(strip, width, 1))
            strips.append(strip >> (lane // 16))
        self.ambit, self.first_row = ambit, first_row
        self.sources = {"main": mains, "strip": strips}
        self.refs = {"main": main_ref, "strip": strip_ref}
        self.laid = {"main": set(), "strip": set()}

    def view(self, first_row):
        view = copy.copy(self)
        view.first_row, view.laid = first_row, {"main": set(), "strip": set()}
        return view

    def lay(self, kind, rows):
        for row in rows:
            row -= self.first_row
            if row in self.laid[kind]:
                continue
            self.laid[kind].add(row)
            word, bit = divmod(row, WORD)
            source = self.sources[kind]
            for pair in range(self.ambit // 16):
                value = jnp.concatenate(
                    [source[2 * pair + part][8 * word : 8 * word + 8] for part in range(2)], axis=0
                )
                plane = ((value >> bit) & 1).astype(jnp.float32).astype(jnp.bfloat16)
                at = self.ambit * row + 16 * pair
                self.refs[kind][at : at + 16, :] = plane


class Total:
    def __init__(self, ref, source, planes):
        self.ref, self.source, self.planes = ref, source, planes
        self.waiting = {
            (group, half)
            for group in range(ref.shape[0] // planes)
            for half in range(ref.shape[1] // (2 * LANES))
        }

    def add(self, first, last, half, value):
        lanes = slice(2 * LANES * half, 2 * LANES * (half + 1))
        group = first
        while group <= last:
            fresh, end = (group, half) in self.waiting, group
            while end <= last and ((end, half) in self.waiting) == fresh:
                self.waiting.discard((end, half))
                end += 1
            place = (slice(self.planes * group, self.planes * end), lanes)
            piece = value[self.planes * (group - first) : self.planes * (end - first)]
            if not fresh:
                piece = self.ref[place] + piece
            elif self.source is not None:
                piece = self.source[place] + piece
            self.ref[place] = piece
            group = end

    def finish(self):
        for group, half in sorted(self.waiting):
            lanes = slice(2 * LANES * half, 2 * LANES * (half + 1))
            place = (slice(self.planes * group, self.planes * (group + 1)), lanes)
            self.ref[place] = jnp.zeros_like(self.ref[place]) if self.source is None else self.source[place]
        self.waiting = set()


def add_main(plan, total, taps_ref, shifts, s):
    groups, tap_groups, ambit = plan.groups, plan.tap_groups, plan.ambit
    planes = total.planes
    shifts.lay("main", plan.main[s])
    main_ref = shifts.refs["main"]
    first, last = max(0, s - tap_groups + 1), min(groups - 1, s)
    taps = taps_ref[planes * (tap_groups - 1 - s + first) : planes * (tap_groups - s + last), :]
    depth = GROUP * ambit
    for half in range(2):
        at = ambit * (GROUP * s + 2 * half - shifts.first_row)
        moved = jnp.concatenate([main_ref[at : at + depth], main_ref[at + ambit : at + ambit + depth]], axis=1)
        total.add(first, last, half, jnp.dot(taps, moved, preferred_element_type=jnp.float32))


def add_strip(plan, total, taps_ref, shifts, s):
    groups, tap_groups, ambit = plan.groups, plan.tap_groups, plan.ambit
    planes = total.planes
    shifts.lay("strip", plan.strip[s])
    strip_ref = shifts.refs["strip"]
    members = [g for g in range(groups // GROUP) if 0 <= s - GROUP * g < tap_groups]
    pieces = [tap_groups - 1 - s + GROUP * g for g in members]
    taps = jnp.concatenate([taps_ref[planes * p : planes * (p + 1), :] for p in pieces], axis=0)
    depth = GROUP * ambit
    at = ambit * (GROUP * s - shifts.first_row)
    moved = jnp.concatenate(
        [strip_ref[at : at + depth], strip_ref[at + 8 * ambit : at + 8 * ambit + depth]], axis=1
    )
    total.add(members[0], members[-1], 0, jnp.dot(taps, moved, preferred_element_type=jnp.float32))


class Plan:
    def __init__(self, rows, ambit):
        self.rows, self.ambit = rows, ambit
        self.lead = ambit // 2 + RIM
        self.height, self.span = rows + 2 * RIM, rows + 2 * self.lead
        self.groups, self.tap_groups = self.height // GROUP, ambit // GROUP
        self.strip_groups = self.height // 16
        main = {s: range(GROUP * s, GROUP * s + 7) for s in range(self.groups + self.tap_groups - 1)}
        strip = {
            s: range(GROUP * s, GROUP * s + 12) for s in range(GROUP * (self.strip_groups - 1) + self.tap_groups)
        }
        self.main, self.strip = main, strip
        first, middle, last = RIM, self.lead, self.lead + rows
        self.parts = {}
        taken = {"main": set(), "strip": set()}
        for name, low, high in (
            ("own", middle, last),
            ("upper", first, last),
            ("lower", middle, last + rows),
            ("top", 0, last),
            ("bottom", middle, self.span),
        ):
            self.parts[name] = {}
            for kind, steps, reach in (("main", main, 0), ("strip", strip, 7)):
                chosen = [
                    s for s, used in steps.items()
                    if s not in taken[kind] and low <= used[0] and used[-1] + reach < high
                ]
                taken[kind].update(chosen)
                self.parts[name][kind] = chosen
        assert taken == {"main": set(main), "strip": set(strip)}

    def add(self, name, totals, taps_ref, shifts):
        for s in self.parts[name]["main"]:
            add_main(self, totals[0], taps_ref, shifts, s)
        for s in self.parts[name]["strip"]:
            add_strip(self, totals[1], taps_ref, shifts, s)


def near_rows_kernel(
    plan,
    kern_count,
    kernels_ref,
    weights_ref,
    mask_ref,
    pair_ref,
    taps_ref,
    main_total_ref,
    strip_total_ref,
    weight_ref,
    own_ref,
    main_ref,
    strip_ref,
):
    ambit = plan.ambit
    planes = kernels_ref.shape[0] * kernels_ref.shape[1]
    wanted = (weight_ref.shape[0], weights_ref.shape[0])
    plane = lax.broadcasted_iota(jnp.int32, wanted, 0)
    member = lax.broadcasted_iota(jnp.int32, wanted, 1)
    spread = jnp.broadcast_to(weights_ref[...].reshape(1, wanted[1]), wanted)
    column = jnp.sum(jnp.where(plane // 2 == member, spread, 0.0), axis=1, keepdims=True)
    weight_ref[...] = jnp.broadcast_to(column, weight_ref.shape)
    depth = GROUP * ambit
    tap = lax.broadcasted_iota(jnp.int32, (depth, depth), 0)
    lane = lax.broadcasted_iota(jnp.int32, (depth, depth), 1)
    turned = jnp.where(tap == (lane ^ 7), 1.0, 0.0).astype(jnp.bfloat16)
    by_row = jnp.transpose(kernels_ref[...].reshape(planes, ambit, ambit), (1, 0, 2))
    for group in range(plan.tap_groups):
        pieces = [by_row[GROUP * group + part] for part in range(GROUP)]
        place = planes * (plan.tap_groups - 1 - group)
        taps = jnp.concatenate(pieces, axis=1)
        taps = jnp.dot(taps, turned, preferred_element_type=jnp.float32)
        taps_ref[place : place + planes, :] = taps.astype(jnp.bfloat16)
    even = lax.axis_index("tile") % 2 == 0
    own, pair = own_window(mask_ref, lax.axis_index("kern"), kern_count, plan.lead), pair_ref[...]
    own_ref[...] = own
    window = jnp.concatenate([jnp.where(even, own, pair), jnp.where(even, pair, own)], axis=0)
    shifts = Shifts(window, ambit, 0, main_ref, strip_ref)
    first_row = {"upper": RIM, "lower": plan.lead}
    add_side(plan, even, (main_total_ref, strip_total_ref), (None, None), taps_ref, shifts, first_row, before=("own",))


def weighted_rows(weight, total_ref, group):
    planes = weight.shape[0]
    field = total_ref[planes * group : planes * (group + 1), :]
    return jnp.sum(weight * (field * field), axis=0, keepdims=True)


def write_main_rows(image_ref, weight, total_ref, groups):
    for group in groups:
        summed = weighted_rows(weight, total_ref, group)
        for part in range(GROUP):
            row = GROUP * group + part
            image_ref[row : row + 1, :LANES] = summed[:, LANES * part : LANES * (part + 1)]


def add_side(plan, below, refs, sources, taps_ref, shifts, first_row, before=(), after=(), then=None):
    planes = taps_ref.shape[0] // plan.tap_groups

    def add(name):
        totals = [Total(ref, source, planes) for ref, source in zip(refs, sources)]
        view = shifts.view(first_row[name])
        for part in (*before, name, *after):
            plan.add(part, totals, taps_ref, view)
        for total in totals:
            total.finish()
        if then is not None:
            then()

    pl.when(below)(lambda: add("lower"))
    pl.when(jnp.logical_not(below))(lambda: add("upper"))


def resist_kernel(
    plan,
    kern_count,
    tile_count,
    own_ref,
    other_ref,
    pair_ref,
    received_ref,
    quencher_ref,
    taps_ref,
    main_in_ref,
    strip_in_ref,
    weight_ref,
    intensity_ref,
    acid_ref,
    base_ref,
    main_ref,
    strip_ref,
    main_total_ref,
    strip_total_ref,
    image_ref,
    result_ref,
    result_sem,
):
    kern, tile = lax.axis_index("kern"), lax.axis_index("tile")
    rows, ambit = plan.rows, plan.ambit
    planes = taps_ref.shape[0] // plan.tap_groups

    def far_rows(step):
        place = jnp.clip(tile + step, 0, tile_count - 1)
        inside_tile = jnp.logical_and(tile + step >= 0, tile + step < tile_count)
        blocks = []
        for side in (-1, 0, 1):
            column = jnp.clip(kern + side, 0, kern_count - 1)
            inside = jnp.logical_and(kern + side >= 0, kern + side < kern_count)
            block = received_ref[column, place]
            blocks.append(jnp.where(jnp.logical_and(inside, inside_tile), block, 0.0))
        return lane_roll_left(jnp.concatenate(blocks, axis=1), LANES - plan.lead)[:, : 2 * LANES]

    even = tile % 2 == 0
    pair, other = pair_ref[...], other_ref[...]
    above, below = jnp.where(even, other, pair), jnp.where(even, pair, other)
    window = jnp.concatenate([far_rows(-2), above, own_ref[...], below, far_rows(2)], axis=0)
    shifts = Shifts(window, ambit, 0, main_ref, strip_ref)
    first_row = {"upper": 0, "lower": 0}
    refs, sources = (main_total_ref, strip_total_ref), (main_in_ref, strip_in_ref)
    weight = weight_ref[:, :1]

    def write_image():
        write_main_rows(image_ref, weight, main_total_ref, range(plan.groups))
        for group in range(plan.strip_groups):
            summed = weighted_rows(weight, strip_total_ref, group)
            for part in range(16):
                row = 16 * group + part
                half = summed[:, LANES * (part // 8) : LANES * (part // 8 + 1)]
                image_ref[row : row + 1, LANES:] = lane_roll_left(half, 16 * (part % 8))

    below_is_new = jnp.logical_not(even)
    add_side(
        plan, below_is_new, refs, sources, taps_ref, shifts, first_row, after=("top", "bottom"), then=write_image
    )

    image = image_ref[...]
    row_id = lax.broadcasted_iota(jnp.int32, image.shape, 0)
    lane_id = lax.broadcasted_iota(jnp.int32, image.shape, 1)
    at_row = tile * rows + row_id - RIM
    at_column = kern * LANES + lane_id - RIM
    valid = (at_row >= 0) & (at_row < tile_count * rows) & (at_column >= 0) & (at_column < kern_count * LANES)
    valid = valid & (lane_id < LANES + 2 * RIM)

    def rim_rows(step):
        place = jnp.clip(tile + step, 0, tile_count - 1)
        return jnp.concatenate(
            [received_ref[jnp.clip(kern + side, 0, kern_count - 1), place] for side in (-1, 0, 1)], axis=1
        )

    before = received_ref[jnp.clip(kern - 1, 0, kern_count - 1), tile]
    after = received_ref[jnp.clip(kern + 1, 0, kern_count - 1), tile]
    middle = [
        jnp.concatenate(
            [
                lane_roll_left(before, RIM * part + RIM),
                quencher_ref[RIM * part : RIM * part + RIM, :],
                lane_roll_left(after, RIM * part),
            ],
            axis=1,
        )
        for part in range(rows // RIM)
    ]
    base = jnp.concatenate([rim_rows(-1)] + middle + [rim_rows(1)], axis=0)
    base = lane_roll_left(base, LANES - RIM)[:, : 2 * LANES]
    base = jnp.where(valid, base, 0.0)
    acid = jnp.where(valid, 1.0 - jnp.exp(-EXPOSURE * image), 0.0)

    def spread(value):
        return (
            pltpu.roll(value, 1, 0)
            + pltpu.roll(value, value.shape[0] - 1, 0)
            + pltpu.roll(value, 1, 1)
            + pltpu.roll(value, value.shape[1] - 1, 1)
            - 4.0 * value
        )

    sent = []

    def send_out(place, value, ref):
        result_ref[place] = lane_roll_left(value, RIM)[RIM : RIM + rows, :LANES]
        sent.append(pltpu.make_async_copy(result_ref.at[place], ref, result_sem.at[place]))
        sent[-1].start()

    send_out(0, image, intensity_ref)
    for _ in range(STEPS):
        quenched = QUENCH_RATE * acid * base
        acid, base = (
            jnp.where(valid, acid + DIFFUSE_ACID * spread(acid) - quenched, 0.0),
            jnp.where(valid, base + DIFFUSE_BASE * spread(base) - quenched, 0.0),
        )
    send_out(1, acid, acid_ref)
    send_out(2, base, base_ref)
    for copy_out in sent:
        copy_out.wait()


def on_device(mask, kernels, socs_weights, quencher):
    ambit = kernels.shape[2]
    planes = kernels.shape[0] * kernels.shape[1]
    kern_count, tile_count = lax.axis_size("kern"), lax.axis_size("tile")
    rows = mask.shape[0]
    plan = Plan(rows, ambit)
    vmem = pl.BlockSpec(memory_space=pltpu.VMEM)
    limit = pltpu.CompilerParams(vmem_limit_bytes=24 * 1024 * 1024)

    send, window = pl.pallas_call(
        functools.partial(prepare_kernel, kern_count, tile_count, plan.lead),
        out_shape=(
            jax.ShapeDtypeStruct((kern_count, tile_count, RIM, LANES), jnp.float32),
            jax.ShapeDtypeStruct((rows, 2 * LANES), jnp.float32),
        ),
        cost_estimate=pl.CostEstimate(flops=10**9, bytes_accessed=10**7, transcendentals=0),
        name="prepare",
    )(mask, quencher)
    received = lax.all_to_all(
        send.reshape(kern_count * tile_count, RIM, LANES), ("kern", "tile"), 0, 0, tiled=True
    ).reshape(send.shape)
    pair = swapped(window, "tile", 0)
    other = swapped(window, "tile", 1)

    main_total = jax.ShapeDtypeStruct((plan.groups * planes, 4 * LANES), jnp.float32)
    strip_total = jax.ShapeDtypeStruct((plan.strip_groups * planes, 2 * LANES), jnp.float32)
    taps, *totals, weight, own = pl.pallas_call(
        functools.partial(near_rows_kernel, plan, kern_count),
        out_shape=(
            jax.ShapeDtypeStruct((plan.tap_groups * planes, GROUP * ambit), jnp.bfloat16),
            main_total,
            strip_total,
            jax.ShapeDtypeStruct((planes, LANES), jnp.float32),
            jax.ShapeDtypeStruct(window.shape, jnp.float32),
        ),
        in_specs=[vmem] * 4,
        out_specs=(vmem,) * 5,
        scratch_shapes=[pltpu.VMEM((2 * rows * ambit, LANES), jnp.bfloat16)] * 2,
        compiler_params=limit,
        name="near_rows",
    )(kernels, socs_weights, mask, pair)
    block = jax.ShapeDtypeStruct((rows, LANES), jnp.float32)
    return pl.pallas_call(
        functools.partial(resist_kernel, plan, kern_count, tile_count),
        out_shape=(block, block, block),
        in_specs=[vmem] * 9,
        out_specs=(pl.BlockSpec(memory_space=pl.ANY),) * 3,
        scratch_shapes=[pltpu.VMEM((plan.span * ambit, LANES), jnp.bfloat16)] * 2
        + [
            pltpu.VMEM(main_total.shape, jnp.float32),
            pltpu.VMEM(strip_total.shape, jnp.float32),
            pltpu.VMEM((plan.height, 2 * LANES), jnp.float32),
            pltpu.VMEM((3, rows, LANES), jnp.float32),
            pltpu.SemaphoreType.DMA((3,)),
        ],
        compiler_params=limit,
        name="image_and_resist",
    )(own, other, pair, received, quencher, taps, *totals, weight)


def solution(mesh):
    placed = (P("tile", None), P(), P(), P("tile", "kern"))
    return jax.shard_map(
        on_device,
        mesh=mesh,
        in_specs=placed,
        out_specs=(P("tile", "kern"), P("tile", "kern"), P("tile", "kern")),
        check_vma=False,
    )
```

```python
import copy
import functools

import jax
import jax.numpy as jnp
from jax import lax
from jax.experimental import pallas as pl
from jax.experimental.pallas import tpu as pltpu
from jax.sharding import PartitionSpec as P

STEPS = 8
DIFFUSE_ACID = 0.2
DIFFUSE_BASE = 0.1
QUENCH_RATE = 0.5
EXPOSURE = 0.35

LANES = 128
RIM = 8
GROUP = 4
WORD = 16


def lane_roll_left(value, amount):
    width = value.shape[1]
    amount %= width
    return value if amount == 0 else pltpu.roll(value, width - amount, 1)


def three_blocks(ref, rows, kern, kern_count):
    blocks = []
    for step in (-1, 0, 1):
        place = jnp.clip(kern + step, 0, kern_count - 1)
        block = ref[rows, pl.ds(pl.multiple_of(place * LANES, LANES), LANES)].astype(jnp.float32)
        inside = jnp.logical_and(kern + step >= 0, kern + step < kern_count)
        blocks.append(jnp.where(inside, block, 0.0))
    return jnp.concatenate(blocks, axis=1)


def own_window(mask_ref, kern, kern_count, lead):
    blocks = three_blocks(mask_ref, slice(None), kern, kern_count)
    return lane_roll_left(blocks, LANES - lead)[:, : 2 * LANES]


def turn_kernel(turned_ref):
    row = lax.broadcasted_iota(jnp.int32, turned_ref.shape, 0)
    lane = lax.broadcasted_iota(jnp.int32, turned_ref.shape, 1)
    turned_ref[...] = jnp.where(row == (lane ^ 7), 1.0, 0.0).astype(jnp.bfloat16)


def rim_kernel(
    kern_count, lead, _, mask_ref, quencher_ref, beside_ref, across_ref, wide_ref, for_pair_ref, for_other_ref
):
    rows = mask_ref.shape[0]
    kern = lax.axis_index("kern")
    odd = kern % 2 == 1
    window = own_window(mask_ref, kern, kern_count, lead)
    beside, across = beside_ref[...], across_ref[...]
    before, after = jnp.where(odd, beside, across), jnp.where(odd, across, beside)
    wide = jnp.concatenate([before, quencher_ref[...], after], axis=1)
    wide = lane_roll_left(wide, LANES - RIM)[:, : 2 * LANES]
    wide_ref[...] = wide
    first, last = wide[:RIM], wide[rows - RIM :]
    even = lax.axis_index("tile") % 2 == 0
    for ref, rim in ((for_pair_ref, jnp.where(even, last, first)), (for_other_ref, jnp.where(even, first, last))):
        ref[:rows, :] = window
        ref[rows:, :] = rim


def swapped(value, axis, first, step=1):
    count = lax.axis_size(axis)
    pairs = [
        (low, low + step) for low in range(count - step) if low // step >= first and (low // step - first) % 2 == 0
    ]
    return lax.ppermute(value, axis, pairs + [(high, low) for low, high in pairs])


def mask_words(window):
    bits = window.astype(jnp.int32)
    row = lax.broadcasted_iota(jnp.int32, (WORD, bits.shape[1]), 0)
    count = bits.shape[0] // WORD
    low = [
        jnp.sum(bits[WORD * w : WORD * (w + 1)] << row, axis=0, keepdims=True) for w in range(count)
    ]
    return [low[w] + (((low[w + 1] & 0xFF) << WORD) if w + 1 < count else 0) for w in range(count)]


class Shifts:
    def __init__(self, window, ambit, first_row, main_ref, strip_ref):
        words = mask_words(window)
        slanted = [
            pltpu.roll(jnp.broadcast_to(word, (8, 2 * LANES)), 2 * LANES - 7, 1, stride=1, stride_axis=0)
            for word in words
        ]
        slanted = jnp.concatenate(slanted, axis=0)
        low, high = slanted[:, :LANES], slanted[:, LANES:]
        lane = lax.broadcasted_iota(jnp.int32, low.shape, 1)
        mains, strips = [], []
        for offset in range(0, ambit, 8):
            mains.append(lane_roll_left(jnp.where(lane < offset, high, low), offset))
            strip = lane_roll_left(high, offset)
            for width in (16, 32, 64):
                strip = jnp.where(lane < width, strip, pltpu.roll(strip, width, 1))
            strips.append(strip >> (lane // 16))
        self.ambit, self.first_row = ambit, first_row
        self.sources = {"main": mains, "strip": strips}
        self.refs = {"main": main_ref, "strip": strip_ref}
        self.laid = {"main": set(), "strip": set()}

    def view(self, first_row):
        view = copy.copy(self)
        view.first_row, view.laid = first_row, {"main": set(), "strip": set()}
        return view

    def lay(self, kind, rows):
        for row in rows:
            row -= self.first_row
            if row in self.laid[kind]:
                continue
            self.laid[kind].add(row)
            word, bit = divmod(row, WORD)
            source = self.sources[kind]
            for pair in range(self.ambit // 16):
                value = jnp.concatenate(
                    [source[2 * pair + part][8 * word : 8 * word + 8] for part in range(2)], axis=0
                )
                plane = ((value >> bit) & 1).astype(jnp.float32).astype(jnp.bfloat16)
                at = self.ambit * row + 16 * pair
                self.refs[kind][at : at + 16, :] = plane


class Total:
    def __init__(self, ref, source, planes):
        self.ref, self.source, self.planes = ref, source, planes
        self.waiting = {
            (group, half)
            for group in range(ref.shape[0] // planes)
            for half in range(ref.shape[1] // (2 * LANES))
        }

    def add(self, first, last, half, value):
        lanes = slice(2 * LANES * half, 2 * LANES * (half + 1))
        group = first
        while group <= last:
            fresh, end = (group, half) in self.waiting, group
            while end <= last and ((end, half) in self.waiting) == fresh:
                self.waiting.discard((end, half))
                end += 1
            place = (slice(self.planes * group, self.planes * end), lanes)
            piece = value[self.planes * (group - first) : self.planes * (end - first)]
            if not fresh:
                piece = self.ref[place] + piece
            elif self.source is not None:
                piece = self.source[place] + piece
            self.ref[place] = piece
            group = end

    def finish(self):
        for group, half in sorted(self.waiting):
            lanes = slice(2 * LANES * half, 2 * LANES * (half + 1))
            place = (slice(self.planes * group, self.planes * (group + 1)), lanes)
            self.ref[place] = jnp.zeros_like(self.ref[place]) if self.source is None else self.source[place]
        self.waiting = set()


def add_main(plan, total, taps_ref, shifts, s):
    groups, tap_groups, ambit = plan.groups, plan.tap_groups, plan.ambit
    planes = total.planes
    shifts.lay("main", plan.main[s])
    main_ref = shifts.refs["main"]
    first, last = max(0, s - tap_groups + 1), min(groups - 1, s)
    taps = taps_ref[planes * (tap_groups - 1 - s + first) : planes * (tap_groups - s + last), :]
    depth = GROUP * ambit
    for half in range(2):
        at = ambit * (GROUP * s + 2 * half - shifts.first_row)
        moved = jnp.concatenate([main_ref[at : at + depth], main_ref[at + ambit : at + ambit + depth]], axis=1)
        total.add(first, last, half, jnp.dot(taps, moved, preferred_element_type=jnp.float32))


def add_strip(plan, total, taps_ref, shifts, s):
    groups, tap_groups, ambit = plan.groups, plan.tap_groups, plan.ambit
    planes = total.planes
    shifts.lay("strip", plan.strip[s])
    strip_ref = shifts.refs["strip"]
    members = [g for g in range(groups // GROUP) if 0 <= s - GROUP * g < tap_groups]
    pieces = [tap_groups - 1 - s + GROUP * g for g in members]
    taps = jnp.concatenate([taps_ref[planes * p : planes * (p + 1), :] for p in pieces], axis=0)
    depth = GROUP * ambit
    at = ambit * (GROUP * s - shifts.first_row)
    moved = jnp.concatenate(
        [strip_ref[at : at + depth], strip_ref[at + 8 * ambit : at + 8 * ambit + depth]], axis=1
    )
    total.add(members[0], members[-1], 0, jnp.dot(taps, moved, preferred_element_type=jnp.float32))


class Plan:
    def __init__(self, rows, ambit):
        self.rows, self.ambit = rows, ambit
        self.lead = ambit // 2 + RIM
        self.height, self.span = rows + 2 * RIM, rows + 2 * self.lead
        self.groups, self.tap_groups = self.height // GROUP, ambit // GROUP
        self.strip_groups = self.height // 16
        main = {s: range(GROUP * s, GROUP * s + 7) for s in range(self.groups + self.tap_groups - 1)}
        strip = {
            s: range(GROUP * s, GROUP * s + 12) for s in range(GROUP * (self.strip_groups - 1) + self.tap_groups)
        }
        self.main, self.strip = main, strip
        first, middle, last = RIM, self.lead, self.lead + rows
        self.parts = {}
        taken = {"main": set(), "strip": set()}
        for name, low, high in (
            ("own", middle, last),
            ("upper", first, last),
            ("lower", middle, last + rows),
            ("top", 0, last),
            ("bottom", middle, self.span),
        ):
            self.parts[name] = {}
            for kind, steps, reach in (("main", main, 0), ("strip", strip, 7)):
                chosen = [
                    s for s, used in steps.items()
                    if s not in taken[kind] and low <= used[0] and used[-1] + reach < high
                ]
                taken[kind].update(chosen)
                self.parts[name][kind] = chosen
        assert taken == {"main": set(main), "strip": set(strip)}

    def add(self, name, totals, taps_ref, shifts):
        for s in self.parts[name]["main"]:
            add_main(self, totals[0], taps_ref, shifts, s)
        for s in self.parts[name]["strip"]:
            add_strip(self, totals[1], taps_ref, shifts, s)


def near_rows_kernel(
    plan,
    kernels_ref,
    weights_ref,
    turned_ref,
    own_ref,
    pair_ref,
    taps_ref,
    main_total_ref,
    strip_total_ref,
    weight_ref,
    main_ref,
    strip_ref,
):
    ambit = plan.ambit
    planes = kernels_ref.shape[0] * kernels_ref.shape[1]
    wanted = (weight_ref.shape[0], weights_ref.shape[0])
    plane = lax.broadcasted_iota(jnp.int32, wanted, 0)
    member = lax.broadcasted_iota(jnp.int32, wanted, 1)
    spread = jnp.broadcast_to(weights_ref[...].reshape(1, wanted[1]), wanted)
    column = jnp.sum(jnp.where(plane // 2 == member, spread, 0.0), axis=1, keepdims=True)
    weight_ref[...] = jnp.broadcast_to(column, weight_ref.shape)
    turned = turned_ref[...]
    by_row = jnp.transpose(kernels_ref[...].reshape(planes, ambit, ambit), (1, 0, 2))
    for group in range(plan.tap_groups):
        pieces = [by_row[GROUP * group + part] for part in range(GROUP)]
        place = planes * (plan.tap_groups - 1 - group)
        taps = jnp.concatenate(pieces, axis=1)
        taps = jnp.dot(taps, turned, preferred_element_type=jnp.float32)
        taps_ref[place : place + planes, :] = taps.astype(jnp.bfloat16)
    even = lax.axis_index("tile") % 2 == 0
    own, pair = own_ref[: plan.rows], pair_ref[: plan.rows]
    window = jnp.concatenate([jnp.where(even, own, pair), jnp.where(even, pair, own)], axis=0)
    shifts = Shifts(window, ambit, 0, main_ref, strip_ref)
    first_row = {"upper": RIM, "lower": plan.lead}
    add_side(plan, even, (main_total_ref, strip_total_ref), (None, None), taps_ref, shifts, first_row, before=("own",))


def weighted_rows(weight, total_ref, group):
    planes = weight.shape[0]
    field = total_ref[planes * group : planes * (group + 1), :]
    return jnp.sum(weight * (field * field), axis=0, keepdims=True)


def write_main_rows(image_ref, weight, total_ref, groups):
    for group in groups:
        summed = weighted_rows(weight, total_ref, group)
        for part in range(GROUP):
            row = GROUP * group + part
            image_ref[row : row + 1, :LANES] = summed[:, LANES * part : LANES * (part + 1)]


def add_side(plan, below, refs, sources, taps_ref, shifts, first_row, before=(), after=(), then=None):
    planes = taps_ref.shape[0] // plan.tap_groups

    def add(name):
        totals = [Total(ref, source, planes) for ref, source in zip(refs, sources)]
        view = shifts.view(first_row[name])
        for part in (*before, name, *after):
            plan.add(part, totals, taps_ref, view)
        for total in totals:
            total.finish()
        if then is not None:
            then()

    pl.when(below)(lambda: add("lower"))
    pl.when(jnp.logical_not(below))(lambda: add("upper"))


def resist_kernel(
    plan,
    kern_count,
    tile_count,
    own_ref,
    other_ref,
    pair_ref,
    far_pair_ref,
    far_other_ref,
    wide_ref,
    taps_ref,
    main_in_ref,
    strip_in_ref,
    weight_ref,
    intensity_ref,
    acid_ref,
    base_ref,
    main_ref,
    strip_ref,
    main_total_ref,
    strip_total_ref,
    image_ref,
    result_ref,
    result_sem,
):
    kern, tile = lax.axis_index("kern"), lax.axis_index("tile")
    rows, ambit = plan.rows, plan.ambit
    planes = taps_ref.shape[0] // plan.tap_groups

    def far_rows(above_tile):
        place = slice(rows - RIM, rows) if above_tile else slice(RIM)
        blocks = [three_blocks(ref, place, kern, kern_count) for ref in (far_pair_ref, far_other_ref)]
        with_pair = ((tile // 2) % 2 == 1) == above_tile
        chosen = jnp.where(with_pair, blocks[0], blocks[1])
        return lane_roll_left(chosen, LANES - plan.lead)[:, : 2 * LANES]

    even = tile % 2 == 0
    pair, other = pair_ref[...], other_ref[...]
    above, below = jnp.where(even, other, pair), jnp.where(even, pair, other)
    window = jnp.concatenate(
        [far_rows(True), above[:rows], own_ref[:rows], below[:rows], far_rows(False)], axis=0
    )
    shifts = Shifts(window, ambit, 0, main_ref, strip_ref)
    first_row = {"upper": 0, "lower": 0}
    refs, sources = (main_total_ref, strip_total_ref), (main_in_ref, strip_in_ref)
    weight = weight_ref[:, :1]

    def write_image():
        write_main_rows(image_ref, weight, main_total_ref, range(plan.groups))
        for group in range(plan.strip_groups):
            summed = weighted_rows(weight, strip_total_ref, group)
            for part in range(16):
                row = 16 * group + part
                half = summed[:, LANES * (part // 8) : LANES * (part // 8 + 1)]
                image_ref[row : row + 1, LANES:] = lane_roll_left(half, 16 * (part % 8))

    below_is_new = jnp.logical_not(even)
    add_side(
        plan, below_is_new, refs, sources, taps_ref, shifts, first_row, after=("top", "bottom"), then=write_image
    )

    image = image_ref[...]
    row_id = lax.broadcasted_iota(jnp.int32, image.shape, 0)
    lane_id = lax.broadcasted_iota(jnp.int32, image.shape, 1)
    at_row = tile * rows + row_id - RIM
    at_column = kern * LANES + lane_id - RIM
    valid = (at_row >= 0) & (at_row < tile_count * rows) & (at_column >= 0) & (at_column < kern_count * LANES)
    valid = valid & (lane_id < LANES + 2 * RIM)

    base = jnp.concatenate([above[rows:], wide_ref[...], below[rows:]], axis=0)
    base = jnp.where(valid, base, 0.0)
    acid = jnp.where(valid, 1.0 - jnp.exp(-EXPOSURE * image), 0.0)

    def spread(value):
        return (
            pltpu.roll(value, 1, 0)
            + pltpu.roll(value, value.shape[0] - 1, 0)
            + pltpu.roll(value, 1, 1)
            + pltpu.roll(value, value.shape[1] - 1, 1)
            - 4.0 * value
        )

    sent = []

    def send_out(place, value, ref):
        result_ref[place] = lane_roll_left(value, RIM)[RIM : RIM + rows, :LANES]
        sent.append(pltpu.make_async_copy(result_ref.at[place], ref, result_sem.at[place]))
        sent[-1].start()

    send_out(0, image, intensity_ref)
    for _ in range(STEPS):
        quenched = QUENCH_RATE * acid * base
        acid, base = (
            jnp.where(valid, acid + DIFFUSE_ACID * spread(acid) - quenched, 0.0),
            jnp.where(valid, base + DIFFUSE_BASE * spread(base) - quenched, 0.0),
        )
    send_out(1, acid, acid_ref)
    send_out(2, base, base_ref)
    for copy_out in sent:
        copy_out.wait()


def on_device(mask, kernels, socs_weights, quencher):
    ambit = kernels.shape[2]
    planes = kernels.shape[0] * kernels.shape[1]
    kern_count, tile_count = lax.axis_size("kern"), lax.axis_size("tile")
    rows = mask.shape[0]
    plan = Plan(rows, ambit)
    vmem = pl.BlockSpec(memory_space=pltpu.VMEM)
    limit = pltpu.CompilerParams(vmem_limit_bytes=24 * 1024 * 1024)

    assert kern_count <= 4
    turned = pl.pallas_call(
        turn_kernel,
        out_shape=jax.ShapeDtypeStruct((GROUP * ambit, GROUP * ambit), jnp.bfloat16),
        out_specs=vmem,
        compiler_params=limit,
        cost_estimate=pl.CostEstimate(flops=10**9, bytes_accessed=10**7, transcendentals=0),
        name="turned",
    )()
    across = swapped(quencher, "kern", 0, 2)
    far_pair = swapped(mask, "tile", 0, 2)
    beside = swapped(quencher, "kern", 0)
    across = swapped(across, "kern", 0)
    far_other = swapped(mask, "tile", 1, 2)
    sent = jax.ShapeDtypeStruct((rows + RIM, 2 * LANES), jnp.float32)
    wide, for_pair, for_other = pl.pallas_call(
        functools.partial(rim_kernel, kern_count, plan.lead),
        out_shape=(jax.ShapeDtypeStruct((rows, 2 * LANES), jnp.float32), sent, sent),
        in_specs=[vmem] * 5,
        out_specs=(vmem,) * 3,
        compiler_params=limit,
        name="rims",
    )(turned, mask, quencher, beside, across)
    pair = swapped(for_pair, "tile", 0)
    other = swapped(for_other, "tile", 1)

    main_total = jax.ShapeDtypeStruct((plan.groups * planes, 4 * LANES), jnp.float32)
    strip_total = jax.ShapeDtypeStruct((plan.strip_groups * planes, 2 * LANES), jnp.float32)
    taps, *totals, weight = pl.pallas_call(
        functools.partial(near_rows_kernel, plan),
        out_shape=(
            jax.ShapeDtypeStruct((plan.tap_groups * planes, GROUP * ambit), jnp.bfloat16),
            main_total,
            strip_total,
            jax.ShapeDtypeStruct((planes, LANES), jnp.float32),
        ),
        in_specs=[vmem] * 5,
        out_specs=(vmem,) * 4,
        scratch_shapes=[pltpu.VMEM((2 * rows * ambit, LANES), jnp.bfloat16)] * 2,
        compiler_params=limit,
        name="near_rows",
    )(kernels, socs_weights, turned, for_pair, pair)
    block = jax.ShapeDtypeStruct((rows, LANES), jnp.float32)
    return pl.pallas_call(
        functools.partial(resist_kernel, plan, kern_count, tile_count),
        out_shape=(block, block, block),
        in_specs=[vmem] * 10,
        out_specs=(pl.BlockSpec(memory_space=pl.ANY),) * 3,
        scratch_shapes=[pltpu.VMEM((plan.span * ambit, LANES), jnp.bfloat16)] * 2
        + [
            pltpu.VMEM(main_total.shape, jnp.float32),
            pltpu.VMEM(strip_total.shape, jnp.float32),
            pltpu.VMEM((plan.height, 2 * LANES), jnp.float32),
            pltpu.VMEM((3, rows, LANES), jnp.float32),
            pltpu.SemaphoreType.DMA((3,)),
        ],
        compiler_params=limit,
        name="image_and_resist",
    )(for_pair, other, pair, far_pair, far_other, wide, taps, *totals, weight)


def solution(mesh):
    placed = (P("tile", None), P(), P(), P("tile", "kern"))
    return jax.shard_map(
        on_device,
        mesh=mesh,
        in_specs=placed,
        out_specs=(P("tile", "kern"), P("tile", "kern"), P("tile", "kern")),
        check_vma=False,
    )
```

```python
import copy
import functools

import jax
import jax.numpy as jnp
from jax import lax
from jax.experimental import pallas as pl
from jax.experimental.pallas import tpu as pltpu
from jax.sharding import PartitionSpec as P

STEPS = 8
DIFFUSE_ACID = 0.2
DIFFUSE_BASE = 0.1
QUENCH_RATE = 0.5
EXPOSURE = 0.35

LANES = 128
RIM = 8
GROUP = 4
WORD = 16


def lane_roll_left(value, amount):
    width = value.shape[1]
    amount %= width
    return value if amount == 0 else pltpu.roll(value, width - amount, 1)


def three_blocks(ref, rows, kern, kern_count):
    blocks = []
    for step in (-1, 0, 1):
        place = jnp.clip(kern + step, 0, kern_count - 1)
        block = ref[rows, pl.ds(pl.multiple_of(place * LANES, LANES), LANES)].astype(jnp.float32)
        inside = jnp.logical_and(kern + step >= 0, kern + step < kern_count)
        blocks.append(jnp.where(inside, block, 0.0))
    return jnp.concatenate(blocks, axis=1)


def own_window(mask_ref, kern, kern_count, lead):
    blocks = three_blocks(mask_ref, slice(None), kern, kern_count)
    return lane_roll_left(blocks, LANES - lead)[:, : 2 * LANES]


def turn_kernel(turned_ref):
    row = lax.broadcasted_iota(jnp.int32, turned_ref.shape, 0)
    lane = lax.broadcasted_iota(jnp.int32, turned_ref.shape, 1)
    turned_ref[...] = jnp.where(row == (lane ^ 7), 1.0, 0.0).astype(jnp.bfloat16)


def rim_kernel(
    kern_count, lead, _, mask_ref, quencher_ref, beside_ref, across_ref, window_ref, wide_ref, for_pair_ref, for_other_ref
):
    rows = mask_ref.shape[0]
    kern = lax.axis_index("kern")
    odd = kern % 2 == 1
    window = own_window(mask_ref, kern, kern_count, lead)
    window_ref[...] = window
    beside, across = beside_ref[...], across_ref[...]
    before, after = jnp.where(odd, beside, across), jnp.where(odd, across, beside)
    wide = jnp.concatenate([before, quencher_ref[...], after], axis=1)
    wide = lane_roll_left(wide, LANES - RIM)[:, : 2 * LANES]
    wide_ref[...] = wide
    first, last = wide[:RIM], wide[rows - RIM :]
    even = lax.axis_index("tile") % 2 == 0
    for ref, rim in ((for_pair_ref, jnp.where(even, last, first)), (for_other_ref, jnp.where(even, first, last))):
        ref[:rows, :] = window
        ref[rows:, :] = rim


def swapped(value, axis, first, step=1):
    count = lax.axis_size(axis)
    pairs = [
        (low, low + step) for low in range(count - step) if low // step >= first and (low // step - first) % 2 == 0
    ]
    return lax.ppermute(value, axis, pairs + [(high, low) for low, high in pairs])


def mask_words(window):
    bits = window.astype(jnp.int32)
    row = lax.broadcasted_iota(jnp.int32, (WORD, bits.shape[1]), 0)
    count = bits.shape[0] // WORD
    low = [
        jnp.sum(bits[WORD * w : WORD * (w + 1)] << row, axis=0, keepdims=True) for w in range(count)
    ]
    return [low[w] + (((low[w + 1] & 0xFF) << WORD) if w + 1 < count else 0) for w in range(count)]


class Shifts:
    def __init__(self, window, ambit, first_row, main_ref, strip_ref):
        words = mask_words(window)
        slanted = [
            pltpu.roll(jnp.broadcast_to(word, (8, 2 * LANES)), 2 * LANES - 7, 1, stride=1, stride_axis=0)
            for word in words
        ]
        slanted = jnp.concatenate(slanted, axis=0)
        low, high = slanted[:, :LANES], slanted[:, LANES:]
        lane = lax.broadcasted_iota(jnp.int32, low.shape, 1)
        mains, strips = [], []
        for offset in range(0, ambit, 8):
            mains.append(lane_roll_left(jnp.where(lane < offset, high, low), offset))
            strip = lane_roll_left(high, offset)
            for width in (16, 32, 64):
                strip = jnp.where(lane < width, strip, pltpu.roll(strip, width, 1))
            strips.append(strip >> (lane // 16))
        self.ambit, self.first_row = ambit, first_row
        self.sources = {"main": mains, "strip": strips}
        self.refs = {"main": main_ref, "strip": strip_ref}
        self.laid = {"main": set(), "strip": set()}

    def view(self, first_row):
        view = copy.copy(self)
        view.first_row, view.laid = first_row, {"main": set(), "strip": set()}
        return view

    def lay(self, kind, rows):
        for row in rows:
            row -= self.first_row
            if row in self.laid[kind]:
                continue
            self.laid[kind].add(row)
            word, bit = divmod(row, WORD)
            source = self.sources[kind]
            for pair in range(self.ambit // 16):
                value = jnp.concatenate(
                    [source[2 * pair + part][8 * word : 8 * word + 8] for part in range(2)], axis=0
                )
                plane = ((value >> bit) & 1).astype(jnp.float32).astype(jnp.bfloat16)
                at = self.ambit * row + 16 * pair
                self.refs[kind][at : at + 16, :] = plane


class Total:
    def __init__(self, ref, source, planes):
        self.ref, self.source, self.planes = ref, source, planes
        self.waiting = {
            (group, half)
            for group in range(ref.shape[0] // planes)
            for half in range(ref.shape[1] // (2 * LANES))
        }

    def add(self, first, last, half, value):
        lanes = slice(2 * LANES * half, 2 * LANES * (half + 1))
        group = first
        while group <= last:
            fresh, end = (group, half) in self.waiting, group
            while end <= last and ((end, half) in self.waiting) == fresh:
                self.waiting.discard((end, half))
                end += 1
            place = (slice(self.planes * group, self.planes * end), lanes)
            piece = value[self.planes * (group - first) : self.planes * (end - first)]
            if not fresh:
                piece = self.ref[place] + piece
            elif self.source is not None:
                piece = self.source[place] + piece
            self.ref[place] = piece
            group = end

    def finish(self):
        for group, half in sorted(self.waiting):
            lanes = slice(2 * LANES * half, 2 * LANES * (half + 1))
            place = (slice(self.planes * group, self.planes * (group + 1)), lanes)
            self.ref[place] = jnp.zeros_like(self.ref[place]) if self.source is None else self.source[place]
        self.waiting = set()


def add_main(plan, total, taps_ref, shifts, s):
    groups, tap_groups, ambit = plan.groups, plan.tap_groups, plan.ambit
    planes = total.planes
    shifts.lay("main", plan.main[s])
    main_ref = shifts.refs["main"]
    first, last = max(0, s - tap_groups + 1), min(groups - 1, s)
    taps = taps_ref[planes * (tap_groups - 1 - s + first) : planes * (tap_groups - s + last), :]
    depth = GROUP * ambit
    for half in range(2):
        at = ambit * (GROUP * s + 2 * half - shifts.first_row)
        moved = jnp.concatenate([main_ref[at : at + depth], main_ref[at + ambit : at + ambit + depth]], axis=1)
        total.add(first, last, half, jnp.dot(taps, moved, preferred_element_type=jnp.float32))


def add_strip(plan, total, taps_ref, shifts, s):
    groups, tap_groups, ambit = plan.groups, plan.tap_groups, plan.ambit
    planes = total.planes
    shifts.lay("strip", plan.strip[s])
    strip_ref = shifts.refs["strip"]
    members = [g for g in range(groups // GROUP) if 0 <= s - GROUP * g < tap_groups]
    pieces = [tap_groups - 1 - s + GROUP * g for g in members]
    taps = jnp.concatenate([taps_ref[planes * p : planes * (p + 1), :] for p in pieces], axis=0)
    depth = GROUP * ambit
    at = ambit * (GROUP * s - shifts.first_row)
    moved = jnp.concatenate(
        [strip_ref[at : at + depth], strip_ref[at + 8 * ambit : at + 8 * ambit + depth]], axis=1
    )
    total.add(members[0], members[-1], 0, jnp.dot(taps, moved, preferred_element_type=jnp.float32))


class Plan:
    def __init__(self, rows, ambit):
        self.rows, self.ambit = rows, ambit
        self.lead = ambit // 2 + RIM
        self.height, self.span = rows + 2 * RIM, rows + 2 * self.lead
        self.groups, self.tap_groups = self.height // GROUP, ambit // GROUP
        self.strip_groups = self.height // 16
        main = {s: range(GROUP * s, GROUP * s + 7) for s in range(self.groups + self.tap_groups - 1)}
        strip = {
            s: range(GROUP * s, GROUP * s + 12) for s in range(GROUP * (self.strip_groups - 1) + self.tap_groups)
        }
        self.main, self.strip = main, strip
        first, middle, last = RIM, self.lead, self.lead + rows
        self.parts = {}
        taken = {"main": set(), "strip": set()}
        for name, low, high in (
            ("own", middle, last),
            ("upper", first, last),
            ("lower", middle, last + rows),
            ("top", 0, last),
            ("bottom", middle, self.span),
        ):
            self.parts[name] = {}
            for kind, steps, reach in (("main", main, 0), ("strip", strip, 7)):
                chosen = [
                    s for s, used in steps.items()
                    if s not in taken[kind] and low <= used[0] and used[-1] + reach < high
                ]
                taken[kind].update(chosen)
                self.parts[name][kind] = chosen
        assert taken == {"main": set(main), "strip": set(strip)}

    def add(self, name, totals, taps_ref, shifts):
        for s in self.parts[name]["main"]:
            add_main(self, totals[0], taps_ref, shifts, s)
        for s in self.parts[name]["strip"]:
            add_strip(self, totals[1], taps_ref, shifts, s)


def own_rows_kernel(
    plan,
    kernels_ref,
    weights_ref,
    turned_ref,
    window_ref,
    taps_ref,
    main_total_ref,
    strip_total_ref,
    weight_ref,
    main_ref,
    strip_ref,
):
    ambit = plan.ambit
    planes = kernels_ref.shape[0] * kernels_ref.shape[1]
    wanted = (weight_ref.shape[0], weights_ref.shape[0])
    plane = lax.broadcasted_iota(jnp.int32, wanted, 0)
    member = lax.broadcasted_iota(jnp.int32, wanted, 1)
    spread = jnp.broadcast_to(weights_ref[...].reshape(1, wanted[1]), wanted)
    column = jnp.sum(jnp.where(plane // 2 == member, spread, 0.0), axis=1, keepdims=True)
    weight_ref[...] = jnp.broadcast_to(column, weight_ref.shape)
    turned = turned_ref[...]
    by_row = jnp.transpose(kernels_ref[...].reshape(planes, ambit, ambit), (1, 0, 2))
    for group in range(plan.tap_groups):
        pieces = [by_row[GROUP * group + part] for part in range(GROUP)]
        place = planes * (plan.tap_groups - 1 - group)
        taps = jnp.concatenate(pieces, axis=1)
        taps = jnp.dot(taps, turned, preferred_element_type=jnp.float32)
        taps_ref[place : place + planes, :] = taps.astype(jnp.bfloat16)
    shifts = Shifts(window_ref[...], ambit, plan.lead, main_ref, strip_ref)
    totals = Total(main_total_ref, None, planes), Total(strip_total_ref, None, planes)
    plan.add("own", totals, taps_ref, shifts)
    for total in totals:
        total.finish()


def weighted_rows(weight, total_ref, group):
    planes = weight.shape[0]
    field = total_ref[planes * group : planes * (group + 1), :]
    return jnp.sum(weight * (field * field), axis=0, keepdims=True)


def write_main_rows(image_ref, weight, total_ref, groups):
    for group in groups:
        summed = weighted_rows(weight, total_ref, group)
        for part in range(GROUP):
            row = GROUP * group + part
            image_ref[row : row + 1, :LANES] = summed[:, LANES * part : LANES * (part + 1)]


def add_side(plan, below, refs, sources, taps_ref, shifts, first_row, after=(), then=None):
    planes = taps_ref.shape[0] // plan.tap_groups

    def add(name):
        totals = [Total(ref, source, planes) for ref, source in zip(refs, sources)]
        view = shifts.view(first_row[name])
        for part in (name, *after):
            plan.add(part, totals, taps_ref, view)
        for total in totals:
            total.finish()
        if then is not None:
            then()

    pl.when(below)(lambda: add("lower"))
    pl.when(jnp.logical_not(below))(lambda: add("upper"))


def pair_rows_kernel(
    plan,
    own_ref,
    pair_ref,
    taps_ref,
    main_in_ref,
    strip_in_ref,
    main_total_ref,
    strip_total_ref,
    main_ref,
    strip_ref,
):
    even = lax.axis_index("tile") % 2 == 0
    own, pair = own_ref[...], pair_ref[: plan.rows]
    window = jnp.concatenate([jnp.where(even, own, pair), jnp.where(even, pair, own)], axis=0)
    shifts = Shifts(window, plan.ambit, 0, main_ref, strip_ref)
    refs, sources = (main_total_ref, strip_total_ref), (main_in_ref, strip_in_ref)
    add_side(plan, even, refs, sources, taps_ref, shifts, {"upper": RIM, "lower": plan.lead})


def resist_kernel(
    plan,
    kern_count,
    tile_count,
    own_ref,
    other_ref,
    pair_ref,
    far_other_ref,
    far_pair_ref,
    wide_ref,
    taps_ref,
    main_in_ref,
    strip_in_ref,
    weight_ref,
    intensity_ref,
    acid_ref,
    base_ref,
    main_ref,
    strip_ref,
    main_total_ref,
    strip_total_ref,
    image_ref,
    result_ref,
    result_sem,
):
    kern, tile = lax.axis_index("kern"), lax.axis_index("tile")
    rows, ambit = plan.rows, plan.ambit
    planes = taps_ref.shape[0] // plan.tap_groups

    def far_rows(above_tile):
        place = slice(rows - RIM, rows) if above_tile else slice(RIM)
        blocks = [three_blocks(ref, place, kern, kern_count) for ref in (far_pair_ref, far_other_ref)]
        with_pair = ((tile // 2) % 2 == 1) == above_tile
        chosen = jnp.where(with_pair, blocks[0], blocks[1])
        return lane_roll_left(chosen, LANES - plan.lead)[:, : 2 * LANES]

    even = tile % 2 == 0
    pair, other = pair_ref[...], other_ref[...]
    above, below = jnp.where(even, other, pair), jnp.where(even, pair, other)
    window = jnp.concatenate(
        [far_rows(True), above[:rows], own_ref[...], below[:rows], far_rows(False)], axis=0
    )
    shifts = Shifts(window, ambit, 0, main_ref, strip_ref)
    first_row = {"upper": 0, "lower": 0}
    refs, sources = (main_total_ref, strip_total_ref), (main_in_ref, strip_in_ref)
    weight = weight_ref[:, :1]

    def write_image():
        write_main_rows(image_ref, weight, main_total_ref, range(plan.groups))
        for group in range(plan.strip_groups):
            summed = weighted_rows(weight, strip_total_ref, group)
            for part in range(16):
                row = 16 * group + part
                half = summed[:, LANES * (part // 8) : LANES * (part // 8 + 1)]
                image_ref[row : row + 1, LANES:] = lane_roll_left(half, 16 * (part % 8))

    below_is_new = jnp.logical_not(even)
    add_side(
        plan, below_is_new, refs, sources, taps_ref, shifts, first_row, after=("top", "bottom"), then=write_image
    )

    image = image_ref[...]
    row_id = lax.broadcasted_iota(jnp.int32, image.shape, 0)
    lane_id = lax.broadcasted_iota(jnp.int32, image.shape, 1)
    at_row = tile * rows + row_id - RIM
    at_column = kern * LANES + lane_id - RIM
    valid = (at_row >= 0) & (at_row < tile_count * rows) & (at_column >= 0) & (at_column < kern_count * LANES)
    valid = valid & (lane_id < LANES + 2 * RIM)

    base = jnp.concatenate([above[rows:], wide_ref[...], below[rows:]], axis=0)
    base = jnp.where(valid, base, 0.0)
    acid = jnp.where(valid, 1.0 - jnp.exp(-EXPOSURE * image), 0.0)

    def spread(value):
        return (
            pltpu.roll(value, 1, 0)
            + pltpu.roll(value, value.shape[0] - 1, 0)
            + pltpu.roll(value, 1, 1)
            + pltpu.roll(value, value.shape[1] - 1, 1)
            - 4.0 * value
        )

    sent = []

    def send_out(place, value, ref):
        result_ref[place] = lane_roll_left(value, RIM)[RIM : RIM + rows, :LANES]
        sent.append(pltpu.make_async_copy(result_ref.at[place], ref, result_sem.at[place]))
        sent[-1].start()

    send_out(0, image, intensity_ref)
    for _ in range(STEPS):
        quenched = QUENCH_RATE * acid * base
        acid, base = (
            jnp.where(valid, acid + DIFFUSE_ACID * spread(acid) - quenched, 0.0),
            jnp.where(valid, base + DIFFUSE_BASE * spread(base) - quenched, 0.0),
        )
    send_out(1, acid, acid_ref)
    send_out(2, base, base_ref)
    for copy_out in sent:
        copy_out.wait()


def on_device(mask, kernels, socs_weights, quencher):
    ambit = kernels.shape[2]
    planes = kernels.shape[0] * kernels.shape[1]
    kern_count, tile_count = lax.axis_size("kern"), lax.axis_size("tile")
    rows = mask.shape[0]
    plan = Plan(rows, ambit)
    vmem = pl.BlockSpec(memory_space=pltpu.VMEM)
    limit = pltpu.CompilerParams(vmem_limit_bytes=24 * 1024 * 1024)

    assert kern_count <= 4
    turned = pl.pallas_call(
        turn_kernel,
        out_shape=jax.ShapeDtypeStruct((GROUP * ambit, GROUP * ambit), jnp.bfloat16),
        out_specs=vmem,
        compiler_params=limit,
        cost_estimate=pl.CostEstimate(flops=10**9, bytes_accessed=10**7, transcendentals=0),
        name="turned",
    )()
    across = swapped(quencher, "kern", 0, 2)
    far_pair = swapped(mask, "tile", 0, 2)
    beside = swapped(quencher, "kern", 0)
    far_other = swapped(mask, "tile", 1, 2)
    main_total = jax.ShapeDtypeStruct((plan.groups * planes, 4 * LANES), jnp.float32)
    strip_total = jax.ShapeDtypeStruct((plan.strip_groups * planes, 2 * LANES), jnp.float32)
    wide_rows = jax.ShapeDtypeStruct((rows, 2 * LANES), jnp.float32)
    sent = jax.ShapeDtypeStruct((rows + RIM, 2 * LANES), jnp.float32)
    across = swapped(across, "kern", 0)
    window, wide, for_pair, for_other = pl.pallas_call(
        functools.partial(rim_kernel, kern_count, plan.lead),
        out_shape=(wide_rows, wide_rows, sent, sent),
        in_specs=[vmem] * 5,
        out_specs=(vmem,) * 4,
        compiler_params=limit,
        name="rims",
    )(turned, mask, quencher, beside, across)
    pair = swapped(for_pair, "tile", 0)
    other = swapped(for_other, "tile", 1)
    taps, *totals, weight = pl.pallas_call(
        functools.partial(own_rows_kernel, plan),
        out_shape=(
            jax.ShapeDtypeStruct((plan.tap_groups * planes, GROUP * ambit), jnp.bfloat16),
            main_total,
            strip_total,
            jax.ShapeDtypeStruct((planes, LANES), jnp.float32),
        ),
        in_specs=[vmem] * 4,
        out_specs=(vmem,) * 4,
        scratch_shapes=[pltpu.VMEM((rows * ambit, LANES), jnp.bfloat16)] * 2,
        compiler_params=limit,
        name="own_rows",
    )(kernels, socs_weights, turned, window)
    totals = pl.pallas_call(
        functools.partial(pair_rows_kernel, plan),
        out_shape=(main_total, strip_total),
        in_specs=[vmem] * 5,
        out_specs=(vmem,) * 2,
        scratch_shapes=[pltpu.VMEM((2 * rows * ambit, LANES), jnp.bfloat16)] * 2,
        compiler_params=limit,
        name="pair_rows",
    )(window, pair, taps, *totals)
    block = jax.ShapeDtypeStruct((rows, LANES), jnp.float32)
    return pl.pallas_call(
        functools.partial(resist_kernel, plan, kern_count, tile_count),
        out_shape=(block, block, block),
        in_specs=[vmem] * 10,
        out_specs=(pl.BlockSpec(memory_space=pl.ANY),) * 3,
        scratch_shapes=[pltpu.VMEM((plan.span * ambit, LANES), jnp.bfloat16)] * 2
        + [
            pltpu.VMEM(main_total.shape, jnp.float32),
            pltpu.VMEM(strip_total.shape, jnp.float32),
            pltpu.VMEM((plan.height, 2 * LANES), jnp.float32),
            pltpu.VMEM((3, rows, LANES), jnp.float32),
            pltpu.SemaphoreType.DMA((3,)),
        ],
        compiler_params=limit,
        name="image_and_resist",
    )(window, other, pair, far_other, far_pair, wide, taps, *totals, weight)


def solution(mesh):
    placed = (P("tile", None), P(), P(), P("tile", "kern"))
    return jax.shard_map(
        on_device,
        mesh=mesh,
        in_specs=placed,
        out_specs=(P("tile", "kern"), P("tile", "kern"), P("tile", "kern")),
        check_vma=False,
    )
```

```python
import functools

import jax
import jax.numpy as jnp
from jax import lax
from jax.experimental import pallas as pl
from jax.experimental.pallas import tpu as pltpu
from jax.sharding import PartitionSpec as P

STEPS = 8
DIFFUSE_ACID = 0.2
DIFFUSE_BASE = 0.1
QUENCH_RATE = 0.5
EXPOSURE = 0.35

LANES = 128
RIM = 8
GROUP = 4
WORD = 16


def lane_roll_left(value, amount):
    width = value.shape[1]
    amount %= width
    return value if amount == 0 else pltpu.roll(value, width - amount, 1)


def three_blocks(ref, rows, kern, kern_count):
    blocks = []
    for step in (-1, 0, 1):
        place = jnp.clip(kern + step, 0, kern_count - 1)
        block = ref[rows, pl.ds(pl.multiple_of(place * LANES, LANES), LANES)].astype(jnp.float32)
        inside = jnp.logical_and(kern + step >= 0, kern + step < kern_count)
        blocks.append(jnp.where(inside, block, 0.0))
    return jnp.concatenate(blocks, axis=1)


def own_window(mask_ref, kern, kern_count, lead):
    blocks = three_blocks(mask_ref, slice(None), kern, kern_count)
    return lane_roll_left(blocks, LANES - lead)[:, : 2 * LANES]


def turn_kernel(turned_ref):
    row = lax.broadcasted_iota(jnp.int32, turned_ref.shape, 0)
    lane = lax.broadcasted_iota(jnp.int32, turned_ref.shape, 1)
    turned_ref[...] = jnp.where(row == (lane ^ 7), 1.0, 0.0).astype(jnp.bfloat16)


def rim_kernel(
    kern_count, lead, _, mask_ref, quencher_ref, beside_ref, across_ref, window_ref, wide_ref, for_pair_ref, for_other_ref
):
    rows = mask_ref.shape[0]
    kern = lax.axis_index("kern")
    odd = kern % 2 == 1
    window = own_window(mask_ref, kern, kern_count, lead)
    window_ref[...] = window
    beside, across = beside_ref[...], across_ref[...]
    before, after = jnp.where(odd, beside, across), jnp.where(odd, across, beside)
    wide = jnp.concatenate([before, quencher_ref[...], after], axis=1)
    wide = lane_roll_left(wide, LANES - RIM)[:, : 2 * LANES]
    wide_ref[...] = wide
    first, last = wide[:RIM], wide[rows - RIM :]
    even = lax.axis_index("tile") % 2 == 0
    for ref, rim in ((for_pair_ref, jnp.where(even, last, first)), (for_other_ref, jnp.where(even, first, last))):
        ref[:rows, :] = window
        ref[rows:, :] = rim


def swapped(value, axis, first, step=1):
    count = lax.axis_size(axis)
    pairs = [
        (low, low + step) for low in range(count - step) if low // step >= first and (low // step - first) % 2 == 0
    ]
    return lax.ppermute(value, axis, pairs + [(high, low) for low, high in pairs])


def mask_words(window):
    bits = window.astype(jnp.int32)
    row = lax.broadcasted_iota(jnp.int32, (WORD, bits.shape[1]), 0)
    count = bits.shape[0] // WORD
    low = [
        jnp.sum(bits[WORD * w : WORD * (w + 1)] << row, axis=0, keepdims=True) for w in range(count)
    ]
    return [low[w] + (((low[w + 1] & 0xFF) << WORD) if w + 1 < count else 0) for w in range(count)]


class Shifts:
    def __init__(self, window, ambit, first_row, main_ref, strip_ref):
        words = mask_words(window)
        slanted = [
            pltpu.roll(jnp.broadcast_to(word, (8, 2 * LANES)), 2 * LANES - 7, 1, stride=1, stride_axis=0)
            for word in words
        ]
        slanted = jnp.concatenate(slanted, axis=0)
        low, high = slanted[:, :LANES], slanted[:, LANES:]
        lane = lax.broadcasted_iota(jnp.int32, low.shape, 1)
        mains, strips = [], []
        for offset in range(0, ambit, 8):
            mains.append(lane_roll_left(jnp.where(lane < offset, high, low), offset))
            strip = lane_roll_left(high, offset)
            for block in (1, 2, 3):
                strip = jnp.where(lane < 16 * block, strip, lane_roll_left(high, offset - 16 * block))
            strip = jnp.where(lane < 64, strip, pltpu.roll(strip, 64, 1))
            strips.append(strip >> (lane // 16))
        self.ambit, self.first_row = ambit, first_row
        self.sources = {"main": mains, "strip": strips}
        self.refs = {"main": main_ref, "strip": strip_ref}
        self.laid = {"main": set(), "strip": set()}

    def lay(self, kind, rows):
        for row in rows:
            row -= self.first_row
            if row in self.laid[kind]:
                continue
            self.laid[kind].add(row)
            word, bit = divmod(row, WORD)
            source = self.sources[kind]
            for pair in range(self.ambit // 16):
                value = jnp.concatenate(
                    [source[2 * pair + part][8 * word : 8 * word + 8] for part in range(2)], axis=0
                )
                plane = ((value >> bit) & 1).astype(jnp.float32).astype(jnp.bfloat16)
                at = self.ambit * row + 16 * pair
                self.refs[kind][at : at + 16, :] = plane


class Total:
    def __init__(self, ref, source, planes):
        self.ref, self.source, self.planes = ref, source, planes
        self.waiting = {
            (group, half)
            for group in range(ref.shape[0] // planes)
            for half in range(ref.shape[1] // (2 * LANES))
        }

    def add(self, first, last, half, value):
        lanes = slice(2 * LANES * half, 2 * LANES * (half + 1))
        group = first
        while group <= last:
            fresh, end = (group, half) in self.waiting, group
            while end <= last and ((end, half) in self.waiting) == fresh:
                self.waiting.discard((end, half))
                end += 1
            place = (slice(self.planes * group, self.planes * end), lanes)
            piece = value[self.planes * (group - first) : self.planes * (end - first)]
            if not fresh:
                piece = self.ref[place] + piece
            elif self.source is not None:
                piece = self.source[place] + piece
            self.ref[place] = piece
            group = end

    def finish(self):
        for group, half in sorted(self.waiting):
            lanes = slice(2 * LANES * half, 2 * LANES * (half + 1))
            place = (slice(self.planes * group, self.planes * (group + 1)), lanes)
            self.ref[place] = jnp.zeros_like(self.ref[place]) if self.source is None else self.source[place]
        self.waiting = set()


def add_main(plan, total, taps_ref, shifts, s):
    groups, tap_groups, ambit = plan.groups, plan.tap_groups, plan.ambit
    planes = total.planes
    shifts.lay("main", plan.main[s])
    main_ref = shifts.refs["main"]
    first, last = max(0, s - tap_groups + 1), min(groups - 1, s)
    taps = taps_ref[planes * (tap_groups - 1 - s + first) : planes * (tap_groups - s + last), :]
    depth = GROUP * ambit
    for half in range(2):
        at = ambit * (GROUP * s + 2 * half - shifts.first_row)
        moved = jnp.concatenate([main_ref[at : at + depth], main_ref[at + ambit : at + ambit + depth]], axis=1)
        total.add(first, last, half, jnp.dot(taps, moved, preferred_element_type=jnp.float32))


def add_strip(plan, total, taps_ref, shifts, s):
    groups, tap_groups, ambit = plan.groups, plan.tap_groups, plan.ambit
    planes = total.planes
    shifts.lay("strip", plan.strip[s])
    strip_ref = shifts.refs["strip"]
    members = [g for g in range(groups // GROUP) if 0 <= s - GROUP * g < tap_groups]
    pieces = [tap_groups - 1 - s + GROUP * g for g in members]
    taps = jnp.concatenate([taps_ref[planes * p : planes * (p + 1), :] for p in pieces], axis=0)
    depth = GROUP * ambit
    at = ambit * (GROUP * s - shifts.first_row)
    moved = jnp.concatenate(
        [strip_ref[at : at + depth], strip_ref[at + 8 * ambit : at + 8 * ambit + depth]], axis=1
    )
    total.add(members[0], members[-1], 0, jnp.dot(taps, moved, preferred_element_type=jnp.float32))


class Plan:
    def __init__(self, rows, ambit):
        self.rows, self.ambit = rows, ambit
        self.lead = ambit // 2 + RIM
        self.height, self.span = rows + 2 * RIM, rows + 2 * self.lead
        self.groups, self.tap_groups = self.height // GROUP, ambit // GROUP
        self.strip_groups = self.height // 16
        main = {s: range(GROUP * s, GROUP * s + 7) for s in range(self.groups + self.tap_groups - 1)}
        strip = {
            s: range(GROUP * s, GROUP * s + 12) for s in range(GROUP * (self.strip_groups - 1) + self.tap_groups)
        }
        self.main, self.strip = main, strip
        first, middle, last = RIM, self.lead, self.lead + rows
        self.parts = {}
        taken = {"main": set(), "strip": set()}
        for name, low, high in (
            ("own", middle, last),
            ("upper", first, last),
            ("lower", middle, last + rows),
            ("top", 0, last),
            ("bottom", middle, self.span),
        ):
            self.parts[name] = {}
            for kind, steps, reach in (("main", main, 0), ("strip", strip, 7)):
                chosen = [
                    s for s, used in steps.items()
                    if s not in taken[kind] and low <= used[0] and used[-1] + reach < high
                ]
                taken[kind].update(chosen)
                self.parts[name][kind] = chosen
        assert taken == {"main": set(main), "strip": set(strip)}

    def add(self, name, totals, taps_ref, shifts):
        for s in self.parts[name]["main"]:
            add_main(self, totals[0], taps_ref, shifts, s)
        for s in self.parts[name]["strip"]:
            add_strip(self, totals[1], taps_ref, shifts, s)


def taps_kernel(plan, kernels_ref, weights_ref, turned_ref, taps_ref, weight_ref):
    ambit = plan.ambit
    planes = kernels_ref.shape[0] * kernels_ref.shape[1]
    wanted = (weight_ref.shape[0], weights_ref.shape[0])
    plane = lax.broadcasted_iota(jnp.int32, wanted, 0)
    member = lax.broadcasted_iota(jnp.int32, wanted, 1)
    spread = jnp.broadcast_to(weights_ref[...].reshape(1, wanted[1]), wanted)
    column = jnp.sum(jnp.where(plane // 2 == member, spread, 0.0), axis=1, keepdims=True)
    weight_ref[...] = jnp.broadcast_to(column, weight_ref.shape)
    turned = turned_ref[...]
    by_row = jnp.transpose(kernels_ref[...].reshape(planes, ambit, ambit), (1, 0, 2))
    for group in range(plan.tap_groups):
        pieces = [by_row[GROUP * group + part] for part in range(GROUP)]
        place = planes * (plan.tap_groups - 1 - group)
        taps = jnp.concatenate(pieces, axis=1)
        taps = jnp.dot(taps, turned, preferred_element_type=jnp.float32)
        taps_ref[place : place + planes, :] = taps.astype(jnp.bfloat16)


def own_rows_kernel(plan, window_ref, taps_ref, main_total_ref, strip_total_ref, main_ref, strip_ref):
    planes = taps_ref.shape[0] // plan.tap_groups
    shifts = Shifts(window_ref[...], plan.ambit, plan.lead, main_ref, strip_ref)
    totals = Total(main_total_ref, None, planes), Total(strip_total_ref, None, planes)
    plan.add("own", totals, taps_ref, shifts)
    for total in totals:
        total.finish()


def weighted_rows(weight, total_ref, group):
    planes = weight.shape[0]
    field = total_ref[planes * group : planes * (group + 1), :]
    return jnp.sum(weight * (field * field), axis=0, keepdims=True)


def write_main_rows(image_ref, weight, total_ref, groups):
    for group in groups:
        summed = weighted_rows(weight, total_ref, group)
        for part in range(GROUP):
            row = GROUP * group + part
            image_ref[row : row + 1, :LANES] = summed[:, LANES * part : LANES * (part + 1)]


def add_side(plan, below, refs, sources, taps_ref, laid, windows, first_row, after=(), then=None):
    planes = taps_ref.shape[0] // plan.tap_groups

    def add(name):
        totals = [Total(ref, source, planes) for ref, source in zip(refs, sources)]
        shifts = Shifts(jnp.concatenate(windows[name], axis=0), plan.ambit, first_row[name], *laid)
        for part in (name, *after):
            plan.add(part, totals, taps_ref, shifts)
        for total in totals:
            total.finish()
        if then is not None:
            then()

    pl.when(below)(lambda: add("lower"))
    pl.when(jnp.logical_not(below))(lambda: add("upper"))


def pair_rows_kernel(
    plan,
    own_ref,
    pair_ref,
    taps_ref,
    main_in_ref,
    strip_in_ref,
    main_total_ref,
    strip_total_ref,
    main_ref,
    strip_ref,
):
    even = lax.axis_index("tile") % 2 == 0
    own, pair = own_ref[...], pair_ref[: plan.rows]
    windows = {"upper": [pair, own], "lower": [own, pair]}
    refs, sources = (main_total_ref, strip_total_ref), (main_in_ref, strip_in_ref)
    first_row = {"upper": RIM, "lower": plan.lead}
    add_side(plan, even, refs, sources, taps_ref, (main_ref, strip_ref), windows, first_row)


def resist_kernel(
    plan,
    kern_count,
    tile_count,
    own_ref,
    other_ref,
    pair_ref,
    far_other_ref,
    far_pair_ref,
    wide_ref,
    taps_ref,
    main_in_ref,
    strip_in_ref,
    weight_ref,
    intensity_ref,
    acid_ref,
    base_ref,
    main_ref,
    strip_ref,
    main_total_ref,
    strip_total_ref,
    image_ref,
    result_ref,
    result_sem,
):
    kern, tile = lax.axis_index("kern"), lax.axis_index("tile")
    rows, ambit = plan.rows, plan.ambit
    planes = taps_ref.shape[0] // plan.tap_groups

    def far_rows(above_tile):
        place = slice(rows - RIM, rows) if above_tile else slice(RIM)
        blocks = [three_blocks(ref, place, kern, kern_count) for ref in (far_pair_ref, far_other_ref)]
        with_pair = ((tile // 2) % 2 == 1) == above_tile
        chosen = jnp.where(with_pair, blocks[0], blocks[1])
        return lane_roll_left(chosen, LANES - plan.lead)[:, : 2 * LANES]

    even = tile % 2 == 0
    pair, other = pair_ref[...], other_ref[...]
    above, below = jnp.where(even, other, pair), jnp.where(even, pair, other)
    far_above, far_below, own = far_rows(True), far_rows(False), own_ref[...]
    windows = {
        "upper": [far_above, other[:rows], own, pair[:rows], far_below],
        "lower": [far_above, pair[:rows], own, other[:rows], far_below],
    }
    first_row = {"upper": 0, "lower": 0}
    refs, sources = (main_total_ref, strip_total_ref), (main_in_ref, strip_in_ref)
    weight = weight_ref[:, :1]

    def write_image():
        write_main_rows(image_ref, weight, main_total_ref, range(plan.groups))
        for group in range(plan.strip_groups):
            summed = weighted_rows(weight, strip_total_ref, group)
            for part in range(16):
                row = 16 * group + part
                half = summed[:, LANES * (part // 8) : LANES * (part // 8 + 1)]
                image_ref[row : row + 1, LANES:] = lane_roll_left(half, 16 * (part % 8))

    below_is_new = jnp.logical_not(even)
    laid = main_ref, strip_ref
    after = "top", "bottom"
    add_side(plan, below_is_new, refs, sources, taps_ref, laid, windows, first_row, after, write_image)

    image = image_ref[...]
    row_id = lax.broadcasted_iota(jnp.int32, image.shape, 0)
    lane_id = lax.broadcasted_iota(jnp.int32, image.shape, 1)
    at_row = tile * rows + row_id - RIM
    at_column = kern * LANES + lane_id - RIM
    valid = (at_row >= 0) & (at_row < tile_count * rows) & (at_column >= 0) & (at_column < kern_count * LANES)
    valid = valid & (lane_id < LANES + 2 * RIM)

    base = jnp.concatenate([above[rows:], wide_ref[...], below[rows:]], axis=0)
    base = jnp.where(valid, base, 0.0)
    acid = jnp.where(valid, 1.0 - jnp.exp(-EXPOSURE * image), 0.0)

    def spread(value):
        return (
            pltpu.roll(value, 1, 0)
            + pltpu.roll(value, value.shape[0] - 1, 0)
            + pltpu.roll(value, 1, 1)
            + pltpu.roll(value, value.shape[1] - 1, 1)
            - 4.0 * value
        )

    sent = []

    def send_out(place, value, ref):
        result_ref[place] = lane_roll_left(value, RIM)[RIM : RIM + rows, :LANES]
        sent.append(pltpu.make_async_copy(result_ref.at[place], ref, result_sem.at[place]))
        sent[-1].start()

    send_out(0, image, intensity_ref)
    for _ in range(STEPS):
        quenched = QUENCH_RATE * acid * base
        acid, base = (
            jnp.where(valid, acid + DIFFUSE_ACID * spread(acid) - quenched, 0.0),
            jnp.where(valid, base + DIFFUSE_BASE * spread(base) - quenched, 0.0),
        )
    send_out(1, acid, acid_ref)
    send_out(2, base, base_ref)
    for copy_out in sent:
        copy_out.wait()


def on_device(mask, kernels, socs_weights, quencher):
    ambit = kernels.shape[2]
    planes = kernels.shape[0] * kernels.shape[1]
    kern_count, tile_count = lax.axis_size("kern"), lax.axis_size("tile")
    rows = mask.shape[0]
    plan = Plan(rows, ambit)
    vmem = pl.BlockSpec(memory_space=pltpu.VMEM)
    limit = pltpu.CompilerParams(vmem_limit_bytes=24 * 1024 * 1024)

    assert kern_count <= 4
    turned = pl.pallas_call(
        turn_kernel,
        out_shape=jax.ShapeDtypeStruct((GROUP * ambit, GROUP * ambit), jnp.bfloat16),
        out_specs=vmem,
        compiler_params=limit,
        cost_estimate=pl.CostEstimate(flops=10**9, bytes_accessed=10**7, transcendentals=0),
        name="turned",
    )()
    across = swapped(quencher, "kern", 0, 2)
    far_pair = swapped(mask, "tile", 0, 2)
    beside = swapped(quencher, "kern", 0)
    far_other = swapped(mask, "tile", 1, 2)
    main_total = jax.ShapeDtypeStruct((plan.groups * planes, 4 * LANES), jnp.float32)
    strip_total = jax.ShapeDtypeStruct((plan.strip_groups * planes, 2 * LANES), jnp.float32)
    wide_rows = jax.ShapeDtypeStruct((rows, 2 * LANES), jnp.float32)
    sent = jax.ShapeDtypeStruct((rows + RIM, 2 * LANES), jnp.float32)
    across = swapped(across, "kern", 0)
    taps, weight = pl.pallas_call(
        functools.partial(taps_kernel, plan),
        out_shape=(
            jax.ShapeDtypeStruct((plan.tap_groups * planes, GROUP * ambit), jnp.bfloat16),
            jax.ShapeDtypeStruct((planes, LANES), jnp.float32),
        ),
        in_specs=[vmem] * 3,
        out_specs=(vmem,) * 2,
        compiler_params=limit,
        name="taps",
    )(kernels, socs_weights, turned)
    window, wide, for_pair, for_other = pl.pallas_call(
        functools.partial(rim_kernel, kern_count, plan.lead),
        out_shape=(wide_rows, wide_rows, sent, sent),
        in_specs=[vmem] * 5,
        out_specs=(vmem,) * 4,
        compiler_params=limit,
        name="rims",
    )(taps, mask, quencher, beside, across)
    pair = swapped(for_pair, "tile", 0)
    other = swapped(for_other, "tile", 1)
    totals = pl.pallas_call(
        functools.partial(own_rows_kernel, plan),
        out_shape=(main_total, strip_total),
        in_specs=[vmem] * 2,
        out_specs=(vmem,) * 2,
        scratch_shapes=[pltpu.VMEM((rows * ambit, LANES), jnp.bfloat16)] * 2,
        compiler_params=limit,
        name="own_rows",
    )(window, taps)
    totals = pl.pallas_call(
        functools.partial(pair_rows_kernel, plan),
        out_shape=(main_total, strip_total),
        in_specs=[vmem] * 5,
        out_specs=(vmem,) * 2,
        scratch_shapes=[pltpu.VMEM((2 * rows * ambit, LANES), jnp.bfloat16)] * 2,
        compiler_params=limit,
        name="pair_rows",
    )(window, pair, taps, *totals)
    block = jax.ShapeDtypeStruct((rows, LANES), jnp.float32)
    return pl.pallas_call(
        functools.partial(resist_kernel, plan, kern_count, tile_count),
        out_shape=(block, block, block),
        in_specs=[vmem] * 10,
        out_specs=(pl.BlockSpec(memory_space=pl.ANY),) * 3,
        scratch_shapes=[pltpu.VMEM((plan.span * ambit, LANES), jnp.bfloat16)] * 2
        + [
            pltpu.VMEM(main_total.shape, jnp.float32),
            pltpu.VMEM(strip_total.shape, jnp.float32),
            pltpu.VMEM((plan.height, 2 * LANES), jnp.float32),
            pltpu.VMEM((3, rows, LANES), jnp.float32),
            pltpu.SemaphoreType.DMA((3,)),
        ],
        compiler_params=limit,
        name="image_and_resist",
    )(window, other, pair, far_other, far_pair, wide, taps, *totals, weight)


def solution(mesh):
    placed = (P("tile", None), P(), P(), P("tile", "kern"))
    return jax.shard_map(
        on_device,
        mesh=mesh,
        in_specs=placed,
        out_specs=(P("tile", "kern"), P("tile", "kern"), P("tile", "kern")),
        check_vma=False,
    )
```

```python
import functools

import jax
import jax.numpy as jnp
from jax import lax
from jax.experimental import pallas as pl
from jax.experimental.pallas import tpu as pltpu
from jax.sharding import PartitionSpec as P

STEPS = 8
DIFFUSE_ACID = 0.2
DIFFUSE_BASE = 0.1
QUENCH_RATE = 0.5
EXPOSURE = 0.35

LANES = 128
RIM = 8
GROUP = 4
WORD = 16


def lane_roll_left(value, amount):
    width = value.shape[1]
    amount %= width
    return value if amount == 0 else pltpu.roll(value, width - amount, 1)


def three_blocks(ref, rows, kern, kern_count):
    blocks = []
    for step in (-1, 0, 1):
        place = jnp.clip(kern + step, 0, kern_count - 1)
        block = ref[rows, pl.ds(pl.multiple_of(place * LANES, LANES), LANES)].astype(jnp.float32)
        inside = jnp.logical_and(kern + step >= 0, kern + step < kern_count)
        blocks.append(jnp.where(inside, block, 0.0))
    return jnp.concatenate(blocks, axis=1)


def own_window(mask_ref, kern, kern_count, lead):
    blocks = three_blocks(mask_ref, slice(None), kern, kern_count)
    return lane_roll_left(blocks, LANES - lead)[:, : 2 * LANES]


def turn_kernel(turned_ref):
    row = lax.broadcasted_iota(jnp.int32, turned_ref.shape, 0)
    lane = lax.broadcasted_iota(jnp.int32, turned_ref.shape, 1)
    turned_ref[...] = jnp.where(row == (lane ^ 7), 1.0, 0.0).astype(jnp.bfloat16)


def rim_kernel(
    kern_count, lead, _, mask_ref, quencher_ref, beside_ref, across_ref, window_ref, wide_ref, for_pair_ref, for_other_ref
):
    rows = mask_ref.shape[0]
    kern = lax.axis_index("kern")
    odd = kern % 2 == 1
    window = own_window(mask_ref, kern, kern_count, lead)
    window_ref[...] = window
    beside, across = beside_ref[...], across_ref[...]
    before, after = jnp.where(odd, beside, across), jnp.where(odd, across, beside)
    wide = jnp.concatenate([before, quencher_ref[...], after], axis=1)
    wide = lane_roll_left(wide, LANES - RIM)[:, : 2 * LANES]
    wide_ref[...] = wide
    first, last = wide[:RIM], wide[rows - RIM :]
    even = lax.axis_index("tile") % 2 == 0
    for ref, rim in ((for_pair_ref, jnp.where(even, last, first)), (for_other_ref, jnp.where(even, first, last))):
        ref[:rows, :] = window
        ref[rows:, :] = rim


def swapped(value, axis, first, step=1):
    count = lax.axis_size(axis)
    pairs = [
        (low, low + step) for low in range(count - step) if low // step >= first and (low // step - first) % 2 == 0
    ]
    return lax.ppermute(value, axis, pairs + [(high, low) for low, high in pairs])


def mask_words(window):
    bits = window.astype(jnp.int32)
    row = lax.broadcasted_iota(jnp.int32, (WORD, bits.shape[1]), 0)
    count = bits.shape[0] // WORD
    low = [
        jnp.sum(bits[WORD * w : WORD * (w + 1)] << row, axis=0, keepdims=True) for w in range(count)
    ]
    return [low[w] + (((low[w + 1] & 0xFF) << WORD) if w + 1 < count else 0) for w in range(count)]


class Shifts:
    def __init__(self, window, ambit, first_row, main_ref, strip_ref):
        words = mask_words(window)
        slanted = [
            pltpu.roll(jnp.broadcast_to(word, (8, 2 * LANES)), 2 * LANES - 7, 1, stride=1, stride_axis=0)
            for word in words
        ]
        slanted = jnp.concatenate(slanted, axis=0)
        low, high = slanted[:, :LANES], slanted[:, LANES:]
        lane = lax.broadcasted_iota(jnp.int32, low.shape, 1)
        mains, strips = [], []
        for offset in range(0, ambit, 8):
            mains.append(lane_roll_left(jnp.where(lane < offset, high, low), offset))
            strip = lane_roll_left(high, offset)
            for block in (1, 2, 3):
                strip = jnp.where(lane < 16 * block, strip, lane_roll_left(high, offset - 16 * block))
            strip = jnp.where(lane < 64, strip, pltpu.roll(strip, 64, 1))
            strips.append(strip >> (lane // 16))
        self.ambit, self.first_row = ambit, first_row
        self.sources = {"main": mains, "strip": strips}
        self.refs = {"main": main_ref, "strip": strip_ref}
        self.laid = {"main": set(), "strip": set()}

    def lay(self, kind, rows):
        for row in rows:
            row -= self.first_row
            if row in self.laid[kind]:
                continue
            self.laid[kind].add(row)
            word, bit = divmod(row, WORD)
            source = self.sources[kind]
            for pair in range(self.ambit // 16):
                value = jnp.concatenate(
                    [source[2 * pair + part][8 * word : 8 * word + 8] for part in range(2)], axis=0
                )
                plane = ((value >> bit) & 1).astype(jnp.float32).astype(jnp.bfloat16)
                at = self.ambit * row + 16 * pair
                self.refs[kind][at : at + 16, :] = plane


class Total:
    def __init__(self, ref, source, planes):
        self.ref, self.source, self.planes = ref, source, planes
        self.waiting = {
            (group, half)
            for group in range(ref.shape[0] // planes)
            for half in range(ref.shape[1] // (2 * LANES))
        }

    def add(self, first, last, half, value):
        lanes = slice(2 * LANES * half, 2 * LANES * (half + 1))
        group = first
        while group <= last:
            fresh, end = (group, half) in self.waiting, group
            while end <= last and ((end, half) in self.waiting) == fresh:
                self.waiting.discard((end, half))
                end += 1
            place = (slice(self.planes * group, self.planes * end), lanes)
            piece = value[self.planes * (group - first) : self.planes * (end - first)]
            if not fresh:
                piece = self.ref[place] + piece
            elif self.source is not None:
                piece = self.source[place] + piece
            self.ref[place] = piece
            group = end

    def finish(self):
        for group, half in sorted(self.waiting):
            lanes = slice(2 * LANES * half, 2 * LANES * (half + 1))
            place = (slice(self.planes * group, self.planes * (group + 1)), lanes)
            self.ref[place] = jnp.zeros_like(self.ref[place]) if self.source is None else self.source[place]
        self.waiting = set()


def add_main(plan, total, taps_ref, shifts, s):
    groups, tap_groups, ambit = plan.groups, plan.tap_groups, plan.ambit
    planes = total.planes
    shifts.lay("main", plan.main[s])
    main_ref = shifts.refs["main"]
    first, last = max(0, s - tap_groups + 1), min(groups - 1, s)
    taps = taps_ref[planes * (tap_groups - 1 - s + first) : planes * (tap_groups - s + last), :]
    depth = GROUP * ambit
    for half in range(2):
        at = ambit * (GROUP * s + 2 * half - shifts.first_row)
        moved = jnp.concatenate([main_ref[at : at + depth], main_ref[at + ambit : at + ambit + depth]], axis=1)
        total.add(first, last, half, jnp.dot(taps, moved, preferred_element_type=jnp.float32))


def add_strip(plan, total, taps_ref, shifts, s):
    groups, tap_groups, ambit = plan.groups, plan.tap_groups, plan.ambit
    planes = total.planes
    shifts.lay("strip", plan.strip[s])
    strip_ref = shifts.refs["strip"]
    members = [g for g in range(groups // GROUP) if 0 <= s - GROUP * g < tap_groups]
    pieces = [tap_groups - 1 - s + GROUP * g for g in members]
    taps = jnp.concatenate([taps_ref[planes * p : planes * (p + 1), :] for p in pieces], axis=0)
    depth = GROUP * ambit
    at = ambit * (GROUP * s - shifts.first_row)
    moved = jnp.concatenate(
        [strip_ref[at : at + depth], strip_ref[at + 8 * ambit : at + 8 * ambit + depth]], axis=1
    )
    total.add(members[0], members[-1], 0, jnp.dot(taps, moved, preferred_element_type=jnp.float32))


class Plan:
    def __init__(self, rows, ambit):
        self.rows, self.ambit = rows, ambit
        self.lead = ambit // 2 + RIM
        self.height, self.span = rows + 2 * RIM, rows + 2 * self.lead
        self.groups, self.tap_groups = self.height // GROUP, ambit // GROUP
        self.strip_groups = self.height // 16
        main = {s: range(GROUP * s, GROUP * s + 7) for s in range(self.groups + self.tap_groups - 1)}
        strip = {
            s: range(GROUP * s, GROUP * s + 12) for s in range(GROUP * (self.strip_groups - 1) + self.tap_groups)
        }
        self.main, self.strip = main, strip
        first, middle, last = RIM, self.lead, self.lead + rows
        self.parts = {}
        taken = {"main": set(), "strip": set()}
        for name, low, high in (
            ("own", middle, last),
            ("upper", first, last),
            ("lower", middle, last + rows),
            ("top", 0, last),
            ("bottom", middle, self.span),
        ):
            self.parts[name] = {}
            for kind, steps, reach in (("main", main, 0), ("strip", strip, 7)):
                chosen = [
                    s for s, used in steps.items()
                    if s not in taken[kind] and low <= used[0] and used[-1] + reach < high
                ]
                taken[kind].update(chosen)
                self.parts[name][kind] = chosen
        assert taken == {"main": set(main), "strip": set(strip)}

    def add(self, name, totals, taps_ref, shifts):
        for s in self.parts[name]["main"]:
            add_main(self, totals[0], taps_ref, shifts, s)
        for s in self.parts[name]["strip"]:
            add_strip(self, totals[1], taps_ref, shifts, s)


def taps_kernel(plan, kernels_ref, weights_ref, turned_ref, taps_ref, weight_ref):
    ambit = plan.ambit
    planes = kernels_ref.shape[0] * kernels_ref.shape[1]
    wanted = (weight_ref.shape[0], weights_ref.shape[0])
    plane = lax.broadcasted_iota(jnp.int32, wanted, 0)
    member = lax.broadcasted_iota(jnp.int32, wanted, 1)
    spread = jnp.broadcast_to(weights_ref[...].reshape(1, wanted[1]), wanted)
    column = jnp.sum(jnp.where(plane // 2 == member, spread, 0.0), axis=1, keepdims=True)
    weight_ref[...] = jnp.broadcast_to(column, weight_ref.shape)
    turned = turned_ref[...]
    by_row = jnp.transpose(kernels_ref[...].reshape(planes, ambit, ambit), (1, 0, 2))
    for group in range(plan.tap_groups):
        pieces = [by_row[GROUP * group + part] for part in range(GROUP)]
        place = planes * (plan.tap_groups - 1 - group)
        taps = jnp.concatenate(pieces, axis=1)
        taps = jnp.dot(taps, turned, preferred_element_type=jnp.float32)
        taps_ref[place : place + planes, :] = taps.astype(jnp.bfloat16)


def own_rows_kernel(plan, window_ref, taps_ref, main_total_ref, strip_total_ref, main_ref, strip_ref):
    planes = taps_ref.shape[0] // plan.tap_groups
    shifts = Shifts(window_ref[...], plan.ambit, plan.lead, main_ref, strip_ref)
    totals = Total(main_total_ref, None, planes), Total(strip_total_ref, None, planes)
    plan.add("own", totals, taps_ref, shifts)
    for total in totals:
        total.finish()


def weighted_rows(weight, total_ref, group):
    planes = weight.shape[0]
    field = total_ref[planes * group : planes * (group + 1), :]
    return jnp.sum(weight * (field * field), axis=0, keepdims=True)


def write_main_rows(image_ref, weight, total_ref, groups):
    for group in groups:
        summed = weighted_rows(weight, total_ref, group)
        for part in range(GROUP):
            row = GROUP * group + part
            image_ref[row : row + 1, :LANES] = summed[:, LANES * part : LANES * (part + 1)]


def far_rows(plan, far_pair_ref, far_other_ref, above_tile):
    kern, tile = lax.axis_index("kern"), lax.axis_index("tile")
    kern_count = far_pair_ref.shape[1] // LANES
    place = slice(plan.rows - RIM, plan.rows) if above_tile else slice(RIM)
    blocks = [three_blocks(ref, place, kern, kern_count) for ref in (far_pair_ref, far_other_ref)]
    with_pair = ((tile // 2) % 2 == 1) == above_tile
    chosen = jnp.where(with_pair, blocks[0], blocks[1])
    return lane_roll_left(chosen, LANES - plan.lead)[:, : 2 * LANES]


def add_side(plan, below, refs, sources, taps_ref, laid, own, rows, far_refs, then=None):
    planes = taps_ref.shape[0] // plan.tap_groups
    rest = jnp.zeros((RIM, 2 * LANES), jnp.float32)

    def add(name):
        totals = [Total(ref, source, planes) for ref, source in zip(refs, sources)]
        far = far_rows(plan, *far_refs, name == "upper")
        if name == "upper":
            window, first_row, parts = [far, rows, own, rest], 0, ("upper", "top")
        else:
            window, first_row, parts = [rest, own, rows, far], plan.lead - RIM, ("lower", "bottom")
        shifts = Shifts(jnp.concatenate(window, axis=0), plan.ambit, first_row, *laid)
        for part in parts:
            plan.add(part, totals, taps_ref, shifts)
        for total in totals:
            total.finish()
        if then is not None:
            then()

    pl.when(below)(lambda: add("lower"))
    pl.when(jnp.logical_not(below))(lambda: add("upper"))


def pair_rows_kernel(
    plan,
    own_ref,
    pair_ref,
    far_other_ref,
    far_pair_ref,
    taps_ref,
    main_in_ref,
    strip_in_ref,
    main_total_ref,
    strip_total_ref,
    main_ref,
    strip_ref,
):
    even = lax.axis_index("tile") % 2 == 0
    own, pair = own_ref[...], pair_ref[: plan.rows]
    refs, sources = (main_total_ref, strip_total_ref), (main_in_ref, strip_in_ref)
    far_refs = far_pair_ref, far_other_ref
    add_side(plan, even, refs, sources, taps_ref, (main_ref, strip_ref), own, pair, far_refs)


def resist_kernel(
    plan,
    kern_count,
    tile_count,
    own_ref,
    other_ref,
    pair_ref,
    far_pair_ref,
    far_other_ref,
    wide_ref,
    taps_ref,
    main_in_ref,
    strip_in_ref,
    weight_ref,
    intensity_ref,
    acid_ref,
    base_ref,
    main_ref,
    strip_ref,
    main_total_ref,
    strip_total_ref,
    image_ref,
    result_ref,
    result_sem,
):
    kern, tile = lax.axis_index("kern"), lax.axis_index("tile")
    rows, ambit = plan.rows, plan.ambit
    planes = taps_ref.shape[0] // plan.tap_groups

    even = tile % 2 == 0
    pair, other = pair_ref[...], other_ref[...]
    above, below = jnp.where(even, other, pair), jnp.where(even, pair, other)
    refs, sources = (main_total_ref, strip_total_ref), (main_in_ref, strip_in_ref)
    weight = weight_ref[:, :1]

    def write_image():
        write_main_rows(image_ref, weight, main_total_ref, range(plan.groups))
        for group in range(plan.strip_groups):
            summed = weighted_rows(weight, strip_total_ref, group)
            for part in range(16):
                row = 16 * group + part
                half = summed[:, LANES * (part // 8) : LANES * (part // 8 + 1)]
                image_ref[row : row + 1, LANES:] = lane_roll_left(half, 16 * (part % 8))

    below_is_new = jnp.logical_not(even)
    laid, far_refs = (main_ref, strip_ref), (far_pair_ref, far_other_ref)
    add_side(
        plan, below_is_new, refs, sources, taps_ref, laid, own_ref[...], other[:rows], far_refs, write_image
    )

    image = image_ref[...]
    row_id = lax.broadcasted_iota(jnp.int32, image.shape, 0)
    lane_id = lax.broadcasted_iota(jnp.int32, image.shape, 1)
    at_row = tile * rows + row_id - RIM
    at_column = kern * LANES + lane_id - RIM
    valid = (at_row >= 0) & (at_row < tile_count * rows) & (at_column >= 0) & (at_column < kern_count * LANES)
    valid = valid & (lane_id < LANES + 2 * RIM)

    base = jnp.concatenate([above[rows:], wide_ref[...], below[rows:]], axis=0)
    base = jnp.where(valid, base, 0.0)
    acid = jnp.where(valid, 1.0 - jnp.exp(-EXPOSURE * image), 0.0)

    def spread(value):
        return (
            pltpu.roll(value, 1, 0)
            + pltpu.roll(value, value.shape[0] - 1, 0)
            + pltpu.roll(value, 1, 1)
            + pltpu.roll(value, value.shape[1] - 1, 1)
            - 4.0 * value
        )

    sent = []

    def send_out(place, value, ref):
        result_ref[place] = lane_roll_left(value, RIM)[RIM : RIM + rows, :LANES]
        sent.append(pltpu.make_async_copy(result_ref.at[place], ref, result_sem.at[place]))
        sent[-1].start()

    send_out(0, image, intensity_ref)
    for _ in range(STEPS):
        quenched = QUENCH_RATE * acid * base
        acid, base = (
            jnp.where(valid, acid + DIFFUSE_ACID * spread(acid) - quenched, 0.0),
            jnp.where(valid, base + DIFFUSE_BASE * spread(base) - quenched, 0.0),
        )
    send_out(1, acid, acid_ref)
    send_out(2, base, base_ref)
    for copy_out in sent:
        copy_out.wait()


def on_device(mask, kernels, socs_weights, quencher):
    ambit = kernels.shape[2]
    planes = kernels.shape[0] * kernels.shape[1]
    kern_count, tile_count = lax.axis_size("kern"), lax.axis_size("tile")
    rows = mask.shape[0]
    plan = Plan(rows, ambit)
    vmem = pl.BlockSpec(memory_space=pltpu.VMEM)
    limit = pltpu.CompilerParams(vmem_limit_bytes=24 * 1024 * 1024)

    assert kern_count <= 4
    turned = pl.pallas_call(
        turn_kernel,
        out_shape=jax.ShapeDtypeStruct((GROUP * ambit, GROUP * ambit), jnp.bfloat16),
        out_specs=vmem,
        compiler_params=limit,
        cost_estimate=pl.CostEstimate(flops=10**9, bytes_accessed=10**7, transcendentals=0),
        name="turned",
    )()
    across = swapped(quencher, "kern", 0, 2)
    far_pair = swapped(mask, "tile", 0, 2)
    beside = swapped(quencher, "kern", 0)
    far_other = swapped(mask, "tile", 1, 2)
    main_total = jax.ShapeDtypeStruct((plan.groups * planes, 4 * LANES), jnp.float32)
    strip_total = jax.ShapeDtypeStruct((plan.strip_groups * planes, 2 * LANES), jnp.float32)
    wide_rows = jax.ShapeDtypeStruct((rows, 2 * LANES), jnp.float32)
    sent = jax.ShapeDtypeStruct((rows + RIM, 2 * LANES), jnp.float32)
    across = swapped(across, "kern", 0)
    taps, weight = pl.pallas_call(
        functools.partial(taps_kernel, plan),
        out_shape=(
            jax.ShapeDtypeStruct((plan.tap_groups * planes, GROUP * ambit), jnp.bfloat16),
            jax.ShapeDtypeStruct((planes, LANES), jnp.float32),
        ),
        in_specs=[vmem] * 3,
        out_specs=(vmem,) * 2,
        compiler_params=limit,
        name="taps",
    )(kernels, socs_weights, turned)
    window, wide, for_pair, for_other = pl.pallas_call(
        functools.partial(rim_kernel, kern_count, plan.lead),
        out_shape=(wide_rows, wide_rows, sent, sent),
        in_specs=[vmem] * 5,
        out_specs=(vmem,) * 4,
        compiler_params=limit,
        name="rims",
    )(taps, mask, quencher, beside, across)
    pair = swapped(for_pair, "tile", 0)
    other = swapped(for_other, "tile", 1)
    totals = pl.pallas_call(
        functools.partial(own_rows_kernel, plan),
        out_shape=(main_total, strip_total),
        in_specs=[vmem] * 2,
        out_specs=(vmem,) * 2,
        scratch_shapes=[pltpu.VMEM((rows * ambit, LANES), jnp.bfloat16)] * 2,
        compiler_params=limit,
        name="own_rows",
    )(window, taps)
    totals = pl.pallas_call(
        functools.partial(pair_rows_kernel, plan),
        out_shape=(main_total, strip_total),
        in_specs=[vmem] * 7,
        out_specs=(vmem,) * 2,
        scratch_shapes=[pltpu.VMEM(((2 * rows + 2 * RIM) * ambit, LANES), jnp.bfloat16)] * 2,
        compiler_params=limit,
        name="pair_rows",
    )(window, pair, far_other, far_pair, taps, *totals)
    block = jax.ShapeDtypeStruct((rows, LANES), jnp.float32)
    return pl.pallas_call(
        functools.partial(resist_kernel, plan, kern_count, tile_count),
        out_shape=(block, block, block),
        in_specs=[vmem] * 10,
        out_specs=(pl.BlockSpec(memory_space=pl.ANY),) * 3,
        scratch_shapes=[pltpu.VMEM(((2 * rows + 2 * RIM) * ambit, LANES), jnp.bfloat16)] * 2
        + [
            pltpu.VMEM(main_total.shape, jnp.float32),
            pltpu.VMEM(strip_total.shape, jnp.float32),
            pltpu.VMEM((plan.height, 2 * LANES), jnp.float32),
            pltpu.VMEM((3, rows, LANES), jnp.float32),
            pltpu.SemaphoreType.DMA((3,)),
        ],
        compiler_params=limit,
        name="image_and_resist",
    )(window, other, pair, far_pair, far_other, wide, taps, *totals, weight)


def solution(mesh):
    placed = (P("tile", None), P(), P(), P("tile", "kern"))
    return jax.shard_map(
        on_device,
        mesh=mesh,
        in_specs=placed,
        out_specs=(P("tile", "kern"), P("tile", "kern"), P("tile", "kern")),
        check_vma=False,
    )
```

```python
import functools

import jax
import jax.numpy as jnp
from jax import lax
from jax.experimental import pallas as pl
from jax.experimental.pallas import tpu as pltpu
from jax.sharding import PartitionSpec as P

STEPS = 8
DIFFUSE_ACID = 0.2
DIFFUSE_BASE = 0.1
QUENCH_RATE = 0.5
EXPOSURE = 0.35

LANES = 128
RIM = 8
GROUP = 4
WORD = 16


def lane_roll_left(value, amount):
    width = value.shape[1]
    amount %= width
    return value if amount == 0 else pltpu.roll(value, width - amount, 1)


def three_blocks(ref, rows, kern, kern_count):
    blocks = []
    for step in (-1, 0, 1):
        place = jnp.clip(kern + step, 0, kern_count - 1)
        block = ref[rows, pl.ds(pl.multiple_of(place * LANES, LANES), LANES)].astype(jnp.float32)
        inside = jnp.logical_and(kern + step >= 0, kern + step < kern_count)
        blocks.append(jnp.where(inside, block, 0.0))
    return jnp.concatenate(blocks, axis=1)


def own_window(mask_ref, kern, kern_count, lead):
    blocks = three_blocks(mask_ref, slice(None), kern, kern_count)
    return lane_roll_left(blocks, LANES - lead)[:, : 2 * LANES]


def turn_kernel(turned_ref):
    row = lax.broadcasted_iota(jnp.int32, turned_ref.shape, 0)
    lane = lax.broadcasted_iota(jnp.int32, turned_ref.shape, 1)
    turned_ref[...] = jnp.where(row == (lane ^ 7), 1.0, 0.0).astype(jnp.bfloat16)


def rim_kernel(
    kern_count, lead, _, mask_ref, quencher_ref, beside_ref, across_ref, window_ref, wide_ref, for_pair_ref, for_other_ref
):
    rows = mask_ref.shape[0]
    kern = lax.axis_index("kern")
    odd = kern % 2 == 1
    window = own_window(mask_ref, kern, kern_count, lead)
    window_ref[...] = window
    beside, across = beside_ref[...], across_ref[...]
    before, after = jnp.where(odd, beside, across), jnp.where(odd, across, beside)
    wide = jnp.concatenate([before, quencher_ref[...], after], axis=1)
    wide = lane_roll_left(wide, LANES - RIM)[:, : 2 * LANES]
    wide_ref[...] = wide
    first, last = wide[:RIM], wide[rows - RIM :]
    even = lax.axis_index("tile") % 2 == 0
    for ref, rim in ((for_pair_ref, jnp.where(even, last, first)), (for_other_ref, jnp.where(even, first, last))):
        ref[:rows, :] = window
        ref[rows:, :] = rim


def swapped(value, axis, first, step=1):
    count = lax.axis_size(axis)
    pairs = [
        (low, low + step) for low in range(count - step) if low // step >= first and (low // step - first) % 2 == 0
    ]
    return lax.ppermute(value, axis, pairs + [(high, low) for low, high in pairs])


def mask_words(window):
    bits = window.astype(jnp.int32)
    row = lax.broadcasted_iota(jnp.int32, (WORD, bits.shape[1]), 0)
    count = bits.shape[0] // WORD
    low = [
        jnp.sum(bits[WORD * w : WORD * (w + 1)] << row, axis=0, keepdims=True) for w in range(count)
    ]
    return [low[w] + (((low[w + 1] & 0xFF) << WORD) if w + 1 < count else 0) for w in range(count)]


class Shifts:
    def __init__(self, window, ambit, first_row, main_ref, strip_ref):
        words = mask_words(window)
        slanted = [
            pltpu.roll(jnp.broadcast_to(word, (8, 2 * LANES)), 2 * LANES - 7, 1, stride=1, stride_axis=0)
            for word in words
        ]
        slanted = jnp.concatenate(slanted, axis=0)
        low, high = slanted[:, :LANES], slanted[:, LANES:]
        lane = lax.broadcasted_iota(jnp.int32, low.shape, 1)
        mains, strips = [], []
        for offset in range(0, ambit, 8):
            mains.append(lane_roll_left(jnp.where(lane < offset, high, low), offset))
            strip = lane_roll_left(high, offset)
            for block in (1, 2, 3):
                strip = jnp.where(lane < 16 * block, strip, lane_roll_left(high, offset - 16 * block))
            strip = jnp.where(lane < 64, strip, pltpu.roll(strip, 64, 1))
            strips.append(strip >> (lane // 16))
        self.ambit, self.first_row = ambit, first_row
        self.sources = {"main": mains, "strip": strips}
        self.refs = {"main": main_ref, "strip": strip_ref}
        self.laid = {"main": set(), "strip": set()}

    def lay(self, kind, rows):
        for row in rows:
            row -= self.first_row
            if row in self.laid[kind]:
                continue
            self.laid[kind].add(row)
            word, bit = divmod(row, WORD)
            source = self.sources[kind]
            for pair in range(self.ambit // 16):
                value = jnp.concatenate(
                    [source[2 * pair + part][8 * word : 8 * word + 8] for part in range(2)], axis=0
                )
                plane = ((value >> bit) & 1).astype(jnp.float32).astype(jnp.bfloat16)
                at = self.ambit * row + 16 * pair
                self.refs[kind][at : at + 16, :] = plane


class Total:
    def __init__(self, ref, source, planes):
        self.ref, self.source, self.planes = ref, source, planes
        self.waiting = {
            (group, half)
            for group in range(ref.shape[0] // planes)
            for half in range(ref.shape[1] // (2 * LANES))
        }

    def add(self, first, last, half, value):
        lanes = slice(2 * LANES * half, 2 * LANES * (half + 1))
        group = first
        while group <= last:
            fresh, end = (group, half) in self.waiting, group
            while end <= last and ((end, half) in self.waiting) == fresh:
                self.waiting.discard((end, half))
                end += 1
            place = (slice(self.planes * group, self.planes * end), lanes)
            piece = value[self.planes * (group - first) : self.planes * (end - first)]
            if not fresh:
                piece = self.ref[place] + piece
            elif self.source is not None:
                piece = self.source[place] + piece
            self.ref[place] = piece
            group = end

    def finish(self):
        for group, half in sorted(self.waiting):
            lanes = slice(2 * LANES * half, 2 * LANES * (half + 1))
            place = (slice(self.planes * group, self.planes * (group + 1)), lanes)
            self.ref[place] = jnp.zeros_like(self.ref[place]) if self.source is None else self.source[place]
        self.waiting = set()


def add_main(plan, total, taps_ref, shifts, s):
    groups, tap_groups, ambit = plan.groups, plan.tap_groups, plan.ambit
    planes = total.planes
    shifts.lay("main", plan.main[s])
    main_ref = shifts.refs["main"]
    first, last = max(0, s - tap_groups + 1), min(groups - 1, s)
    taps = taps_ref[planes * (tap_groups - 1 - s + first) : planes * (tap_groups - s + last), :]
    depth = GROUP * ambit
    for half in range(2):
        at = ambit * (GROUP * s + 2 * half - shifts.first_row)
        moved = jnp.concatenate([main_ref[at : at + depth], main_ref[at + ambit : at + ambit + depth]], axis=1)
        total.add(first, last, half, jnp.dot(taps, moved, preferred_element_type=jnp.float32))


def add_strip(plan, total, taps_ref, shifts, s):
    groups, tap_groups, ambit = plan.groups, plan.tap_groups, plan.ambit
    planes = total.planes
    shifts.lay("strip", plan.strip[s])
    strip_ref = shifts.refs["strip"]
    members = [g for g in range(groups // GROUP) if 0 <= s - GROUP * g < tap_groups]
    pieces = [tap_groups - 1 - s + GROUP * g for g in members]
    taps = jnp.concatenate([taps_ref[planes * p : planes * (p + 1), :] for p in pieces], axis=0)
    depth = GROUP * ambit
    at = ambit * (GROUP * s - shifts.first_row)
    moved = jnp.concatenate(
        [strip_ref[at : at + depth], strip_ref[at + 8 * ambit : at + 8 * ambit + depth]], axis=1
    )
    total.add(members[0], members[-1], 0, jnp.dot(taps, moved, preferred_element_type=jnp.float32))


class Plan:
    def __init__(self, rows, ambit):
        self.rows, self.ambit = rows, ambit
        self.lead = ambit // 2 + RIM
        self.height, self.span = rows + 2 * RIM, rows + 2 * self.lead
        self.groups, self.tap_groups = self.height // GROUP, ambit // GROUP
        self.strip_groups = self.height // 16
        main = {s: range(GROUP * s, GROUP * s + 7) for s in range(self.groups + self.tap_groups - 1)}
        strip = {
            s: range(GROUP * s, GROUP * s + 12) for s in range(GROUP * (self.strip_groups - 1) + self.tap_groups)
        }
        self.main, self.strip = main, strip
        first, middle, last = RIM, self.lead, self.lead + rows
        self.parts = {}
        taken = {"main": set(), "strip": set()}
        for name, low, high in (
            ("own", middle, last),
            ("upper", first, last),
            ("lower", middle, last + rows),
            ("top", 0, last),
            ("bottom", middle, self.span),
        ):
            self.parts[name] = {}
            for kind, steps, reach in (("main", main, 0), ("strip", strip, 7)):
                chosen = [
                    s for s, used in steps.items()
                    if s not in taken[kind] and low <= used[0] and used[-1] + reach < high
                ]
                taken[kind].update(chosen)
                self.parts[name][kind] = chosen
        assert taken == {"main": set(main), "strip": set(strip)}

    def add(self, name, totals, taps_ref, shifts):
        for s in self.parts[name]["main"]:
            add_main(self, totals[0], taps_ref, shifts, s)
        for s in self.parts[name]["strip"]:
            add_strip(self, totals[1], taps_ref, shifts, s)


def taps_kernel(plan, kernels_ref, weights_ref, turned_ref, taps_ref, weight_ref):
    ambit = plan.ambit
    planes = kernels_ref.shape[0] * kernels_ref.shape[1]
    wanted = (weight_ref.shape[0], weights_ref.shape[0])
    plane = lax.broadcasted_iota(jnp.int32, wanted, 0)
    member = lax.broadcasted_iota(jnp.int32, wanted, 1)
    spread = jnp.broadcast_to(weights_ref[...].reshape(1, wanted[1]), wanted)
    column = jnp.sum(jnp.where(plane // 2 == member, spread, 0.0), axis=1, keepdims=True)
    weight_ref[...] = jnp.broadcast_to(column, weight_ref.shape)
    turned = turned_ref[...]
    by_row = jnp.transpose(kernels_ref[...].reshape(planes, ambit, ambit), (1, 0, 2))
    for group in range(plan.tap_groups):
        pieces = [by_row[GROUP * group + part] for part in range(GROUP)]
        place = planes * (plan.tap_groups - 1 - group)
        taps = jnp.concatenate(pieces, axis=1)
        taps = jnp.dot(taps, turned, preferred_element_type=jnp.float32)
        taps_ref[place : place + planes, :] = taps.astype(jnp.bfloat16)


def own_rows_kernel(plan, window_ref, taps_ref, main_total_ref, strip_total_ref, main_ref, strip_ref):
    planes = taps_ref.shape[0] // plan.tap_groups
    shifts = Shifts(window_ref[...], plan.ambit, plan.lead, main_ref, strip_ref)
    totals = Total(main_total_ref, None, planes), Total(strip_total_ref, None, planes)
    plan.add("own", totals, taps_ref, shifts)
    for total in totals:
        total.finish()


def weighted_rows(weight, total_ref, group):
    planes = weight.shape[0]
    field = total_ref[planes * group : planes * (group + 1), :]
    return jnp.sum(weight * (field * field), axis=0, keepdims=True)


def write_main_rows(image_ref, weight, total_ref, groups):
    for group in groups:
        summed = weighted_rows(weight, total_ref, group)
        for part in range(GROUP):
            row = GROUP * group + part
            image_ref[row : row + 1, :LANES] = summed[:, LANES * part : LANES * (part + 1)]


def far_rows(plan, far_pair_ref, far_other_ref, above_tile):
    kern, tile = lax.axis_index("kern"), lax.axis_index("tile")
    kern_count = far_pair_ref.shape[1] // LANES
    place = slice(plan.rows - RIM, plan.rows) if above_tile else slice(RIM)
    blocks = [three_blocks(ref, place, kern, kern_count) for ref in (far_pair_ref, far_other_ref)]
    with_pair = ((tile // 2) % 2 == 1) == above_tile
    chosen = jnp.where(with_pair, blocks[0], blocks[1])
    return lane_roll_left(chosen, LANES - plan.lead)[:, : 2 * LANES]


def add_side(plan, below, refs, sources, taps_ref, laid, own, rows, far_of, then=None):
    planes = taps_ref.shape[0] // plan.tap_groups
    rest = jnp.zeros((RIM, 2 * LANES), jnp.float32)

    def add(name):
        totals = [Total(ref, source, planes) for ref, source in zip(refs, sources)]
        far = far_of(name)
        if name == "upper":
            window, first_row, parts = [far, rows, own, rest], 0, ("upper", "top")
        else:
            window, first_row, parts = [rest, own, rows, far], plan.lead - RIM, ("lower", "bottom")
        shifts = Shifts(jnp.concatenate(window, axis=0), plan.ambit, first_row, *laid)
        for part in parts:
            plan.add(part, totals, taps_ref, shifts)
        for total in totals:
            total.finish()
        if then is not None:
            then()

    pl.when(below)(lambda: add("lower"))
    pl.when(jnp.logical_not(below))(lambda: add("upper"))


def pair_rows_kernel(
    plan,
    own_ref,
    pair_ref,
    far_pair_ref,
    far_other_ref,
    taps_ref,
    main_in_ref,
    strip_in_ref,
    main_total_ref,
    strip_total_ref,
    next_far_ref,
    main_ref,
    strip_ref,
):
    even = lax.axis_index("tile") % 2 == 0
    own, pair = own_ref[...], pair_ref[: plan.rows]
    refs, sources = (main_total_ref, strip_total_ref), (main_in_ref, strip_in_ref)
    far = {name: far_rows(plan, far_pair_ref, far_other_ref, name == "upper") for name in ("upper", "lower")}
    next_far_ref[...] = jnp.where(even, far["upper"], far["lower"])
    add_side(plan, even, refs, sources, taps_ref, (main_ref, strip_ref), own, pair, far.get)


def resist_kernel(
    plan,
    kern_count,
    tile_count,
    own_ref,
    other_ref,
    pair_ref,
    next_far_ref,
    wide_ref,
    taps_ref,
    main_in_ref,
    strip_in_ref,
    weight_ref,
    intensity_ref,
    acid_ref,
    base_ref,
    main_ref,
    strip_ref,
    main_total_ref,
    strip_total_ref,
    image_ref,
    result_ref,
    result_sem,
):
    kern, tile = lax.axis_index("kern"), lax.axis_index("tile")
    rows, ambit = plan.rows, plan.ambit
    planes = taps_ref.shape[0] // plan.tap_groups

    even = tile % 2 == 0
    pair, other = pair_ref[...], other_ref[...]
    above, below = jnp.where(even, other, pair), jnp.where(even, pair, other)
    refs, sources = (main_total_ref, strip_total_ref), (main_in_ref, strip_in_ref)
    weight = weight_ref[:, :1]

    def write_image():
        write_main_rows(image_ref, weight, main_total_ref, range(plan.groups))
        for group in range(plan.strip_groups):
            summed = weighted_rows(weight, strip_total_ref, group)
            for part in range(16):
                row = 16 * group + part
                half = summed[:, LANES * (part // 8) : LANES * (part // 8 + 1)]
                image_ref[row : row + 1, LANES:] = lane_roll_left(half, 16 * (part % 8))

    below_is_new = jnp.logical_not(even)
    laid, next_far = (main_ref, strip_ref), next_far_ref[...]
    add_side(
        plan, below_is_new, refs, sources, taps_ref, laid, own_ref[...], other[:rows], lambda _: next_far, write_image
    )

    image = image_ref[...]
    row_id = lax.broadcasted_iota(jnp.int32, image.shape, 0)
    lane_id = lax.broadcasted_iota(jnp.int32, image.shape, 1)
    at_row = tile * rows + row_id - RIM
    at_column = kern * LANES + lane_id - RIM
    valid = (at_row >= 0) & (at_row < tile_count * rows) & (at_column >= 0) & (at_column < kern_count * LANES)
    valid = valid & (lane_id < LANES + 2 * RIM)

    base = jnp.concatenate([above[rows:], wide_ref[...], below[rows:]], axis=0)
    base = jnp.where(valid, base, 0.0)
    acid = jnp.where(valid, 1.0 - jnp.exp(-EXPOSURE * image), 0.0)

    def spread(value):
        return (
            pltpu.roll(value, 1, 0)
            + pltpu.roll(value, value.shape[0] - 1, 0)
            + pltpu.roll(value, 1, 1)
            + pltpu.roll(value, value.shape[1] - 1, 1)
            - 4.0 * value
        )

    sent = []

    def send_out(place, value, ref):
        result_ref[place] = lane_roll_left(value, RIM)[RIM : RIM + rows, :LANES]
        sent.append(pltpu.make_async_copy(result_ref.at[place], ref, result_sem.at[place]))
        sent[-1].start()

    send_out(0, image, intensity_ref)
    for _ in range(STEPS):
        quenched = QUENCH_RATE * acid * base
        acid, base = (
            jnp.where(valid, acid + DIFFUSE_ACID * spread(acid) - quenched, 0.0),
            jnp.where(valid, base + DIFFUSE_BASE * spread(base) - quenched, 0.0),
        )
    send_out(1, acid, acid_ref)
    send_out(2, base, base_ref)
    for copy_out in sent:
        copy_out.wait()


def on_device(mask, kernels, socs_weights, quencher):
    ambit = kernels.shape[2]
    planes = kernels.shape[0] * kernels.shape[1]
    kern_count, tile_count = lax.axis_size("kern"), lax.axis_size("tile")
    rows = mask.shape[0]
    plan = Plan(rows, ambit)
    vmem = pl.BlockSpec(memory_space=pltpu.VMEM)
    limit = pltpu.CompilerParams(vmem_limit_bytes=24 * 1024 * 1024)

    assert kern_count <= 4
    turned = pl.pallas_call(
        turn_kernel,
        out_shape=jax.ShapeDtypeStruct((GROUP * ambit, GROUP * ambit), jnp.bfloat16),
        out_specs=vmem,
        compiler_params=limit,
        cost_estimate=pl.CostEstimate(flops=10**9, bytes_accessed=10**7, transcendentals=0),
        name="turned",
    )()
    across = swapped(quencher, "kern", 0, 2)
    far_pair = swapped(mask, "tile", 0, 2)
    beside = swapped(quencher, "kern", 0)
    far_other = swapped(mask, "tile", 1, 2)
    main_total = jax.ShapeDtypeStruct((plan.groups * planes, 4 * LANES), jnp.float32)
    strip_total = jax.ShapeDtypeStruct((plan.strip_groups * planes, 2 * LANES), jnp.float32)
    wide_rows = jax.ShapeDtypeStruct((rows, 2 * LANES), jnp.float32)
    sent = jax.ShapeDtypeStruct((rows + RIM, 2 * LANES), jnp.float32)
    across = swapped(across, "kern", 0)
    taps, weight = pl.pallas_call(
        functools.partial(taps_kernel, plan),
        out_shape=(
            jax.ShapeDtypeStruct((plan.tap_groups * planes, GROUP * ambit), jnp.bfloat16),
            jax.ShapeDtypeStruct((planes, LANES), jnp.float32),
        ),
        in_specs=[vmem] * 3,
        out_specs=(vmem,) * 2,
        compiler_params=limit,
        name="taps",
    )(kernels, socs_weights, turned)
    window, wide, for_pair, for_other = pl.pallas_call(
        functools.partial(rim_kernel, kern_count, plan.lead),
        out_shape=(wide_rows, wide_rows, sent, sent),
        in_specs=[vmem] * 5,
        out_specs=(vmem,) * 4,
        compiler_params=limit,
        name="rims",
    )(taps, mask, quencher, beside, across)
    pair = swapped(for_pair, "tile", 0)
    other = swapped(for_other, "tile", 1)
    totals = pl.pallas_call(
        functools.partial(own_rows_kernel, plan),
        out_shape=(main_total, strip_total),
        in_specs=[vmem] * 2,
        out_specs=(vmem,) * 2,
        scratch_shapes=[pltpu.VMEM((rows * ambit, LANES), jnp.bfloat16)] * 2,
        compiler_params=limit,
        name="own_rows",
    )(window, taps)
    *totals, next_far = pl.pallas_call(
        functools.partial(pair_rows_kernel, plan),
        out_shape=(main_total, strip_total, jax.ShapeDtypeStruct((RIM, 2 * LANES), jnp.float32)),
        in_specs=[vmem] * 7,
        out_specs=(vmem,) * 3,
        scratch_shapes=[pltpu.VMEM(((2 * rows + 2 * RIM) * ambit, LANES), jnp.bfloat16)] * 2,
        compiler_params=limit,
        name="pair_rows",
    )(window, pair, far_pair, far_other, taps, *totals)
    block = jax.ShapeDtypeStruct((rows, LANES), jnp.float32)
    return pl.pallas_call(
        functools.partial(resist_kernel, plan, kern_count, tile_count),
        out_shape=(block, block, block),
        in_specs=[vmem] * 9,
        out_specs=(pl.BlockSpec(memory_space=pl.ANY),) * 3,
        scratch_shapes=[pltpu.VMEM(((2 * rows + 2 * RIM) * ambit, LANES), jnp.bfloat16)] * 2
        + [
            pltpu.VMEM(main_total.shape, jnp.float32),
            pltpu.VMEM(strip_total.shape, jnp.float32),
            pltpu.VMEM((plan.height, 2 * LANES), jnp.float32),
            pltpu.VMEM((3, rows, LANES), jnp.float32),
            pltpu.SemaphoreType.DMA((3,)),
        ],
        compiler_params=limit,
        name="image_and_resist",
    )(window, other, pair, next_far, wide, taps, *totals, weight)


def solution(mesh):
    placed = (P("tile", None), P(), P(), P("tile", "kern"))
    return jax.shard_map(
        on_device,
        mesh=mesh,
        in_specs=placed,
        out_specs=(P("tile", "kern"), P("tile", "kern"), P("tile", "kern")),
        check_vma=False,
    )
```

```python
import functools

import jax
import jax.numpy as jnp
from jax import lax
from jax.experimental import pallas as pl
from jax.experimental.pallas import tpu as pltpu
from jax.sharding import PartitionSpec as P

STEPS = 8
DIFFUSE_ACID = 0.2
DIFFUSE_BASE = 0.1
QUENCH_RATE = 0.5
EXPOSURE = 0.35

LANES = 128
RIM = 8
GROUP = 4
WORD = 16


def lane_roll_left(value, amount):
    width = value.shape[1]
    amount %= width
    return value if amount == 0 else pltpu.roll(value, width - amount, 1)


def three_blocks(ref, rows, kern, kern_count):
    blocks = []
    for step in (-1, 0, 1):
        place = jnp.clip(kern + step, 0, kern_count - 1)
        block = ref[rows, pl.ds(pl.multiple_of(place * LANES, LANES), LANES)].astype(jnp.float32)
        inside = jnp.logical_and(kern + step >= 0, kern + step < kern_count)
        blocks.append(jnp.where(inside, block, 0.0))
    return jnp.concatenate(blocks, axis=1)


def own_window(mask_ref, kern, kern_count, lead):
    blocks = three_blocks(mask_ref, slice(None), kern, kern_count)
    return lane_roll_left(blocks, LANES - lead)[:, : 2 * LANES]


def turn_kernel(turned_ref):
    row = lax.broadcasted_iota(jnp.int32, turned_ref.shape, 0)
    lane = lax.broadcasted_iota(jnp.int32, turned_ref.shape, 1)
    turned_ref[...] = jnp.where(row == (lane ^ 7), 1.0, 0.0).astype(jnp.bfloat16)


def rim_kernel(
    kern_count, lead, _, mask_ref, quencher_ref, beside_ref, across_ref, window_ref, wide_ref, for_pair_ref, for_other_ref
):
    rows = mask_ref.shape[0]
    kern = lax.axis_index("kern")
    odd = kern % 2 == 1
    window = own_window(mask_ref, kern, kern_count, lead)
    window_ref[...] = window
    beside, across = beside_ref[...], across_ref[...]
    before, after = jnp.where(odd, beside, across), jnp.where(odd, across, beside)
    wide = jnp.concatenate([before, quencher_ref[...], after], axis=1)
    wide = lane_roll_left(wide, LANES - RIM)[:, : 2 * LANES]
    wide_ref[...] = wide
    first, last = wide[:RIM], wide[rows - RIM :]
    even = lax.axis_index("tile") % 2 == 0
    for ref, rim in ((for_pair_ref, jnp.where(even, last, first)), (for_other_ref, jnp.where(even, first, last))):
        ref[:rows, :] = window
        ref[rows:, :] = rim


def swapped(value, axis, first, step=1):
    count = lax.axis_size(axis)
    pairs = [
        (low, low + step) for low in range(count - step) if low // step >= first and (low // step - first) % 2 == 0
    ]
    return lax.ppermute(value, axis, pairs + [(high, low) for low, high in pairs])


def mask_words(window):
    bits = window.astype(jnp.int32)
    row = lax.broadcasted_iota(jnp.int32, (WORD, bits.shape[1]), 0)
    count = bits.shape[0] // WORD
    low = [
        jnp.sum(bits[WORD * w : WORD * (w + 1)] << row, axis=0, keepdims=True) for w in range(count)
    ]
    return [low[w] + (((low[w + 1] & 0xFF) << WORD) if w + 1 < count else 0) for w in range(count)]


class Shifts:
    def __init__(self, window, ambit, first_row, main_ref, strip_ref):
        words = mask_words(window)
        slanted = [
            pltpu.roll(jnp.broadcast_to(word, (8, 2 * LANES)), 2 * LANES - 7, 1, stride=1, stride_axis=0)
            for word in words
        ]
        slanted = jnp.concatenate(slanted, axis=0)
        low, high = slanted[:, :LANES], slanted[:, LANES:]
        lane = lax.broadcasted_iota(jnp.int32, low.shape, 1)
        mains, strips = [], []
        for offset in range(0, ambit, 8):
            mains.append(lane_roll_left(jnp.where(lane < offset, high, low), offset))
            strip = lane_roll_left(high, offset)
            for block in (1, 2, 3):
                strip = jnp.where(lane < 16 * block, strip, lane_roll_left(high, offset - 16 * block))
            strip = jnp.where(lane < 64, strip, pltpu.roll(strip, 64, 1))
            strips.append(strip >> (lane // 16))
        self.ambit, self.first_row = ambit, first_row
        self.sources = {"main": mains, "strip": strips}
        self.refs = {"main": main_ref, "strip": strip_ref}
        self.laid = {"main": set(), "strip": set()}

    def lay(self, kind, rows):
        for row in rows:
            row -= self.first_row
            if row in self.laid[kind]:
                continue
            self.laid[kind].add(row)
            word, bit = divmod(row, WORD)
            source = self.sources[kind]
            for pair in range(self.ambit // 16):
                value = jnp.concatenate(
                    [source[2 * pair + part][8 * word : 8 * word + 8] for part in range(2)], axis=0
                )
                plane = ((value >> bit) & 1).astype(jnp.float32).astype(jnp.bfloat16)
                at = self.ambit * row + 16 * pair
                self.refs[kind][at : at + 16, :] = plane


class Total:
    def __init__(self, ref, source, planes):
        self.ref, self.source, self.planes = ref, source, planes
        self.waiting = {
            (group, half)
            for group in range(ref.shape[0] // planes)
            for half in range(ref.shape[1] // (2 * LANES))
        }

    def add(self, first, last, half, value):
        lanes = slice(2 * LANES * half, 2 * LANES * (half + 1))
        group = first
        while group <= last:
            fresh, end = (group, half) in self.waiting, group
            while end <= last and ((end, half) in self.waiting) == fresh:
                self.waiting.discard((end, half))
                end += 1
            place = (slice(self.planes * group, self.planes * end), lanes)
            piece = value[self.planes * (group - first) : self.planes * (end - first)]
            if not fresh:
                piece = self.ref[place] + piece
            elif self.source is not None:
                piece = self.source[place] + piece
            self.ref[place] = piece
            group = end

    def finish(self):
        for group, half in sorted(self.waiting):
            lanes = slice(2 * LANES * half, 2 * LANES * (half + 1))
            place = (slice(self.planes * group, self.planes * (group + 1)), lanes)
            self.ref[place] = jnp.zeros_like(self.ref[place]) if self.source is None else self.source[place]
        self.waiting = set()


def add_main(plan, total, taps_ref, shifts, s):
    groups, tap_groups, ambit = plan.groups, plan.tap_groups, plan.ambit
    planes = total.planes
    shifts.lay("main", plan.main[s])
    main_ref = shifts.refs["main"]
    first, last = max(0, s - tap_groups + 1), min(groups - 1, s)
    taps = taps_ref[planes * (tap_groups - 1 - s + first) : planes * (tap_groups - s + last), :]
    depth = GROUP * ambit
    for half in range(2):
        at = ambit * (GROUP * s + 2 * half - shifts.first_row)
        moved = jnp.concatenate([main_ref[at : at + depth], main_ref[at + ambit : at + ambit + depth]], axis=1)
        total.add(first, last, half, jnp.dot(taps, moved, preferred_element_type=jnp.float32))


def add_strip(plan, total, taps_ref, shifts, s):
    groups, tap_groups, ambit = plan.groups, plan.tap_groups, plan.ambit
    planes = total.planes
    shifts.lay("strip", plan.strip[s])
    strip_ref = shifts.refs["strip"]
    members = [g for g in range(groups // GROUP) if 0 <= s - GROUP * g < tap_groups]
    pieces = [tap_groups - 1 - s + GROUP * g for g in members]
    taps = jnp.concatenate([taps_ref[planes * p : planes * (p + 1), :] for p in pieces], axis=0)
    depth = GROUP * ambit
    at = ambit * (GROUP * s - shifts.first_row)
    moved = jnp.concatenate(
        [strip_ref[at : at + depth], strip_ref[at + 8 * ambit : at + 8 * ambit + depth]], axis=1
    )
    total.add(members[0], members[-1], 0, jnp.dot(taps, moved, preferred_element_type=jnp.float32))


class Plan:
    def __init__(self, rows, ambit):
        self.rows, self.ambit = rows, ambit
        self.lead = ambit // 2 + RIM
        self.height, self.span = rows + 2 * RIM, rows + 2 * self.lead
        self.groups, self.tap_groups = self.height // GROUP, ambit // GROUP
        self.strip_groups = self.height // 16
        main = {s: range(GROUP * s, GROUP * s + 7) for s in range(self.groups + self.tap_groups - 1)}
        strip = {
            s: range(GROUP * s, GROUP * s + 12) for s in range(GROUP * (self.strip_groups - 1) + self.tap_groups)
        }
        self.main, self.strip = main, strip
        first, middle, last = RIM, self.lead, self.lead + rows
        self.parts = {}
        taken = {"main": set(), "strip": set()}
        for name, low, high in (
            ("own", middle, last),
            ("upper", first, last),
            ("lower", middle, last + rows),
            ("top", 0, last),
            ("bottom", middle, self.span),
        ):
            self.parts[name] = {}
            for kind, steps, reach in (("main", main, 0), ("strip", strip, 7)):
                chosen = [
                    s for s, used in steps.items()
                    if s not in taken[kind] and low <= used[0] and used[-1] + reach < high
                ]
                taken[kind].update(chosen)
                self.parts[name][kind] = chosen
        assert taken == {"main": set(main), "strip": set(strip)}

    def add(self, name, totals, taps_ref, shifts):
        for s in self.parts[name]["main"]:
            add_main(self, totals[0], taps_ref, shifts, s)
        for s in self.parts[name]["strip"]:
            add_strip(self, totals[1], taps_ref, shifts, s)


def taps_kernel(plan, kernels_ref, weights_ref, turned_ref, taps_ref, weight_ref):
    ambit = plan.ambit
    planes = kernels_ref.shape[0] * kernels_ref.shape[1]
    wanted = (weight_ref.shape[0], weights_ref.shape[0])
    plane = lax.broadcasted_iota(jnp.int32, wanted, 0)
    member = lax.broadcasted_iota(jnp.int32, wanted, 1)
    spread = jnp.broadcast_to(weights_ref[...].reshape(1, wanted[1]), wanted)
    column = jnp.sum(jnp.where(plane // 2 == member, spread, 0.0), axis=1, keepdims=True)
    weight_ref[...] = jnp.broadcast_to(column, weight_ref.shape)
    turned = turned_ref[...]
    by_row = jnp.transpose(kernels_ref[...].reshape(planes, ambit, ambit), (1, 0, 2))
    for group in range(plan.tap_groups):
        pieces = [by_row[GROUP * group + part] for part in range(GROUP)]
        place = planes * (plan.tap_groups - 1 - group)
        taps = jnp.concatenate(pieces, axis=1)
        taps = jnp.dot(taps, turned, preferred_element_type=jnp.float32)
        taps_ref[place : place + planes, :] = taps.astype(jnp.bfloat16)


def own_rows_kernel(plan, window_ref, taps_ref, main_total_ref, strip_total_ref, main_ref, strip_ref):
    planes = taps_ref.shape[0] // plan.tap_groups
    shifts = Shifts(window_ref[...], plan.ambit, plan.lead, main_ref, strip_ref)
    totals = Total(main_total_ref, None, planes), Total(strip_total_ref, None, planes)
    plan.add("own", totals, taps_ref, shifts)
    for total in totals:
        total.finish()


def weighted_rows(weight, total_ref, group):
    planes = weight.shape[0]
    field = total_ref[planes * group : planes * (group + 1), :]
    return jnp.sum(weight * (field * field), axis=0, keepdims=True)


def write_main_rows(image_ref, weight, total_ref, groups):
    for group in groups:
        summed = weighted_rows(weight, total_ref, group)
        for part in range(GROUP):
            row = GROUP * group + part
            image_ref[row : row + 1, :LANES] = summed[:, LANES * part : LANES * (part + 1)]


def far_rows(plan, far_pair_ref, far_other_ref, above_tile):
    kern, tile = lax.axis_index("kern"), lax.axis_index("tile")
    kern_count = far_pair_ref.shape[1] // LANES
    place = slice(plan.rows - RIM, plan.rows) if above_tile else slice(RIM)
    blocks = [three_blocks(ref, place, kern, kern_count) for ref in (far_pair_ref, far_other_ref)]
    with_pair = ((tile // 2) % 2 == 1) == above_tile
    chosen = jnp.where(with_pair, blocks[0], blocks[1])
    return lane_roll_left(chosen, LANES - plan.lead)[:, : 2 * LANES]


def add_side(plan, below, refs, sources, taps_ref, laid, own, rows, far_of, then=None):
    planes = taps_ref.shape[0] // plan.tap_groups
    rest = jnp.zeros((RIM, 2 * LANES), jnp.float32)

    def add(name):
        totals = [Total(ref, source, planes) for ref, source in zip(refs, sources)]
        far = far_of(name)
        if name == "upper":
            window, first_row, parts = [far, rows, own, rest], 0, ("upper", "top")
        else:
            window, first_row, parts = [rest, own, rows, far], plan.lead - RIM, ("lower", "bottom")
        shifts = Shifts(jnp.concatenate(window, axis=0), plan.ambit, first_row, *laid)
        for part in parts:
            plan.add(part, totals, taps_ref, shifts)
        for total in totals:
            total.finish()
        if then is not None:
            then()

    pl.when(below)(lambda: add("lower"))
    pl.when(jnp.logical_not(below))(lambda: add("upper"))


def pair_rows_kernel(
    plan,
    own_ref,
    pair_ref,
    far_pair_ref,
    far_other_ref,
    taps_ref,
    main_in_ref,
    strip_in_ref,
    main_total_ref,
    strip_total_ref,
    next_far_ref,
    main_ref,
    strip_ref,
):
    even = lax.axis_index("tile") % 2 == 0
    own, pair = own_ref[...], pair_ref[: plan.rows]
    refs, sources = (main_total_ref, strip_total_ref), (main_in_ref, strip_in_ref)
    far = {name: far_rows(plan, far_pair_ref, far_other_ref, name == "upper") for name in ("upper", "lower")}
    next_far_ref[...] = jnp.where(even, far["upper"], far["lower"])
    add_side(plan, even, refs, sources, taps_ref, (main_ref, strip_ref), own, pair, far.get)


def resist_kernel(
    plan,
    kern_count,
    tile_count,
    own_ref,
    other_ref,
    pair_ref,
    next_far_ref,
    wide_ref,
    taps_ref,
    main_in_ref,
    strip_in_ref,
    weight_ref,
    intensity_ref,
    acid_ref,
    base_ref,
    main_ref,
    strip_ref,
    main_total_ref,
    strip_total_ref,
    image_ref,
    start_ref,
    result_ref,
    result_sem,
):
    kern, tile = lax.axis_index("kern"), lax.axis_index("tile")
    rows, ambit = plan.rows, plan.ambit
    planes = taps_ref.shape[0] // plan.tap_groups

    even = tile % 2 == 0
    pair, other = pair_ref[...], other_ref[...]
    above, below = jnp.where(even, other, pair), jnp.where(even, pair, other)
    refs, sources = (main_total_ref, strip_total_ref), (main_in_ref, strip_in_ref)
    weight = weight_ref[:, :1]

    def write_image():
        start_ref[...] = jnp.concatenate([above[rows:], wide_ref[...], below[rows:]], axis=0)
        write_main_rows(image_ref, weight, main_total_ref, range(plan.groups))
        for group in range(plan.strip_groups):
            summed = weighted_rows(weight, strip_total_ref, group)
            for part in range(16):
                row = 16 * group + part
                half = summed[:, LANES * (part // 8) : LANES * (part // 8 + 1)]
                image_ref[row : row + 1, LANES:] = lane_roll_left(half, 16 * (part % 8))

    below_is_new = jnp.logical_not(even)
    laid, next_far = (main_ref, strip_ref), next_far_ref[...]
    add_side(
        plan, below_is_new, refs, sources, taps_ref, laid, own_ref[...], other[:rows], lambda _: next_far, write_image
    )

    image = image_ref[...]
    row_id = lax.broadcasted_iota(jnp.int32, image.shape, 0)
    lane_id = lax.broadcasted_iota(jnp.int32, image.shape, 1)
    at_row = tile * rows + row_id - RIM
    at_column = kern * LANES + lane_id - RIM
    valid = (at_row >= 0) & (at_row < tile_count * rows) & (at_column >= 0) & (at_column < kern_count * LANES)
    valid = valid & (lane_id < LANES + 2 * RIM)

    base = jnp.where(valid, start_ref[...], 0.0)
    acid = jnp.where(valid, 1.0 - jnp.exp(-EXPOSURE * image), 0.0)

    def spread(value):
        return (
            pltpu.roll(value, 1, 0)
            + pltpu.roll(value, value.shape[0] - 1, 0)
            + pltpu.roll(value, 1, 1)
            + pltpu.roll(value, value.shape[1] - 1, 1)
            - 4.0 * value
        )

    sent = []

    def send_out(place, value, ref):
        result_ref[place] = lane_roll_left(value, RIM)[RIM : RIM + rows, :LANES]
        sent.append(pltpu.make_async_copy(result_ref.at[place], ref, result_sem.at[place]))
        sent[-1].start()

    send_out(0, image, intensity_ref)
    for _ in range(STEPS):
        quenched = QUENCH_RATE * acid * base
        acid, base = (
            jnp.where(valid, acid + DIFFUSE_ACID * spread(acid) - quenched, 0.0),
            jnp.where(valid, base + DIFFUSE_BASE * spread(base) - quenched, 0.0),
        )
    send_out(1, acid, acid_ref)
    send_out(2, base, base_ref)
    for copy_out in sent:
        copy_out.wait()


def on_device(mask, kernels, socs_weights, quencher):
    ambit = kernels.shape[2]
    planes = kernels.shape[0] * kernels.shape[1]
    kern_count, tile_count = lax.axis_size("kern"), lax.axis_size("tile")
    rows = mask.shape[0]
    plan = Plan(rows, ambit)
    vmem = pl.BlockSpec(memory_space=pltpu.VMEM)
    limit = pltpu.CompilerParams(vmem_limit_bytes=24 * 1024 * 1024)

    assert kern_count <= 4
    turned = pl.pallas_call(
        turn_kernel,
        out_shape=jax.ShapeDtypeStruct((GROUP * ambit, GROUP * ambit), jnp.bfloat16),
        out_specs=vmem,
        compiler_params=limit,
        cost_estimate=pl.CostEstimate(flops=10**9, bytes_accessed=10**7, transcendentals=0),
        name="turned",
    )()
    across = swapped(quencher, "kern", 0, 2)
    far_pair = swapped(mask, "tile", 0, 2)
    beside = swapped(quencher, "kern", 0)
    far_other = swapped(mask, "tile", 1, 2)
    main_total = jax.ShapeDtypeStruct((plan.groups * planes, 4 * LANES), jnp.float32)
    strip_total = jax.ShapeDtypeStruct((plan.strip_groups * planes, 2 * LANES), jnp.float32)
    wide_rows = jax.ShapeDtypeStruct((rows, 2 * LANES), jnp.float32)
    sent = jax.ShapeDtypeStruct((rows + RIM, 2 * LANES), jnp.float32)
    across = swapped(across, "kern", 0)
    taps, weight = pl.pallas_call(
        functools.partial(taps_kernel, plan),
        out_shape=(
            jax.ShapeDtypeStruct((plan.tap_groups * planes, GROUP * ambit), jnp.bfloat16),
            jax.ShapeDtypeStruct((planes, LANES), jnp.float32),
        ),
        in_specs=[vmem] * 3,
        out_specs=(vmem,) * 2,
        compiler_params=limit,
        name="taps",
    )(kernels, socs_weights, turned)
    window, wide, for_pair, for_other = pl.pallas_call(
        functools.partial(rim_kernel, kern_count, plan.lead),
        out_shape=(wide_rows, wide_rows, sent, sent),
        in_specs=[vmem] * 5,
        out_specs=(vmem,) * 4,
        compiler_params=limit,
        name="rims",
    )(taps, mask, quencher, beside, across)
    pair = swapped(for_pair, "tile", 0)
    other = swapped(for_other, "tile", 1)
    totals = pl.pallas_call(
        functools.partial(own_rows_kernel, plan),
        out_shape=(main_total, strip_total),
        in_specs=[vmem] * 2,
        out_specs=(vmem,) * 2,
        scratch_shapes=[pltpu.VMEM((rows * ambit, LANES), jnp.bfloat16)] * 2,
        compiler_params=limit,
        name="own_rows",
    )(window, taps)
    *totals, next_far = pl.pallas_call(
        functools.partial(pair_rows_kernel, plan),
        out_shape=(main_total, strip_total, jax.ShapeDtypeStruct((RIM, 2 * LANES), jnp.float32)),
        in_specs=[vmem] * 7,
        out_specs=(vmem,) * 3,
        scratch_shapes=[pltpu.VMEM(((2 * rows + 2 * RIM) * ambit, LANES), jnp.bfloat16)] * 2,
        compiler_params=limit,
        name="pair_rows",
    )(window, pair, far_pair, far_other, taps, *totals)
    block = jax.ShapeDtypeStruct((rows, LANES), jnp.float32)
    return pl.pallas_call(
        functools.partial(resist_kernel, plan, kern_count, tile_count),
        out_shape=(block, block, block),
        in_specs=[vmem] * 9,
        out_specs=(pl.BlockSpec(memory_space=pl.ANY),) * 3,
        scratch_shapes=[pltpu.VMEM(((2 * rows + 2 * RIM) * ambit, LANES), jnp.bfloat16)] * 2
        + [
            pltpu.VMEM(main_total.shape, jnp.float32),
            pltpu.VMEM(strip_total.shape, jnp.float32),
            pltpu.VMEM((plan.height, 2 * LANES), jnp.float32),
            pltpu.VMEM((plan.height, 2 * LANES), jnp.float32),
            pltpu.VMEM((3, rows, LANES), jnp.float32),
            pltpu.SemaphoreType.DMA((3,)),
        ],
        compiler_params=limit,
        name="image_and_resist",
    )(window, other, pair, next_far, wide, taps, *totals, weight)


def solution(mesh):
    placed = (P("tile", None), P(), P(), P("tile", "kern"))
    return jax.shard_map(
        on_device,
        mesh=mesh,
        in_specs=placed,
        out_specs=(P("tile", "kern"), P("tile", "kern"), P("tile", "kern")),
        check_vma=False,
    )
```
